32 devices in a mesh: dp: 8 (over z, x), hid: 4 (over y, core).
Axes of the slice: x: 2, y: 2, z: 4, core: 2. Of those that a mesh axis runs over, the one named last changes fastest.
Arguments:
- bag_offsets: int32 [8192], P('dp'), may hold values from 0 to 4095, as said below
- embed_ids: int32 [32768], P('dp'), may hold values from 0 to 3071
- block_owners: int32 [48], replicated, may hold values from 0 to 7, as said below
- cotangent: bfloat16 [8192, 768], P('dp', 'hid'), may hold values from -6 to 6
- table_w: float32 [6144, 512], P('dp', 'hid'), may hold values from -3 to 3
- table_m: float32 [6144, 512], P('dp', 'hid'), may hold values from -20 to 20
- table_v: float32 [6144, 512], P('dp', 'hid'), may hold values from 11 to 44
- table_ema: float32 [6144, 512], P('dp', 'hid'), may hold values from -3 to 3
- first_w: float32 [512, 1536], P('dp', 'hid'), may hold values from -0.25 to 0.25
- first_m: float32 [512, 1536], P('dp', 'hid'), may hold values from -160 to 160
- first_v: float32 [512, 1536], P('dp', 'hid'), may hold values from 737.28 to 2949.12
- first_ema: float32 [512, 1536], P('dp', 'hid'), may hold values from -0.25 to 0.25
- second_w: float32 [256, 1536], P('hid', 'dp'), may hold values from -0.375 to 0.375
- second_m: float32 [256, 1536], P('hid', 'dp'), may hold values from -160 to 160
- second_v: float32 [256, 1536], P('hid', 'dp'), may hold values from 737.28 to 2949.12
- second_ema: float32 [256, 1536], P('hid', 'dp'), may hold values from -0.375 to 0.375
- vector_w: float32 [3, 1536], P(None, 'hid')
- vector_m: float32 [3, 1536], P(None, 'hid'), may hold values from -160 to 160
- vector_v: float32 [3, 1536], P(None, 'hid'), may hold values from 737.28 to 2949.12
- vector_ema: float32 [3, 1536], P(None, 'hid')
- gate_w: float32 [512, 14], replicated, may hold values from -0.1875 to 0.1875
- gate_m: float32 [512, 14], replicated, may hold values from -2048 to 2048
- gate_v: float32 [512, 14], replicated, may hold values from 131072 to 524288
- gate_ema: float32 [512, 14], replicated, may hold values from -0.1875 to 0.1875
Outputs:
- mixed: bfloat16 [8192, 768], P('dp')
- table_w_new: float32 [6144, 512], P('dp', 'hid')
- table_m_new: float32 [6144, 512], P('dp', 'hid')
- table_v_new: float32 [6144, 512], P('dp', 'hid')
- table_ema_new: float32 [6144, 512], P('dp', 'hid')
- first_w_new: float32 [512, 1536], P('dp', 'hid')
- first_m_new: float32 [512, 1536], P('dp', 'hid')
- first_v_new: float32 [512, 1536], P('dp', 'hid')
- first_ema_new: float32 [512, 1536], P('dp', 'hid')
- second_w_new: float32 [256, 1536], P('hid', 'dp')
- second_m_new: float32 [256, 1536], P('hid', 'dp')
- second_v_new: float32 [256, 1536], P('hid', 'dp')
- second_ema_new: float32 [256, 1536], P('hid', 'dp')
- vector_w_new: float32 [3, 1536], P(None, 'hid')
- vector_m_new: float32 [3, 1536], P(None, 'hid')
- vector_v_new: float32 [3, 1536], P(None, 'hid')
- vector_ema_new: float32 [3, 1536], P(None, 'hid')
- gate_w_new: float32 [512, 14], replicated
- gate_m_new: float32 [512, 14], replicated
- gate_v_new: float32 [512, 14], replicated
- gate_ema_new: float32 [512, 14], replicated
The draws below stay inside these ranges and needn't reach their ends.
Inputs may be any that keep to these rules, and one draw needn't show every extreme that they name: `bag_offsets`: each device's 1024 offsets rise strictly from 0; its last bag holds the single id at position 4095. `block_owners`: no owner holds more than 12 of the 48 blocks, and some owner holds exactly 12.
All inputs are finite; a program needn't handle non-finite values.
Results may differ from the reference program's by a relative error of at most 0.01.
Values may be sent and summed in bfloat16 or wider, within the bound.
No kernel may reach another device: no remote copies, remote signals or barrier semaphores. Data moves between devices by JAX's collectives and lax.ppermute only.
A program may use at most 128 MiB of HBM per device.

```python
import math
import jax
import jax.numpy as jnp
import numpy as np
from jax import lax

D = 512
H = 256
O = 256
EXPERTS = 6
GATE_COLS = 14
STREAMS = 3
TOK_DEV = 1024
BAG = 4
ROWS_BLOCK = 64
OWN_MEAN = 6
STEP = 5
CAP = 12
TOKENS = 8192
IDS_DEV = 4096
IDS = 32768
BLOCKS = 48
VOCAB = 3072
SLOTS = 6144
N_DP = 8


def draw_bag_offsets(key, part):
    key = jax.random.fold_in(key, 11)
    device_keys = jax.random.split(key, N_DP)

    def one_device(device_key):
        order = jax.random.permutation(device_key, IDS_DEV - 2) + 1
        cuts = jnp.sort(order[:TOK_DEV - 2]).astype(jnp.int32)
        return jnp.concatenate([jnp.zeros((1,), jnp.int32), cuts, jnp.full((1,), IDS_DEV - 1, jnp.int32)])
    return jax.vmap(one_device)(device_keys).reshape(-1).astype(jnp.int32)


def draw_block_owners(key, part):
    key = jax.random.fold_in(key, 7)
    pick_key, order_key, shuffle_key = jax.random.split(key, 3)
    chosen = jax.random.randint(pick_key, (), 0, N_DP)
    order = jax.random.permutation(order_key, N_DP * CAP).astype(jnp.int32)
    slot_ids = jnp.arange(N_DP * CAP, dtype=jnp.int32)
    scores = jnp.where(slot_ids // CAP == chosen, slot_ids % CAP, CAP + order)
    picked = jnp.argsort(scores)[:BLOCKS].astype(jnp.int32)
    owners = picked // CAP
    shuffle = jax.random.permutation(shuffle_key, BLOCKS)
    return owners[shuffle].astype(jnp.int32)


def draw_vector_w(key, part):
    key = jax.random.fold_in(key, 5)
    noise = jax.random.normal(key, (3, O * EXPERTS), jnp.float32)
    return jnp.stack([0.3 * noise[0], 1.0 + 0.15 * noise[1], 0.3 * noise[2]]).astype(jnp.float32)


def draw_vector_ema(key, part):
    key = jax.random.fold_in(key, 6)
    noise = jax.random.normal(key, (3, O * EXPERTS), jnp.float32)
    return jnp.stack([0.3 * noise[0], 1.0 + 0.15 * noise[1], 0.3 * noise[2]]).astype(jnp.float32)


def touch_ends(entries, stream_key, low, high):
    shape = entries.shape
    index_at = [jax.random.randint(jax.random.fold_in(stream_key, axis), (), 0, shape[axis]) for axis in range(len(shape))]
    entries = entries.at[tuple(index_at)].set(low)
    longest = shape.index(max(shape))
    index_at[longest] = (index_at[longest] + 1) % shape[longest]
    return entries.at[tuple(index_at)].set(high)


def steps_of(rng, shape, cuts, smallest, top_value):
    loudness = 1.0
    for dim, shards_of in cuts:
        heights = jax.random.uniform(jax.random.fold_in(jax.random.fold_in(rng, 6), dim), (shards_of,), jnp.float32, smallest / len(cuts), top_value / len(cuts))
        loudness = loudness * jnp.repeat(jnp.exp(heights), shape[dim] // shards_of).reshape((-1,) + (1,) * (len(shape) - 1 - dim))
    return loudness


def rank_bounds(number_of, skew):
    loads = [(1 << 20) // math.isqrt(standing ** skew) + 1 for standing in range(1, number_of + 1)]
    deviation = 1 + sum(loads) // (1 << 30)
    return np.cumsum(np.array([max(1, weight // deviation) for weight in loads]))


def ranked_ids(rng, shape, count, slope):
    grid = rank_bounds(count, slope)
    ticket = jax.random.randint(jax.random.fold_in(rng, 1), shape, 0, int(grid[count - 1]))
    grade = jnp.searchsorted(jnp.asarray(grid, jnp.int32), ticket, side="right")
    return jax.random.permutation(jax.random.fold_in(rng, 2), count)[grade].astype(jnp.int32)


def gaussian(stream_key, extent, scale, most, shards=(), kind=jnp.bfloat16):
    values = scale * jax.random.normal(stream_key, extent, jnp.float32)
    if shards:
        values = values * steps_of(stream_key, extent, shards, -0.22, 0.18)
    return jnp.clip(values, -most, most).astype(kind)


def setup_inputs(seed: int = 0) -> dict:
    splits = jax.random.split(jax.random.key(seed), 25)
    return {
        "bag_offsets": draw_bag_offsets(jax.random.fold_in(splits[24], 71), 0),
        "embed_ids": touch_ends(ranked_ids(splits[1], (IDS,), VOCAB, 2), jax.random.fold_in(splits[1], 3), 0, VOCAB - 1).astype(jnp.int32),
        "block_owners": draw_block_owners(jax.random.fold_in(splits[24], 71), 0),
        "cotangent": gaussian(splits[3], (TOKENS, O * STREAMS), 1.0, 6.0, ((0, 8), (1, 4))),
        "table_w": gaussian(splits[4], (SLOTS, D), 0.5, 3.0, ((0, 8), (1, 4)), jnp.float32),
        "table_m": gaussian(splits[5], (SLOTS, D), ((BAG * TOK_DEV // (OWN_MEAN * ROWS_BLOCK) + 1) ** 0.5), 20.0, ((0, 8), (1, 4)), jnp.float32),
        "table_v": jnp.clip(jnp.exp(math.log(44.0) - 1.3862944 * jax.random.uniform(splits[6], (SLOTS, D), jnp.float32) ** steps_of(splits[6], (SLOTS, D), ((0, 8), (1, 4)), -0.2, 0.2)), 11.0, 44.0),
        "table_ema": gaussian(splits[7], (SLOTS, D), 0.5, 3.0, ((0, 8), (1, 4)), jnp.float32),
        "first_w": gaussian(splits[8], (D, H * EXPERTS), D ** -0.5, 0.25, ((0, 8), (1, 4)), jnp.float32),
        "first_m": gaussian(splits[9], (D, H * EXPERTS), (0.3 * (TOK_DEV * N_DP) ** 0.5), 160.0, ((0, 8), (1, 4)), jnp.float32),
        "first_v": jnp.clip(jnp.exp(math.log(2949.12) - 1.3862944 * jax.random.uniform(splits[10], (D, H * EXPERTS), jnp.float32) ** steps_of(splits[10], (D, H * EXPERTS), ((0, 8), (1, 4)), -0.2, 0.2)), 737.28, 2949.12),
        "first_ema": gaussian(splits[11], (D, H * EXPERTS), D ** -0.5, 0.25, ((0, 8), (1, 4)), jnp.float32),
        "second_w": gaussian(splits[12], (H, O * EXPERTS), H ** -0.5, 0.375, ((0, 4), (1, 8)), jnp.float32),
        "second_m": gaussian(splits[13], (H, O * EXPERTS), (0.3 * (TOK_DEV * N_DP) ** 0.5), 160.0, ((0, 4), (1, 8)), jnp.float32),
        "second_v": jnp.clip(jnp.exp(math.log(2949.12) - 1.3862944 * jax.random.uniform(splits[14], (H, O * EXPERTS), jnp.float32) ** steps_of(splits[14], (H, O * EXPERTS), ((0, 4), (1, 8)), -0.2, 0.2)), 737.28, 2949.12),
        "second_ema": gaussian(splits[15], (H, O * EXPERTS), H ** -0.5, 0.375, ((0, 4), (1, 8)), jnp.float32),
        "vector_w": draw_vector_w(jax.random.fold_in(splits[24], 71), 0),
        "vector_m": gaussian(splits[17], (3, O * EXPERTS), (0.3 * (TOK_DEV * N_DP) ** 0.5), 160.0, ((1, 4),), jnp.float32),
        "vector_v": jnp.clip(jnp.exp(math.log(2949.12) - 1.3862944 * jax.random.uniform(splits[18], (3, O * EXPERTS), jnp.float32) ** steps_of(splits[18], (3, O * EXPERTS), ((1, 4),), -0.2, 0.2)), 737.28, 2949.12),
        "vector_ema": draw_vector_ema(jax.random.fold_in(splits[24], 71), 0),
        "gate_w": gaussian(splits[20], (D, GATE_COLS), (2 * D) ** -0.5, 0.1875, (), jnp.float32),
        "gate_m": gaussian(splits[21], (D, GATE_COLS), (4 * (TOK_DEV * N_DP) ** 0.5), 2048.0, (), jnp.float32),
        "gate_v": jnp.clip(jnp.exp(jax.random.uniform(splits[22], (D, GATE_COLS), jnp.float32, math.log(131072.0), math.log(524288.0))), 131072.0, 524288.0),
        "gate_ema": gaussian(splits[23], (D, GATE_COLS), (2 * D) ** -0.5, 0.1875, (), jnp.float32),
    }


@jax.custom_vjp
def low(v):
    return lax.optimization_barrier(v.astype(jnp.bfloat16)).astype(jnp.float32)

@jax.custom_vjp
def low_back(v):
    return v

def low_keep(v):
    return (low(v), None)

def low_pass(kept, grad):
    return (grad,)

def back_keep(v):
    return (v, None)

def back_low(kept, grad):
    return (low(grad),)
low.defvjp(low_keep, low_pass)
low_back.defvjp(back_keep, back_low)
highest = lax.Precision.HIGHEST
norm_eps = 1e-05
adam_eps = 1e-08
decay_rate = 0.01
ema_decay = 0.9

def slot_rows(block_owners, embed_ids):
    owner_hot = (block_owners[:, None] == jnp.arange(N_DP, dtype=jnp.int32)[None, :]).astype(jnp.int32)
    rank_of = lax.optimization_barrier(jnp.sum((jnp.cumsum(owner_hot, 0) - owner_hot) * owner_hot, 1))
    starts = ((block_owners * CAP + rank_of) * ROWS_BLOCK).astype(jnp.int32)
    return (jnp.take(starts, embed_ids // ROWS_BLOCK) + embed_ids % ROWS_BLOCK).astype(jnp.int32)

def segments(bag_offsets):
    offsets = bag_offsets.reshape(N_DP, TOK_DEV)
    device_rows = jnp.arange(N_DP, dtype=jnp.int32)[:, None]
    marks = jnp.zeros((N_DP, IDS_DEV), jnp.int32).at[device_rows, offsets].add(1)
    events = jnp.cumsum(marks, 1) - 1 + device_rows * TOK_DEV
    return events.reshape(-1).astype(jnp.int32)

def coefficients(logits):
    count = logits.shape[0]
    task_zero = jax.nn.softmax(logits[:, 0:4], axis=1)
    task_one = jax.nn.softmax(logits[:, 4:8], axis=1)
    shared = jax.nn.softmax(logits[:, 8:14], axis=1)
    blank = jnp.zeros((count, 2), jnp.float32)
    column_zero = jnp.concatenate([task_zero[:, 0:2], blank, task_zero[:, 2:4]], 1)
    column_one = jnp.concatenate([blank, task_one[:, 0:2], task_one[:, 2:4]], 1)
    return jnp.stack([column_zero, column_one, shared], 2)

def adam_step(weight, moment, second, average, grad, rate):
    new_moment = 0.5 * moment + 0.5 * grad
    new_second = 0.5 * second + 0.5 * grad * grad
    correct = 1.0 - 0.5 ** STEP
    new_weight = weight - rate * (new_moment / correct / (jnp.sqrt(new_second / correct) + adam_eps) + decay_rate * weight)
    new_average = ema_decay * average + (1.0 - ema_decay) * new_weight
    return (new_weight, new_moment, new_second, new_average)

def reference(bag_offsets, embed_ids, block_owners, cotangent, table_w, table_m, table_v, table_ema, first_w, first_m, first_v, first_ema, second_w, second_m, second_v, second_ema, vector_w, vector_m, vector_v, vector_ema, gate_w, gate_m, gate_v, gate_ema):
    row_index = slot_rows(block_owners, embed_ids)
    event_of = segments(bag_offsets)

    def forward(table, first, second, vector, gate):
        table_low = low(table)
        pooled = jax.ops.segment_sum(table_low[row_index], event_of, TOKENS, indices_are_sorted=True)
        pooled = low(pooled)
        pre = low_back(jnp.dot(pooled, low(first), precision=highest) + vector[0][None, :])
        hidden = low(jax.nn.gelu(pre, approximate=False)).reshape(TOKENS, H, EXPERTS)
        second_low = low(second).reshape(H, O, EXPERTS)
        inner = low_back(jnp.einsum('rhe,hoe->roe', hidden, second_low, precision=highest))
        center = lax.optimization_barrier(jnp.mean(inner, 1, keepdims=True))
        spread = lax.optimization_barrier(jnp.mean(jnp.square(inner - center), 1, keepdims=True))
        normed = (inner - center) * lax.rsqrt(spread + norm_eps)
        outputs = normed * vector[1].reshape(O, EXPERTS)[None] + vector[2].reshape(O, EXPERTS)[None]
        logits = low_back(jnp.dot(pooled, low(gate), precision=highest))
        coef = coefficients(logits)
        mixed = jnp.einsum('roe,ret->rot', outputs, coef, precision=highest)
        return mixed.reshape(TOKENS, O * STREAMS)
    result, pullback = jax.vjp(forward, table_w, first_w, second_w, vector_w, gate_w)
    grads = pullback(cotangent.astype(jnp.float32))
    table_new = adam_step(table_w, table_m, table_v, table_ema, grads[0], 0.3)
    first_new = adam_step(first_w, first_m, first_v, first_ema, grads[1], 0.04)
    second_new = adam_step(second_w, second_m, second_v, second_ema, grads[2], 0.06)
    vector_new = adam_step(vector_w, vector_m, vector_v, vector_ema, grads[3], 0.2)
    gate_new = adam_step(gate_w, gate_m, gate_v, gate_ema, grads[4], 0.03)
    return (result.astype(jnp.bfloat16), table_new[0], table_new[1], table_new[2], table_new[3], first_new[0], first_new[1], first_new[2], first_new[3], second_new[0], second_new[1], second_new[2], second_new[3], vector_new[0], vector_new[1], vector_new[2], vector_new[3], gate_new[0], gate_new[1], gate_new[2], gate_new[3])
```

```python
import functools

import jax
import jax.numpy as jnp
from jax import lax
from jax.experimental import pallas as pl
from jax.experimental.pallas import tpu as pltpu
from jax.sharding import PartitionSpec as P

D = 512
H = 256
O = 256
EXPERTS = 6
STREAMS = 3
ROWS_BLOCK = 64
STEP = 5
CAP = 12
HALF = 128
IDS_STEP = 256
EVENTS_STEP = 256

norm_eps = 1e-05
adam_eps = 1e-08
decay_rate = 0.01
ema_decay = 0.9

bf16 = jnp.bfloat16
f32 = jnp.float32
MIB = 1 << 20

STREAM_EXPERTS = ((0, 1, 4, 5), (2, 3, 4, 5), (0, 1, 2, 3, 4, 5))
STREAM_COLS = (0, 4, 8)

VMEM = pl.BlockSpec(memory_space=pltpu.VMEM)
SMEM = pl.BlockSpec(memory_space=pltpu.SMEM)


def shape(dims, dtype):
    return jax.ShapeDtypeStruct(tuple(dims), dtype)


def nn(a, b):
    return lax.dot_general(a, b, (((1,), (0,)), ((), ())), preferred_element_type=f32)


def nt(a, b):
    return lax.dot_general(a, b, (((1,), (1,)), ((), ())), preferred_element_type=f32)


def tn(a, b):
    return lax.dot_general(a, b, (((0,), (0,)), ((), ())), preferred_element_type=f32)


def call(kernel, out_shape, args, in_specs=None, scratch=(), vmem=24, flops=0, moved=0):
    single = not isinstance(out_shape, (list, tuple))
    outs = [out_shape] if single else list(out_shape)
    result = pl.pallas_call(
        kernel,
        out_shape=outs,
        in_specs=in_specs or [VMEM] * len(args),
        out_specs=[VMEM] * len(outs),
        scratch_shapes=list(scratch),
        compiler_params=pltpu.CompilerParams(vmem_limit_bytes=vmem * MIB),
        cost_estimate=pl.CostEstimate(flops=flops, bytes_accessed=moved, transcendentals=0),
    )(*args)
    return result[0] if single else result


def swap(value, axis, mask):
    count = lax.axis_size(axis)
    return lax.ppermute(value, axis, [(i, i ^ mask) for i in range(count)])


def inner_size(dp_count):
    return 1 << ((dp_count.bit_length() - 1) // 2)


def gather_dp(value):
    count = lax.axis_size("dp")
    inner = inner_size(count)
    far = {0: value}
    for step in reversed(range(1, count // inner)):
        far[step] = swap(value, "dp", step * inner)
    pieces = [None] * count
    for step in [0] + list(reversed(range(1, count // inner))):
        pieces[step * inner] = far[step]
        for near in range(1, inner):
            pieces[step * inner + near] = swap(far[step], "dp", near)
    return pieces


def low_kernel(table_ref, first_ref, second_ref, cot_ref, *outs, hid):
    table_out, weight_out = outs[0], outs[1]
    table_out[...] = table_ref[...].astype(bf16)
    rows = first_ref.shape[0]
    weight_out[0:rows, :] = first_ref[...].astype(bf16)
    second = second_ref[...]
    fold = weight_out.shape[0] - rows
    weight_out[rows:, :] = jnp.concatenate(
        [second[i * fold : (i + 1) * fold, :] for i in range(second.shape[0] // fold)], axis=1
    ).astype(bf16)
    me = lax.axis_index("hid")
    width = outs[2].shape[1]
    for m in range(hid):
        start = pl.multiple_of((me ^ m) * width, width)
        outs[2 + m][...] = cot_ref[:, pl.ds(start, width)]


def counts_kernel(offs_ref, ids_ref, off_ref, nxt_ref, c_ref, idb, acc):
    id_rows, lanes = ids_ref.shape
    events, vocab = c_ref.shape
    per = IDS_STEP // lanes
    idt = ids_ref[...].T
    for q in range(id_rows):
        idb[q // per, (q % per) * lanes : (q % per + 1) * lanes, :] = jnp.broadcast_to(
            idt[:, q : q + 1], (lanes, HALF)
        )
    offt = off_ref[...].T
    nxtt = nxt_ref[...].T
    cols = EVENTS_STEP // lanes
    width = 512
    for ec in range(events // EVENTS_STEP):
        first = jnp.concatenate([offt[:, ec * cols + i : ec * cols + i + 1] for i in range(cols)], 0)
        last = jnp.concatenate([nxtt[:, ec * cols + i : ec * cols + i + 1] for i in range(cols)], 0)
        acc[...] = jnp.zeros_like(acc)
        low = offs_ref[ec * EVENTS_STEP]
        if (ec + 1) * EVENTS_STEP < events:
            high = offs_ref[(ec + 1) * EVENTS_STEP]
        else:
            high = jnp.int32(id_rows * lanes)

        def body(step, carry):
            place = step * IDS_STEP + lax.broadcasted_iota(jnp.int32, (EVENTS_STEP, IDS_STEP), 1)
            member = jnp.where((place >= first) & (place < last), 1.0, 0.0).astype(bf16)
            ids = idb[step]
            for v in range(vocab // width):
                hot = jnp.concatenate(
                    [
                        jnp.where(
                            ids
                            == lax.broadcasted_iota(jnp.int32, (IDS_STEP, HALF), 1)
                            + (v * width + i * HALF),
                            1.0,
                            0.0,
                        ).astype(bf16)
                        for i in range(width // HALF)
                    ],
                    axis=1,
                )
                acc[:, v * width : (v + 1) * width] += nn(member, hot)
            return carry

        lax.fori_loop(low // IDS_STEP, (high + IDS_STEP - 1) // IDS_STEP, body, 0)
        c_ref[ec * EVENTS_STEP : (ec + 1) * EVENTS_STEP, :] = acc[...].astype(bf16)


def each_block(owners_ref, count_ref, owners, body):
    for o in range(owners):
        count_ref[o] = 0

    def step(block, carry):
        owner = owners_ref[block]
        rank = count_ref[owner]
        count_ref[owner] = rank + 1
        body(block, owner, rank)
        return carry

    lax.fori_loop(0, owners_ref.shape[0], step, 0)


def pool_kernel(owners_ref, c_ref, *refs, dp, hid):
    pieces, outs = refs[:dp], refs[dp : dp + hid]
    whole, table, pooled, count_ref = refs[dp + hid :]
    me_dp, me_hid = lax.axis_index("dp"), lax.axis_index("hid")
    for r in range(dp):
        whole[me_dp ^ r] = pieces[r][...]

    def place(block, owner, rank):
        table[pl.ds(pl.multiple_of(block * ROWS_BLOCK, ROWS_BLOCK), ROWS_BLOCK), :] = whole[
            owner, pl.ds(pl.multiple_of(rank * ROWS_BLOCK, ROWS_BLOCK), ROWS_BLOCK), :
        ]

    each_block(owners_ref, count_ref, dp, place)
    rows = pooled.shape[1]
    for q in range(hid):
        pooled[q] = nn(c_ref[q * rows : (q + 1) * rows, :], table[...])
    for m in range(hid):
        outs[m][...] = pooled[me_hid ^ m].T.astype(bf16)


def hot_cv(rows, cols, mult, start):
    group = cols // mult
    col = lax.broadcasted_iota(jnp.int32, (8, cols), 1)
    target = ((col % group) * mult + col // group - start)[0:1]
    row = lax.broadcasted_iota(jnp.int32, (rows, cols), 0)
    return jnp.where(row == target, 1.0, 0.0).astype(bf16)


def hot_vc(rows, cols, mult, start):
    group = rows // mult
    row = lax.broadcasted_iota(jnp.int32, (rows, HALF), 0)
    target = ((row % group) * mult + row // group - start)[:, 0:1]
    col = lax.broadcasted_iota(jnp.int32, (rows, cols), 1)
    return jnp.where(col == target, 1.0, 0.0).astype(bf16)


def weights_kernel(*refs, dp, hid):
    pieces, vec_ref = refs[:hid], refs[hid]
    w1p, w1t, w2p, w2t, col_ref, q_ref, q3_ref, q3t_ref = refs[hid + 1 : hid + 9]
    w1s, w2s = refs[hid + 9 :]
    me_dp, me_hid = lax.axis_index("dp"), lax.axis_index("hid")
    rows = D // dp
    fold = H // dp
    width = (O * EXPERTS) // dp
    high = H // hid
    for r in range(hid):
        j = me_hid ^ r
        for s in range(dp):
            k = me_dp ^ s
            w1s[j, pl.ds(pl.multiple_of(k * rows, rows), rows), :] = pieces[r][s, 0:rows, :]
            part = pieces[r][s, rows : rows + fold, :].astype(f32)
            for q in range(high // fold):
                start = pl.multiple_of(j * high + q * fold, fold)
                w2s[k, pl.ds(start, fold), :] = part[:, q * width : (q + 1) * width].astype(bf16)
    span = HALF * EXPERTS
    q_ref[...] = hot_cv(span, span, EXPERTS, 0)
    q3_ref[...] = hot_cv(O * STREAMS, O * STREAMS, STREAMS, 0)
    q3t_ref[...] = hot_vc(O * STREAMS, O * STREAMS, STREAMS, 0)
    j_step = w1s.shape[2]
    k_step = w2s.shape[2]
    for half in range(2):
        lanes = slice(half * HALF, (half + 1) * HALF)
        total_p, total_t = None, None
        for i in range(span // j_step):
            w1 = w1s[half * (span // j_step) + i]
            p = nn(w1, q_ref[i * j_step : (i + 1) * j_step, :])
            t = nt(hot_vc(span, j_step, EXPERTS, i * j_step), w1)
            total_p = p if total_p is None else total_p + p
            total_t = t if total_t is None else total_t + t
        for e in range(EXPERTS):
            w1p[e, :, lanes] = total_p[:, e * HALF : (e + 1) * HALF].astype(bf16)
            w1t[e, lanes, :] = total_t[e * HALF : (e + 1) * HALF, :].astype(bf16)
        total_p, total_t = None, None
        for i in range(span // k_step):
            w2 = w2s[half * (span // k_step) + i]
            p = nn(w2, q_ref[i * k_step : (i + 1) * k_step, :])
            t = nt(hot_vc(span, k_step, EXPERTS, i * k_step), w2)
            total_p = p if total_p is None else total_p + p
            total_t = t if total_t is None else total_t + t
        for e in range(EXPERTS):
            w2p[e, :, lanes] = total_p[:, e * HALF : (e + 1) * HALF].astype(bf16)
            w2t[e, lanes, :] = total_t[e * HALF : (e + 1) * HALF, :].astype(bf16)
        vec = vec_ref[:, half * span : (half + 1) * span]
        v0 = vec.astype(bf16)
        rest = vec - v0.astype(f32)
        v1 = rest.astype(bf16)
        v2 = (rest - v1.astype(f32)).astype(bf16)
        turn = hot_vc(span, span, EXPERTS, 0)
        cols = nt(turn, v0) + nt(turn, v1) + nt(turn, v2)
        for e in range(EXPERTS):
            for i in range(3):
                col_ref[i, e, lanes, :] = jnp.broadcast_to(
                    cols[e * HALF : (e + 1) * HALF, i : i + 1], (HALF, HALF)
                )


def softmax_rows(logits):
    top = jnp.max(logits, axis=0, keepdims=True)
    grown = jnp.exp(logits - top)
    return grown / jnp.sum(grown, axis=0, keepdims=True)


def wide(column, width):
    return jnp.concatenate([column] * (width // HALF), axis=1) if width > HALF else column


def main_kernel(*refs, hid):
    xts, cots = refs[:hid], refs[hid : 2 * hid]
    w1p, w1t, w2p, w2t, col_ref, q_ref, q3_ref, q3t_ref, gate_ref = refs[2 * hid : 2 * hid + 9]
    outs = refs[2 * hid + 9 :]
    mixed_ref, small_ref, xt, hid_ref, dinner_ref, dpre_ref = outs[:6]
    dx_outs = outs[6 : 6 + hid]
    up, upq, mix, work, slope, norm, dout, dx, vec = outs[6 + hid :]
    me = lax.axis_index("hid")
    feats, rows = xts[0].shape
    for m in range(hid):
        j = me ^ m
        xt[pl.ds(pl.multiple_of(j * feats, feats), feats), :] = xts[m][...]
        cols = cots[m].shape[0]
        upq[pl.ds(pl.multiple_of(j * cols, cols), cols), :] = cots[m][...]
    up[...] = nn(q3t_ref[...], upq[...])
    gate = gate_ref[...].astype(bf16)
    logits = nn(gate, xt[...])
    chances = [
        softmax_rows(logits[STREAM_COLS[t] : STREAM_COLS[t] + len(STREAM_EXPERTS[t])])
        for t in range(STREAMS)
    ]
    mix[...] = jnp.zeros_like(mix)
    chunk = 64
    parts = [slice(i * chunk, (i + 1) * chunk) for i in range(O // chunk)]
    ones = jnp.ones((8, rows), bf16)
    d_chances = [[None] * len(STREAM_EXPERTS[t]) for t in range(STREAMS)]
    for e in range(EXPERTS):
        streams = [t for t in range(STREAMS) if e in STREAM_EXPERTS[t]]
        coef = {
            t: chances[t][STREAM_EXPERTS[t].index(e) : STREAM_EXPERTS[t].index(e) + 1]
            for t in streams
        }
        work[...] = nn(w1t[e], xt[...])
        for p in parts:
            pre = work[p, :] + wide(col_ref[0, e, p, :], rows)
            phi = 0.5 + 0.5 * lax.erf(pre * 0.7071067811865476)
            hid_ref[e, p, :] = (pre * phi).astype(bf16)
            slope[p, :] = phi + pre * (jnp.exp(-0.5 * pre * pre) * 0.3989422804014327)
        work[...] = nn(w2t[e], hid_ref[e])
        total = jnp.zeros((1, rows), f32)
        for p in parts:
            total = total + jnp.sum(work[p, :], axis=0, keepdims=True)
        mean = total * (1.0 / O)
        total = jnp.zeros((1, rows), f32)
        for p in parts:
            off = work[p, :] - mean
            total = total + jnp.sum(off * off, axis=0, keepdims=True)
        inverse = lax.rsqrt(total * (1.0 / O) + norm_eps)
        sums = {t: jnp.zeros((1, rows), f32) for t in streams}
        first, second = jnp.zeros((1, rows), f32), jnp.zeros((1, rows), f32)
        for i, p in enumerate(parts):
            normed = (work[p, :] - mean) * inverse
            gain = wide(col_ref[1, e, p, :], rows)
            value = normed * gain + wide(col_ref[2, e, p, :], rows)
            grad = None
            for t in streams:
                rows_t = slice(t * O + i * chunk, t * O + (i + 1) * chunk)
                mix[rows_t, :] += value * coef[t]
                upward = up[rows_t, :]
                sums[t] = sums[t] + jnp.sum(upward * value, axis=0, keepdims=True)
                term = upward * coef[t]
                grad = term if grad is None else grad + term
            d_norm = grad * gain
            first = first + jnp.sum(d_norm, axis=0, keepdims=True)
            second = second + jnp.sum(d_norm * normed, axis=0, keepdims=True)
            norm[p, :] = normed
            work[p, :] = d_norm
            dout[0, p, :] = (grad * normed).astype(bf16)
            dout[1, p, :] = grad.astype(bf16)
        for t in streams:
            d_chances[t][STREAM_EXPERTS[t].index(e)] = sums[t]
        first, second = first * (1.0 / O), second * (1.0 / O)
        for p in parts:
            dinner_ref[e, p, :] = ((work[p, :] - first - norm[p, :] * second) * inverse).astype(bf16)
        work[...] = nn(w2p[e], dinner_ref[e])
        for p in parts:
            dpre_ref[e, p, :] = (work[p, :] * slope[p, :]).astype(bf16)
        vec[0, e] = nt(ones, dpre_ref[e])
        vec[1, e] = nt(ones, dout[0])
        vec[2, e] = nt(ones, dout[1])
        back = nn(w1p[e], dpre_ref[e])
        if e == 0:
            dx[...] = back
        else:
            dx[...] += back
    d_logits = []
    for t in range(STREAMS):
        upward = jnp.concatenate(d_chances[t], axis=0)
        g = chances[t]
        d_logits.append(g * (upward - jnp.sum(g * upward, axis=0, keepdims=True)))
    pad = jnp.zeros((gate_ref.shape[0] - 14, rows), f32)
    d_logits = jnp.concatenate(d_logits + [pad], axis=0).astype(bf16)
    dx[...] += tn(gate, d_logits)
    for m in range(hid):
        start = pl.multiple_of((me ^ m) * feats, feats)
        dx_outs[m][...] = dx[pl.ds(start, feats), :].astype(bf16)
    gates = gate_ref.shape[0]
    small_ref[0:gates, :] = nt(d_logits, xt[...]).astype(bf16)
    small_ref[gates:, :] = jnp.zeros((small_ref.shape[0] - gates, small_ref.shape[1]), bf16)
    width = (H * EXPERTS) // hid
    for half in range(2):
        lanes = slice(half * HALF, (half + 1) * HALF)
        stack = jnp.concatenate(
            [
                jnp.concatenate([vec[i, e, 0:1, lanes] for e in range(EXPERTS)], axis=1)
                for i in range(3)
            ]
            + [jnp.zeros((5, HALF * EXPERTS), f32)],
            axis=0,
        ).astype(bf16)
        turned = nt(stack, q_ref[...])
        per = (HALF * EXPERTS) // width
        for i in range(per):
            j = half * per + i
            small_ref[gates + 16 * j : gates + 16 * j + 8, 0:width] = turned[
                :, i * width : (i + 1) * width
            ].astype(bf16)
    mixed_ref[...] = tn(mix[...].astype(bf16), q3t_ref[...]).astype(bf16)


def grads_kernel(xt, hid_ref, dinner_ref, dpre_ref, q_ref, *refs, dp, hid):
    outs = refs[:hid]
    turned, w1g, w2g = refs[hid:]
    me_dp, me_hid = lax.axis_index("dp"), lax.axis_index("hid")
    span = HALF * EXPERTS
    rows = D // dp
    fold = H // dp
    width = (O * EXPERTS) // dp
    high = H // hid
    cols = (H * EXPERTS) // hid
    inner = inner_size(dp)
    whole = [nt(hid_ref[e], dinner_ref[e]).astype(bf16) for e in range(EXPERTS)]
    for half in range(2):
        part = slice(half * HALF, (half + 1) * HALF)
        block = jnp.concatenate([dpre_ref[e, part, :] for e in range(EXPERTS)], axis=0)
        turned[half * span : (half + 1) * span, :] = nn(q_ref[...], block).astype(bf16)
        block = jnp.concatenate([w[:, part] for w in whole], axis=1)
        w2g[:, half * span : (half + 1) * span] = nt(block, q_ref[...])
    for m in range(hid):
        j = me_hid ^ m
        left = turned[pl.ds(pl.multiple_of(j * cols, cols), cols), :]
        w1g[...] = nt(xt[...], left).astype(bf16)
        for near in range(inner):
            for far in range(dp // inner):
                k = me_dp ^ (far * inner + near)
                start = pl.multiple_of(k * rows, rows)
                outs[m][near, far, 0:rows, :] = w1g[pl.ds(start, rows), :]
        start = pl.multiple_of(j * high, high)
        for k in range(dp):
            part = w2g[pl.ds(start, high), k * width : (k + 1) * width]
            folded = jnp.concatenate(
                [part[i * fold : (i + 1) * fold, :] for i in range(high // fold)], axis=1
            ).astype(bf16)
            r = me_dp ^ k
            outs[m][r % inner, r // inner, rows : rows + fold, :] = folded


def table_kernel(owners_ref, c_ref, *refs, dp, hid):
    pieces, outs = refs[:hid], refs[hid : hid + dp]
    back, grads, slots, count_ref = refs[hid + dp :]
    me_dp, me_hid = lax.axis_index("dp"), lax.axis_index("hid")
    rows = pieces[0].shape[1]
    for m in range(hid):
        start = pl.multiple_of((me_hid ^ m) * rows, rows)
        back[:, pl.ds(start, rows)] = pieces[m][...]
    grads[...] = nn(back[...], c_ref[...]).T.astype(bf16)
    slots[...] = jnp.zeros_like(slots)

    def place(block, owner, rank):
        slots[
            owner ^ me_dp, pl.ds(pl.multiple_of(rank * ROWS_BLOCK, ROWS_BLOCK), ROWS_BLOCK), :
        ] = grads[pl.ds(pl.multiple_of(block * ROWS_BLOCK, ROWS_BLOCK), ROWS_BLOCK), :]

    each_block(owners_ref, count_ref, dp, place)
    for r in range(dp):
        outs[r][...] = slots[r]


def adam(weight, moment, second, average, grad, rate):
    new_moment = 0.5 * moment + 0.5 * grad
    new_second = 0.5 * second + 0.5 * grad * grad
    correct = 1.0 - 0.5**STEP
    new_weight = weight - rate * (
        new_moment / correct / (jnp.sqrt(new_second / correct) + adam_eps) + decay_rate * weight
    )
    new_average = ema_decay * average + (1.0 - ema_decay) * new_weight
    return (new_weight, new_moment, new_second, new_average)


def total(refs, *at):
    value = refs[0][at].astype(f32) if at else refs[0][...].astype(f32)
    for ref in refs[1:]:
        value = value + (ref[at] if at else ref[...]).astype(f32)
    return value


def table_adam_kernel(*refs, terms):
    state, parts, outs = refs[:4], refs[4 : 4 + terms], refs[4 + terms :]
    rows = state[0].shape[0]
    chunk = 64
    for i in range(rows // chunk):
        p = slice(i * chunk, (i + 1) * chunk)
        new = adam(*[s[p, :] for s in state], total(parts, p), 0.3)
        for out, value in zip(outs, new):
            out[p, :] = value


def weight_adam_kernel(*refs, terms, dp, hid):
    first, second, vector, gate = refs[0:4], refs[4:8], refs[8:12], refs[12:16]
    parts, smalls = refs[16 : 16 + terms], refs[16 + terms : 16 + 2 * terms]
    outs = refs[16 + 2 * terms :]
    first_out, second_out, vector_out, gate_out = outs[0:4], outs[4:8], outs[8:12], outs[12:16]
    rows, fold = D // dp, H // dp
    width = (O * EXPERTS) // dp
    new = adam(*[s[...] for s in first], total(parts, slice(0, rows)), 0.04)
    for out, value in zip(first_out, new):
        out[...] = value
    grad = total(parts, slice(rows, rows + fold))
    for i in range((H // hid) // fold):
        p = slice(i * fold, (i + 1) * fold)
        new = adam(*[s[p, :] for s in second], grad[:, i * width : (i + 1) * width], 0.06)
        for out, value in zip(second_out, new):
            out[p, :] = value
    pairs = list(smalls)
    gates = gate[0].shape[0]
    me = lax.axis_index("hid")

    def tree(at):
        values = [s[at].astype(f32) for s in pairs]
        while len(values) > 1:
            values = [values[i] + values[i + 1] for i in range(0, len(values), 2)]
        return values[0]

    new = adam(*[s[...] for s in gate], tree(slice(0, gates)), 0.03)
    for out, value in zip(gate_out, new):
        out[...] = value
    cols = (H * EXPERTS) // hid
    start = pl.multiple_of(16 + me * 16, 16)
    grad = tree(pl.ds(start, 16))[0:3, 0:cols]
    new = adam(*[s[...] for s in vector], grad, 0.2)
    for out, value in zip(vector_out, new):
        out[...] = value


def per_device(
    bag_offsets,
    embed_ids,
    block_owners,
    cotangent,
    table_w,
    table_m,
    table_v,
    table_ema,
    first_w,
    first_m,
    first_v,
    first_ema,
    second_w,
    second_m,
    second_v,
    second_ema,
    vector_w,
    vector_m,
    vector_v,
    vector_ema,
    gate_w,
    gate_m,
    gate_v,
    gate_ema,
):
    dp, hid = lax.axis_size("dp"), lax.axis_size("hid")
    inner = inner_size(dp)
    outer = dp // inner
    events, ids = bag_offsets.shape[0], embed_ids.shape[0]
    rows = events // hid
    slots, feats = table_w.shape
    vocab = block_owners.shape[0] * ROWS_BLOCK
    piece_rows = D // dp + H // dp
    piece_cols = first_w.shape[1]

    table_low, weight_low, *cot_pieces = call(
        functools.partial(low_kernel, hid=hid),
        [
            shape(table_w.shape, bf16),
            shape((piece_rows, piece_cols), bf16),
            *[shape((cotangent.shape[1], rows), bf16) for m in range(hid)],
        ],
        (table_w, first_w, second_w, cotangent.T),
    )
    weight_pieces = gather_dp(weight_low)
    table_pieces = gather_dp(table_low)
    cots = [cot_pieces[0]] + [swap(cot_pieces[m], "hid", m) for m in range(1, hid)]

    weight_here = jnp.stack(weight_pieces)
    weight_hid = {0: weight_here}
    for m in range(2, hid, 2):
        weight_hid[m] = swap(weight_here, "hid", m)
    for m in range(0, hid, 2):
        weight_hid[m + 1] = swap(weight_hid[m], "hid", 1)
    vector_full = lax.all_gather(vector_w, "hid", axis=1, tiled=True)
    vector_full = jnp.pad(vector_full, ((0, 5), (0, 0)))
    span = HALF * EXPERTS
    w1p, w1t, w2p, w2t, columns, turn, turn3, turn3t = call(
        functools.partial(weights_kernel, dp=dp, hid=hid),
        [
            shape((EXPERTS, D, H), bf16),
            shape((EXPERTS, H, D), bf16),
            shape((EXPERTS, H, O), bf16),
            shape((EXPERTS, O, H), bf16),
            shape((3, EXPERTS, H, HALF), f32),
            shape((span, span), bf16),
            shape((O * STREAMS, O * STREAMS), bf16),
            shape((O * STREAMS, O * STREAMS), bf16),
        ],
        (*[weight_hid[m] for m in range(hid)], vector_full),
        scratch=[
            pltpu.VMEM((hid, D, piece_cols), bf16),
            pltpu.VMEM((dp, H, (O * EXPERTS) // dp), bf16),
        ],
        vmem=40,
    )

    lanes = 128
    nexts = jnp.concatenate([bag_offsets[1:], jnp.full((1,), ids, jnp.int32)])
    counts = call(
        counts_kernel,
        shape((events, vocab), bf16),
        (
            bag_offsets,
            embed_ids.reshape(ids // lanes, lanes),
            bag_offsets.reshape(events // lanes, lanes),
            nexts.reshape(events // lanes, lanes),
        ),
        in_specs=[SMEM, VMEM, VMEM, VMEM],
        scratch=[
            pltpu.VMEM((ids // IDS_STEP, IDS_STEP, HALF), jnp.int32),
            pltpu.VMEM((EVENTS_STEP, vocab), f32),
        ],
        vmem=56,
    )
    pooled = call(
        functools.partial(pool_kernel, dp=dp, hid=hid),
        [shape((feats, rows), bf16) for m in range(hid)],
        (block_owners, counts, *table_pieces),
        in_specs=[SMEM] + [VMEM] * (1 + dp),
        scratch=[
            pltpu.VMEM((dp, slots, feats), bf16),
            pltpu.VMEM((vocab, feats), bf16),
            pltpu.VMEM((hid, rows, feats), f32),
            pltpu.SMEM((dp,), jnp.int32),
        ],
        vmem=56,
    )
    xts = [pooled[0]] + [swap(pooled[m], "hid", m) for m in range(1, hid)]

    gates = 16
    gate_pad = jnp.pad(gate_w.T, ((0, gates - gate_w.shape[1]), (0, 0)))
    small_rows = gates + 16 * hid
    mixed_part, small, xt, hidden, d_inner, d_pre, *d_pieces = call(
        functools.partial(main_kernel, hid=hid),
        [
            shape((rows, O * STREAMS), bf16),
            shape((small_rows, D), bf16),
            shape((D, rows), bf16),
            shape((EXPERTS, H, rows), bf16),
            shape((EXPERTS, O, rows), bf16),
            shape((EXPERTS, H, rows), bf16),
            *[shape((feats, rows), bf16) for m in range(hid)],
        ],
        (*xts, *cots, w1p, w1t, w2p, w2t, columns, turn, turn3, turn3t, gate_pad),
        scratch=[
            pltpu.VMEM((O * STREAMS, rows), f32),
            pltpu.VMEM((O * STREAMS, rows), bf16),
            pltpu.VMEM((O * STREAMS, rows), f32),
            pltpu.VMEM((H, rows), f32),
            pltpu.VMEM((H, rows), f32),
            pltpu.VMEM((H, rows), f32),
            pltpu.VMEM((2, H, rows), bf16),
            pltpu.VMEM((D, rows), f32),
            pltpu.VMEM((3, EXPERTS, 8, H), f32),
        ],
        vmem=40,
    )
    mixed = lax.all_gather(mixed_part, "hid", axis=0, tiled=True)
    d_pooled = [d_pieces[0]] + [swap(d_pieces[m], "hid", m) for m in range(1, hid)]

    grads = call(
        functools.partial(grads_kernel, dp=dp, hid=hid),
        [shape((inner, outer, piece_rows, piece_cols), bf16) for m in range(hid)],
        (xt, hidden, d_inner, d_pre, turn),
        scratch=[
            pltpu.VMEM((H * EXPERTS, rows), bf16),
            pltpu.VMEM((D, piece_cols), bf16),
            pltpu.VMEM((H, O * EXPERTS), f32),
        ],
        vmem=40,
    )

    def add(a, b):
        return (a.astype(f32) + b.astype(f32)).astype(bf16)

    half = [add(grads[m], swap(grads[m + 1], "hid", 1)) for m in range(0, hid, 2)]
    small = add(small, swap(small, "hid", 1))
    mine = half[0]
    smalls = [small]
    for m in range(1, hid // 2):
        mine = add(mine, swap(half[m], "hid", 2 * m))
    step = 2
    while step < hid:
        small = add(small, swap(small, "hid", step))
        step *= 2
    near = mine[0]
    for m in range(1, inner):
        near = add(near, swap(mine[m], "dp", m))
    step = 1
    while step < inner:
        small = add(small, swap(small, "dp", step))
        step *= 2
    weight_terms = [near[0]] + [swap(near[m], "dp", m * inner) for m in range(1, outer)]
    small_terms = [small] + [swap(small, "dp", m * inner) for m in range(1, outer)]

    d_table = call(
        functools.partial(table_kernel, dp=dp, hid=hid),
        [shape((slots, feats), bf16) for r in range(dp)],
        (block_owners, counts, *d_pooled),
        in_specs=[SMEM] + [VMEM] * (1 + hid),
        scratch=[
            pltpu.VMEM((feats, events), bf16),
            pltpu.VMEM((vocab, feats), bf16),
            pltpu.VMEM((dp, slots, feats), bf16),
            pltpu.SMEM((dp,), jnp.int32),
        ],
        vmem=56,
    )
    table_terms = []
    for far in reversed(range(outer)):
        value = d_table[far * inner]
        for m in range(1, inner):
            value = add(value, swap(d_table[far * inner + m], "dp", m))
        table_terms.append(swap(value, "dp", far * inner) if far else value)

    table_new = call(
        functools.partial(table_adam_kernel, terms=outer),
        [shape(table_w.shape, f32)] * 4,
        (table_w, table_m, table_v, table_ema, *table_terms),
        vmem=24,
    )
    weights_new = call(
        functools.partial(weight_adam_kernel, terms=outer, dp=dp, hid=hid),
        [shape(first_w.shape, f32)] * 4
        + [shape(second_w.shape, f32)] * 4
        + [shape(vector_w.shape, f32)] * 4
        + [shape((gates, D), f32)] * 4,
        (
            first_w,
            first_m,
            first_v,
            first_ema,
            second_w,
            second_m,
            second_v,
            second_ema,
            vector_w,
            vector_m,
            vector_v,
            vector_ema,
            gate_pad,
            *[jnp.pad(g.T, ((0, gates - g.shape[1]), (0, 0))) for g in (gate_m, gate_v, gate_ema)],
            *weight_terms,
            *small_terms,
        ),
        vmem=24,
    )
    return (
        mixed,
        *table_new,
        *weights_new[0:12],
        *[g[0 : gate_w.shape[1]].T for g in weights_new[12:16]],
    )


def solution(mesh):
    split, spread, whole = P("dp", "hid"), P("hid", "dp"), P()
    return jax.shard_map(
        per_device,
        mesh=mesh,
        in_specs=(P("dp"), P("dp"), whole, split)
        + (split,) * 8
        + (spread,) * 4
        + (P(None, "hid"),) * 4
        + (whole,) * 4,
        out_specs=(P("dp", None),)
        + (split,) * 8
        + (spread,) * 4
        + (P(None, "hid"),) * 4
        + (whole,) * 4,
        check_vma=False,
    )
```

```python
import functools

import jax
import jax.numpy as jnp
from jax import lax
from jax.experimental import pallas as pl
from jax.experimental.pallas import tpu as pltpu
from jax.sharding import PartitionSpec as P

D = 512
H = 256
O = 256
EXPERTS = 6
STREAMS = 3
ROWS_BLOCK = 64
STEP = 5
CAP = 12
HALF = 128
IDS_STEP = 256
EVENTS_STEP = 256

norm_eps = 1e-05
adam_eps = 1e-08
decay_rate = 0.01
ema_decay = 0.9

bf16 = jnp.bfloat16
f32 = jnp.float32
MIB = 1 << 20

STREAM_EXPERTS = ((0, 1, 4, 5), (2, 3, 4, 5), (0, 1, 2, 3, 4, 5))
STREAM_COLS = (0, 4, 8)

VMEM = pl.BlockSpec(memory_space=pltpu.VMEM)
SMEM = pl.BlockSpec(memory_space=pltpu.SMEM)
HBM = pl.BlockSpec(memory_space=pltpu.HBM)
ANY = pl.BlockSpec(memory_space=pl.ANY)


def shape(dims, dtype):
    return jax.ShapeDtypeStruct(tuple(dims), dtype)


def nn(a, b):
    return lax.dot_general(a, b, (((1,), (0,)), ((), ())), preferred_element_type=f32)


def nt(a, b):
    return lax.dot_general(a, b, (((1,), (1,)), ((), ())), preferred_element_type=f32)


def tn(a, b):
    return lax.dot_general(a, b, (((0,), (0,)), ((), ())), preferred_element_type=f32)


def call(kernel, out_shape, args, in_specs=None, scratch=(), vmem=24, us=2.0):
    single = not isinstance(out_shape, (list, tuple))
    outs = [out_shape] if single else list(out_shape)
    result = pl.pallas_call(
        kernel,
        out_shape=outs,
        in_specs=in_specs or [VMEM] * len(args),
        out_specs=[VMEM] * len(outs),
        scratch_shapes=list(scratch),
        compiler_params=pltpu.CompilerParams(vmem_limit_bytes=vmem * MIB),
        cost_estimate=pl.CostEstimate(
            flops=int(us * 1.0e9), bytes_accessed=int(us * 3.0e6), transcendentals=0
        ),
    )(*args)
    return result[0] if single else result


def swap(value, axis, mask):
    count = lax.axis_size(axis)
    return lax.ppermute(value, axis, [(i, i ^ mask) for i in range(count)])


def inner_size(dp_count):
    return 1 << ((dp_count.bit_length() - 1) // 2)


def gather_dp(value):
    count = lax.axis_size("dp")
    inner = inner_size(count)
    far = {0: value}
    for step in reversed(range(1, count // inner)):
        far[step] = swap(value, "dp", step * inner)
    pieces = [None] * count
    for step in [0] + list(reversed(range(1, count // inner))):
        pieces[step * inner] = far[step]
        for near in range(1, inner):
            pieces[step * inner + near] = swap(far[step], "dp", near)
    return pieces


def low_kernel(table_hbm, first_hbm, second_hbm, vector_hbm, cot_hbm, *refs, hid):
    piece, weight_out, cots = refs[0], refs[1], refs[2 : 2 + hid]
    table, first, second, vector, cot, sems = refs[2 + hid :]
    copies = [
        pltpu.make_async_copy(source, target, sems.at[i])
        for i, (source, target) in enumerate(
            (
                (table_hbm, table),
                (first_hbm, first),
                (second_hbm, second),
                (vector_hbm, vector),
                (cot_hbm, cot),
            )
        )
    ]
    for copy in copies:
        copy.start()
    copies[0].wait()
    slots, feats = table.shape
    piece[0:slots, :] = table[...].astype(bf16)
    copies[1].wait()
    copies[2].wait()
    rows = first.shape[0]
    each = weight_out.shape[0] // 3
    fold = each - rows
    folded = jnp.concatenate(
        [second[i * fold : (i + 1) * fold, :] for i in range(second.shape[0] // fold)], axis=1
    )
    for g in range(3):
        lanes = slice(g * feats, (g + 1) * feats)
        for out, start in ((piece, slots), (weight_out, 0)):
            out[start + g * each : start + g * each + rows, :] = first[:, lanes].astype(bf16)
            out[start + g * each + rows : start + (g + 1) * each, :] = folded[:, lanes].astype(bf16)
    copies[3].wait()
    copies[4].wait()
    me = lax.axis_index("hid")
    cols, width = cot.shape[0], cots[0].shape[1]
    rest = vector[...]
    terms = []
    for i in range(3):
        terms.append(rest.astype(bf16).astype(f32))
        rest = rest - terms[i]
    span = vector.shape[1]
    stack = jnp.concatenate(terms + [jnp.zeros((7, span), f32)], axis=0)
    over = jnp.concatenate([stack[:, width:], jnp.zeros((16, 2 * width - span), f32)], axis=1)
    for m in range(hid):
        start = pl.multiple_of((me ^ m) * width, width)
        cots[m][0:cols, :] = cot[:, pl.ds(start, width)]
        cots[m][cols : cols + 16, :] = stack[:, 0:width].astype(bf16)
        cots[m][cols + 16 :, :] = over.astype(bf16)


def counts_kernel(offs_ref, ids_ref, off_ref, nxt_ref, c_ref, idb, acc, *, chunk):
    id_rows, lanes = ids_ref.shape
    vocab = c_ref.shape[1]
    events = off_ref.shape[0] * lanes
    per = IDS_STEP // lanes
    idt = ids_ref[...].T
    for q in range(id_rows):
        idb[q // per, (q % per) * lanes : (q % per + 1) * lanes, :] = jnp.broadcast_to(
            idt[:, q : q + 1], (lanes, HALF)
        ).astype(jnp.int16)
    offt = off_ref[...].T
    nxtt = nxt_ref[...].T
    cols = EVENTS_STEP // lanes
    width = 512
    lane = lax.broadcasted_iota(jnp.int32, (IDS_STEP, HALF), 1).astype(jnp.int16)
    one, zero = jnp.ones((IDS_STEP, HALF), bf16), jnp.zeros((IDS_STEP, HALF), bf16)
    first = jnp.concatenate([offt[:, chunk * cols + i : chunk * cols + i + 1] for i in range(cols)], 0)
    last = jnp.concatenate([nxtt[:, chunk * cols + i : chunk * cols + i + 1] for i in range(cols)], 0)
    acc[...] = jnp.zeros_like(acc)
    low = offs_ref[chunk * EVENTS_STEP]
    if (chunk + 1) * EVENTS_STEP < events:
        high = offs_ref[(chunk + 1) * EVENTS_STEP]
    else:
        high = jnp.int32(id_rows * lanes)

    def body(step, carry):
        place = step * IDS_STEP + lax.broadcasted_iota(jnp.int32, (EVENTS_STEP, IDS_STEP), 1)
        member = jnp.where((place >= first) & (place < last), 1.0, 0.0).astype(bf16)
        ids = idb[step]
        for v in range(vocab // width):
            hot = jnp.concatenate(
                [
                    jnp.where(ids == lane + jnp.int16(v * width + i * HALF), one, zero)
                    for i in range(width // HALF)
                ],
                axis=1,
            )
            acc[:, v * width : (v + 1) * width] += nn(member, hot)
        return carry

    lax.fori_loop(low // IDS_STEP, (high + IDS_STEP - 1) // IDS_STEP, body, 0)
    c_ref[...] = acc[...].astype(bf16)


def each_block(owners_ref, count_ref, owners, body):
    for o in range(owners):
        count_ref[o] = 0

    def step(block, carry):
        owner = owners_ref[block]
        rank = count_ref[owner]
        count_ref[owner] = rank + 1
        body(block, owner, rank)
        return carry

    lax.fori_loop(0, owners_ref.shape[0], step, 0)


def pool_kernel(owners_ref, *refs, chunks, dp, hid):
    counts, pieces = refs[:chunks], refs[chunks : chunks + dp]
    outs = refs[chunks + dp : chunks + dp + hid]
    whole, table, pooled, count_ref = refs[chunks + dp + hid :]
    me_dp, me_hid = lax.axis_index("dp"), lax.axis_index("hid")
    slots = whole.shape[1]
    for r in range(dp):
        whole[me_dp ^ r] = pieces[r][0:slots, :]

    def place(block, owner, rank):
        table[pl.ds(pl.multiple_of(block * ROWS_BLOCK, ROWS_BLOCK), ROWS_BLOCK), :] = whole[
            owner, pl.ds(pl.multiple_of(rank * ROWS_BLOCK, ROWS_BLOCK), ROWS_BLOCK), :
        ]

    each_block(owners_ref, count_ref, dp, place)
    rows = pooled.shape[1]
    per = EVENTS_STEP // rows
    for q in range(hid):
        part = slice((q % per) * rows, (q % per + 1) * rows)
        pooled[q] = nn(counts[q // per][part, :], table[...])
    for m in range(hid):
        outs[m][...] = pooled[me_hid ^ m].T.astype(bf16)


def hot_cv(rows, cols, mult, start):
    group = cols // mult
    col = lax.broadcasted_iota(jnp.int32, (8, cols), 1)
    target = ((col % group) * mult + col // group - start)[0:1]
    row = lax.broadcasted_iota(jnp.int32, (rows, cols), 0)
    return jnp.where(row == target, 1.0, 0.0).astype(bf16)


def hot_vc(rows, cols, mult, start):
    group = rows // mult
    row = lax.broadcasted_iota(jnp.int32, (rows, HALF), 0)
    target = ((row % group) * mult + row // group - start)[:, 0:1]
    col = lax.broadcasted_iota(jnp.int32, (rows, cols), 1)
    return jnp.where(col == target, 1.0, 0.0).astype(bf16)


def weights_kernel(*refs, dp, hid):
    pieces, cots = refs[:hid], refs[hid : 2 * hid]
    w1p, w1t, w2p, w2t, col_ref, q_ref, q3t_ref = refs[2 * hid : 2 * hid + 7]
    w1s, w2s, vecs = refs[2 * hid + 7 :]
    me_dp, me_hid = lax.axis_index("dp"), lax.axis_index("hid")
    rows = D // dp
    fold = H // dp
    each = rows + fold
    width = (O * EXPERTS) // dp
    high = H // hid
    feats = pieces[0].shape[2]
    j_step = w1s.shape[2]
    k_step = w2s.shape[2]
    for r in range(hid):
        j = me_hid ^ r
        for s in range(dp):
            k = me_dp ^ s
            for g in range(3):
                w1s[j, pl.ds(pl.multiple_of(k * rows, rows), rows), g * feats : (g + 1) * feats] = (
                    pieces[r][s, g * each : g * each + rows, :]
                )
            part = jnp.concatenate(
                [pieces[r][s, g * each + rows : (g + 1) * each, :].astype(f32) for g in range(3)],
                axis=1,
            )
            for q in range(high // fold):
                start = pl.multiple_of(j * high + q * fold, fold)
                w2s[k, pl.ds(start, fold), :] = part[:, q * width : (q + 1) * width].astype(bf16)
        cols, near = cots[r].shape[0] - 32, cots[r].shape[1]
        vecs[j] = jnp.concatenate(
            [cots[r][cols : cols + 16, :], cots[r][cols + 16 : cols + 32, 0 : j_step - near]], axis=1
        )
    span = HALF * EXPERTS
    q_ref[...] = hot_cv(span, span, EXPERTS, 0)
    q3t_ref[...] = hot_vc(O * STREAMS, O * STREAMS, STREAMS, 0)
    for half in range(2):
        lanes = slice(half * HALF, (half + 1) * HALF)
        total_p, total_t, total_c = None, None, None
        for i in range(span // j_step):
            w1 = w1s[half * (span // j_step) + i]
            hot = hot_vc(span, j_step, EXPERTS, i * j_step)
            p = nn(w1, q_ref[i * j_step : (i + 1) * j_step, :])
            t = nt(hot, w1)
            c = nt(hot, vecs[half * (span // j_step) + i])
            total_p = p if total_p is None else total_p + p
            total_t = t if total_t is None else total_t + t
            total_c = c if total_c is None else total_c + c
        for e in range(EXPERTS):
            w1p[e, :, lanes] = total_p[:, e * HALF : (e + 1) * HALF].astype(bf16)
            w1t[e, lanes, :] = total_t[e * HALF : (e + 1) * HALF, :].astype(bf16)
        cols = total_c[:, 0:3] + total_c[:, 3:6] + total_c[:, 6:9]
        for e in range(EXPERTS):
            for i in range(3):
                col_ref[i, e, lanes, :] = jnp.broadcast_to(
                    cols[e * HALF : (e + 1) * HALF, i : i + 1], (HALF, HALF)
                )
        total_p, total_t = None, None
        for i in range(span // k_step):
            w2 = w2s[half * (span // k_step) + i]
            p = nn(w2, q_ref[i * k_step : (i + 1) * k_step, :])
            t = nt(hot_vc(span, k_step, EXPERTS, i * k_step), w2)
            total_p = p if total_p is None else total_p + p
            total_t = t if total_t is None else total_t + t
        for e in range(EXPERTS):
            w2p[e, :, lanes] = total_p[:, e * HALF : (e + 1) * HALF].astype(bf16)
            w2t[e, lanes, :] = total_t[e * HALF : (e + 1) * HALF, :].astype(bf16)


def softmax_rows(logits):
    top = jnp.max(logits, axis=0, keepdims=True)
    grown = jnp.exp(logits - top)
    return grown / jnp.sum(grown, axis=0, keepdims=True)


def wide(column, width):
    return jnp.concatenate([column] * (width // HALF), axis=1) if width > HALF else column


def main_kernel(*refs, hid):
    xts, cots = refs[:hid], refs[hid : 2 * hid]
    w1p, w1t, w2p, w2t, col_ref, q_ref, q3t_ref, gate_ref = refs[2 * hid : 2 * hid + 8]
    outs = refs[2 * hid + 8 :]
    mixed_ref, small_ref, xt, hid_ref, dinner_ref, dpre_ref = outs[:6]
    dx_outs = outs[6 : 6 + hid]
    up, upq, mix, work, slope, norm, dout, dx, vec = outs[6 + hid :]
    me = lax.axis_index("hid")
    feats, rows = xts[0].shape
    for m in range(hid):
        j = me ^ m
        xt[pl.ds(pl.multiple_of(j * feats, feats), feats), :] = xts[m][...]
        cols = cots[m].shape[0] - 32
        upq[pl.ds(pl.multiple_of(j * cols, cols), cols), :] = cots[m][0:cols, :]
    up[...] = nn(q3t_ref[...], upq[...])
    gate = gate_ref[...].astype(bf16)
    logits = nn(gate, xt[...])
    chances = [
        softmax_rows(logits[STREAM_COLS[t] : STREAM_COLS[t] + len(STREAM_EXPERTS[t])])
        for t in range(STREAMS)
    ]
    mix[...] = jnp.zeros_like(mix)
    chunk = 64
    parts = [slice(i * chunk, (i + 1) * chunk) for i in range(O // chunk)]
    ones = jnp.ones((8, rows), bf16)
    d_chances = [[None] * len(STREAM_EXPERTS[t]) for t in range(STREAMS)]
    for e in range(EXPERTS):
        streams = [t for t in range(STREAMS) if e in STREAM_EXPERTS[t]]
        coef = {
            t: chances[t][STREAM_EXPERTS[t].index(e) : STREAM_EXPERTS[t].index(e) + 1]
            for t in streams
        }
        work[...] = nn(w1t[e], xt[...])
        for p in parts:
            pre = work[p, :] + wide(col_ref[0, e, p, :], rows)
            phi = 0.5 + 0.5 * lax.erf(pre * 0.7071067811865476)
            hid_ref[e, p, :] = (pre * phi).astype(bf16)
            slope[p, :] = phi + pre * (jnp.exp(-0.5 * pre * pre) * 0.3989422804014327)
        work[...] = nn(w2t[e], hid_ref[e])
        total = jnp.zeros((1, rows), f32)
        for p in parts:
            total = total + jnp.sum(work[p, :], axis=0, keepdims=True)
        mean = total * (1.0 / O)
        total = jnp.zeros((1, rows), f32)
        for p in parts:
            off = work[p, :] - mean
            total = total + jnp.sum(off * off, axis=0, keepdims=True)
        inverse = lax.rsqrt(total * (1.0 / O) + norm_eps)
        sums = {t: jnp.zeros((1, rows), f32) for t in streams}
        first, second = jnp.zeros((1, rows), f32), jnp.zeros((1, rows), f32)
        for i, p in enumerate(parts):
            normed = (work[p, :] - mean) * inverse
            gain = wide(col_ref[1, e, p, :], rows)
            value = normed * gain + wide(col_ref[2, e, p, :], rows)
            grad = None
            for t in streams:
                rows_t = slice(t * O + i * chunk, t * O + (i + 1) * chunk)
                mix[rows_t, :] += value * coef[t]
                upward = up[rows_t, :]
                sums[t] = sums[t] + jnp.sum(upward * value, axis=0, keepdims=True)
                term = upward * coef[t]
                grad = term if grad is None else grad + term
            d_norm = grad * gain
            first = first + jnp.sum(d_norm, axis=0, keepdims=True)
            second = second + jnp.sum(d_norm * normed, axis=0, keepdims=True)
            norm[p, :] = normed
            work[p, :] = d_norm
            dout[0, p, :] = (grad * normed).astype(bf16)
            dout[1, p, :] = grad.astype(bf16)
        for t in streams:
            d_chances[t][STREAM_EXPERTS[t].index(e)] = sums[t]
        first, second = first * (1.0 / O), second * (1.0 / O)
        for p in parts:
            dinner_ref[e, p, :] = ((work[p, :] - first - norm[p, :] * second) * inverse).astype(bf16)
        work[...] = nn(w2p[e], dinner_ref[e])
        for p in parts:
            dpre_ref[e, p, :] = (work[p, :] * slope[p, :]).astype(bf16)
        vec[0, e] = nt(ones, dpre_ref[e])
        vec[1, e] = nt(ones, dout[0])
        vec[2, e] = nt(ones, dout[1])
        back = nn(w1p[e], dpre_ref[e])
        if e == 0:
            dx[...] = back
        else:
            dx[...] += back
    d_logits = []
    for t in range(STREAMS):
        upward = jnp.concatenate(d_chances[t], axis=0)
        g = chances[t]
        d_logits.append(g * (upward - jnp.sum(g * upward, axis=0, keepdims=True)))
    pad = jnp.zeros((gate_ref.shape[0] - 14, rows), f32)
    d_logits = jnp.concatenate(d_logits + [pad], axis=0).astype(bf16)
    dx[...] += tn(gate, d_logits)
    for m in range(hid):
        start = pl.multiple_of((me ^ m) * feats, feats)
        dx_outs[m][...] = dx[pl.ds(start, feats), :].astype(bf16)
    gates = gate_ref.shape[0]
    small_ref[0:gates, :] = nt(d_logits, xt[...]).astype(bf16)
    small_ref[gates:, :] = jnp.zeros((small_ref.shape[0] - gates, small_ref.shape[1]), bf16)
    width = (H * EXPERTS) // hid
    for half in range(2):
        lanes = slice(half * HALF, (half + 1) * HALF)
        stack = jnp.concatenate(
            [
                jnp.concatenate([vec[i, e, 0:1, lanes] for e in range(EXPERTS)], axis=1)
                for i in range(3)
            ]
            + [jnp.zeros((5, HALF * EXPERTS), f32)],
            axis=0,
        ).astype(bf16)
        turned = nt(stack, q_ref[...])
        per = (HALF * EXPERTS) // width
        for i in range(per):
            j = half * per + i
            small_ref[gates + 16 * j : gates + 16 * j + 8, 0:width] = turned[
                :, i * width : (i + 1) * width
            ].astype(bf16)
    mixed_ref[...] = tn(mix[...].astype(bf16), q3t_ref[...]).astype(bf16)


def grads_kernel(xt, hid_ref, dinner_ref, dpre_ref, q_ref, *refs, dp, hid):
    outs = refs[:hid]
    turned, w1g, w2g = refs[hid:]
    me_dp, me_hid = lax.axis_index("dp"), lax.axis_index("hid")
    span = HALF * EXPERTS
    rows = D // dp
    fold = H // dp
    width = (O * EXPERTS) // dp
    high = H // hid
    cols = (H * EXPERTS) // hid
    inner = inner_size(dp)
    whole = [nt(hid_ref[e], dinner_ref[e]).astype(bf16) for e in range(EXPERTS)]
    for half in range(2):
        part = slice(half * HALF, (half + 1) * HALF)
        block = jnp.concatenate([dpre_ref[e, part, :] for e in range(EXPERTS)], axis=0)
        turned[half * span : (half + 1) * span, :] = nn(q_ref[...], block).astype(bf16)
        block = jnp.concatenate([w[:, part] for w in whole], axis=1)
        w2g[:, half * span : (half + 1) * span] = nt(block, q_ref[...])
    for m in range(hid):
        j = me_hid ^ m
        left = turned[pl.ds(pl.multiple_of(j * cols, cols), cols), :]
        w1g[...] = nt(xt[...], left).astype(bf16)
        for near in range(inner):
            for far in range(dp // inner):
                k = me_dp ^ (far * inner + near)
                start = pl.multiple_of(k * rows, rows)
                outs[m][near, far, 0:rows, :] = w1g[pl.ds(start, rows), :]
        start = pl.multiple_of(j * high, high)
        for k in range(dp):
            part = w2g[pl.ds(start, high), k * width : (k + 1) * width]
            folded = jnp.concatenate(
                [part[i * fold : (i + 1) * fold, :] for i in range(high // fold)], axis=1
            ).astype(bf16)
            r = me_dp ^ k
            outs[m][r % inner, r // inner, rows : rows + fold, :] = folded


def table_kernel(owners_ref, *refs, chunks, dp, hid):
    counts, pieces = refs[:chunks], refs[chunks : chunks + hid]
    outs = refs[chunks + hid : chunks + hid + dp]
    back, grads, slots, count_ref = refs[chunks + hid + dp :]
    me_dp, me_hid = lax.axis_index("dp"), lax.axis_index("hid")
    rows = pieces[0].shape[1]
    for m in range(hid):
        start = pl.multiple_of((me_hid ^ m) * rows, rows)
        back[:, pl.ds(start, rows)] = pieces[m][...]
    part = None
    for i in range(chunks):
        p = nn(back[:, i * EVENTS_STEP : (i + 1) * EVENTS_STEP], counts[i][...])
        part = p if part is None else part + p
    grads[...] = part.T.astype(bf16)
    slots[...] = jnp.zeros_like(slots)

    def place(block, owner, rank):
        slots[
            owner ^ me_dp, pl.ds(pl.multiple_of(rank * ROWS_BLOCK, ROWS_BLOCK), ROWS_BLOCK), :
        ] = grads[pl.ds(pl.multiple_of(block * ROWS_BLOCK, ROWS_BLOCK), ROWS_BLOCK), :]

    each_block(owners_ref, count_ref, dp, place)
    for r in range(dp):
        outs[r][...] = slots[r]


def plus(a, b):
    return (a.astype(f32) + b.astype(f32)).astype(bf16)


def core_merge_kernel(*refs, pairs):
    ins, outs = refs[: 2 * pairs], refs[2 * pairs + 1 :]
    for i in range(pairs):
        outs[i][...] = plus(ins[2 * i][...], ins[2 * i + 1][...])


def chip_merge_kernel(*refs, terms, inner):
    parts, small, other, mixed = refs[:terms], refs[terms], refs[terms + 1], refs[terms + 2]
    outs = refs[terms + 3 :]
    for near in range(inner):
        value = parts[0][near].astype(f32)
        for part in parts[1:]:
            value = value + part[near].astype(f32)
        outs[near][...] = value.astype(bf16)
    outs[inner][...] = plus(small[...], other[...])
    outs[inner + 1][...] = mixed[...]


def near_merge_kernel(*refs, terms, outer):
    parts, small, other, outs = refs[:terms], refs[terms], refs[terms + 1], refs[terms + 2 :]
    for far in range(outer):
        outs[far][...] = total(parts, far).astype(bf16)
    outs[outer][...] = plus(small[...], other[...])


def mixed_kernel(*refs, hid):
    out = refs[hid]
    rows = refs[0].shape[0]
    me = lax.axis_index("hid")
    for m in range(hid):
        out[pl.ds(pl.multiple_of((me ^ m) * rows, rows), rows), :] = refs[m][...]


def adam(weight, moment, second, average, grad, rate):
    new_moment = 0.5 * moment + 0.5 * grad
    new_second = 0.5 * second + 0.5 * grad * grad
    correct = 1.0 - 0.5**STEP
    new_weight = weight - rate * (
        new_moment / correct / (jnp.sqrt(new_second / correct) + adam_eps) + decay_rate * weight
    )
    new_average = ema_decay * average + (1.0 - ema_decay) * new_weight
    return (new_weight, new_moment, new_second, new_average)


def total(refs, *at):
    value = refs[0][at].astype(f32) if at else refs[0][...].astype(f32)
    for ref in refs[1:]:
        value = value + (ref[at] if at else ref[...]).astype(f32)
    return value


def table_adam_kernel(*refs, terms):
    state, parts, outs = refs[:4], refs[4 : 4 + terms], refs[4 + terms :]
    rows = state[0].shape[0]
    chunk = 64
    for i in range(rows // chunk):
        p = slice(i * chunk, (i + 1) * chunk)
        new = adam(*[s[p, :] for s in state], total(parts, p), 0.3)
        for out, value in zip(outs, new):
            out[p, :] = value


def weight_adam_kernel(*refs, terms, dp, hid):
    first, second, vector, gate = refs[0:4], refs[4:8], refs[8:12], refs[12:16]
    parts, smalls = refs[16 : 16 + terms], refs[16 + terms : 16 + 2 * terms]
    outs = refs[16 + 2 * terms :]
    first_out, second_out, vector_out, gate_out = outs[0:4], outs[4:8], outs[8:12], outs[12:16]
    rows, fold = D // dp, H // dp
    width = (O * EXPERTS) // dp
    new = adam(*[s[...] for s in first], total(parts, slice(0, rows)), 0.04)
    for out, value in zip(first_out, new):
        out[...] = value
    grad = total(parts, slice(rows, rows + fold))
    for i in range((H // hid) // fold):
        p = slice(i * fold, (i + 1) * fold)
        new = adam(*[s[p, :] for s in second], grad[:, i * width : (i + 1) * width], 0.06)
        for out, value in zip(second_out, new):
            out[p, :] = value
    pairs = list(smalls)
    gates = gate[0].shape[0]
    me = lax.axis_index("hid")

    def tree(at):
        values = [s[at].astype(f32) for s in pairs]
        while len(values) > 1:
            values = [values[i] + values[i + 1] for i in range(0, len(values), 2)]
        return values[0]

    new = adam(*[s[...] for s in gate], tree(slice(0, gates)), 0.03)
    for out, value in zip(gate_out, new):
        out[...] = value
    cols = (H * EXPERTS) // hid
    start = pl.multiple_of(16 + me * 16, 16)
    grad = tree(pl.ds(start, 16))[0:3, 0:cols]
    new = adam(*[s[...] for s in vector], grad, 0.2)
    for out, value in zip(vector_out, new):
        out[...] = value


def per_device(
    bag_offsets,
    embed_ids,
    block_owners,
    cotangent,
    table_w,
    table_m,
    table_v,
    table_ema,
    first_w,
    first_m,
    first_v,
    first_ema,
    second_w,
    second_m,
    second_v,
    second_ema,
    vector_w,
    vector_m,
    vector_v,
    vector_ema,
    gate_w,
    gate_m,
    gate_v,
    gate_ema,
):
    dp, hid = lax.axis_size("dp"), lax.axis_size("hid")
    inner = inner_size(dp)
    outer = dp // inner
    events, ids = bag_offsets.shape[0], embed_ids.shape[0]
    rows = events // hid
    slots, feats = table_w.shape
    vocab = block_owners.shape[0] * ROWS_BLOCK
    piece_rows = D // dp + H // dp
    piece_cols = first_w.shape[1]

    cot_rows = cotangent.shape[1] + 32
    weight_rows = 3 * piece_rows
    piece, weight_low, *cot_pieces = call(
        functools.partial(low_kernel, hid=hid),
        [
            shape((slots + weight_rows, feats), bf16),
            shape((weight_rows, feats), bf16),
            *[shape((cot_rows, rows), bf16) for m in range(hid)],
        ],
        (table_w, first_w, second_w, vector_w, cotangent.T),
        in_specs=[HBM] * 5,
        scratch=[
            pltpu.VMEM(table_w.shape, f32),
            pltpu.VMEM(first_w.shape, f32),
            pltpu.VMEM(second_w.shape, f32),
            pltpu.VMEM(vector_w.shape, f32),
            pltpu.VMEM(cotangent.shape[::-1], bf16),
            pltpu.SemaphoreType.DMA((5,)),
        ],
        vmem=8,
    )
    pieces = gather_dp(piece)
    cots = [cot_pieces[0]] + [swap(cot_pieces[m], "hid", m) for m in range(1, hid)]

    weight_parts = {0: [weight_low] + [p[slots:] for p in pieces[1:]]}
    for m in range(2, hid, 2):
        weight_parts[m] = [swap(w, "hid", m) for w in weight_parts[0]]
    weight_hid = {}
    for m in range(0, hid, 2):
        weight_hid[m] = jnp.stack(weight_parts[m])
        weight_hid[m + 1] = swap(weight_hid[m], "hid", 1)
    span = HALF * EXPERTS
    w1p, w1t, w2p, w2t, columns, turn, turn3t = call(
        functools.partial(weights_kernel, dp=dp, hid=hid),
        [
            shape((EXPERTS, D, H), bf16),
            shape((EXPERTS, H, D), bf16),
            shape((EXPERTS, H, O), bf16),
            shape((EXPERTS, O, H), bf16),
            shape((3, EXPERTS, H, HALF), f32),
            shape((span, span), bf16),
            shape((O * STREAMS, O * STREAMS), bf16),
        ],
        (*[weight_hid[m] for m in range(hid)], *cots),
        scratch=[
            pltpu.VMEM((hid, D, piece_cols), bf16),
            pltpu.VMEM((dp, H, (O * EXPERTS) // dp), bf16),
            pltpu.VMEM((hid, 16, piece_cols), bf16),
        ],
        vmem=32,
        us=8.0,
    )

    lanes = 128
    nexts = jnp.concatenate([bag_offsets[1:], jnp.full((1,), ids, jnp.int32)])
    chunks = events // EVENTS_STEP
    counts = [
        call(
            functools.partial(counts_kernel, chunk=i),
            shape((EVENTS_STEP, vocab), bf16),
            (
                bag_offsets,
                embed_ids.reshape(ids // lanes, lanes),
                bag_offsets.reshape(events // lanes, lanes),
                nexts.reshape(events // lanes, lanes),
            ),
            in_specs=[SMEM, VMEM, VMEM, VMEM],
            scratch=[
                pltpu.VMEM((ids // IDS_STEP, IDS_STEP, HALF), jnp.int16),
                pltpu.VMEM((EVENTS_STEP, vocab), f32),
            ],
            vmem=12 if vocab <= 4096 else 40,
            us=5.0,
        )
        for i in range(chunks)
    ]
    pooled = call(
        functools.partial(pool_kernel, chunks=chunks, dp=dp, hid=hid),
        [shape((feats, rows), bf16) for m in range(hid)],
        (block_owners, *counts, *pieces),
        in_specs=[SMEM] + [VMEM] * (chunks + dp),
        scratch=[
            pltpu.VMEM((dp, slots, feats), bf16),
            pltpu.VMEM((vocab, feats), bf16),
            pltpu.VMEM((hid, rows, feats), f32),
            pltpu.SMEM((dp,), jnp.int32),
        ],
        vmem=20 if vocab <= 4096 else 58,
        us=4.0,
    )
    xts = [pooled[0]] + [swap(pooled[m], "hid", m) for m in range(1, hid)]

    gates = 16
    gate_pad = jnp.pad(gate_w.T, ((0, gates - gate_w.shape[1]), (0, 0)))
    small_rows = gates + 16 * hid
    mixed_part, small, xt, hidden, d_inner, d_pre, *d_pieces = call(
        functools.partial(main_kernel, hid=hid),
        [
            shape((rows, O * STREAMS), bf16),
            shape((small_rows, D), bf16),
            shape((D, rows), bf16),
            shape((EXPERTS, H, rows), bf16),
            shape((EXPERTS, O, rows), bf16),
            shape((EXPERTS, H, rows), bf16),
            *[shape((feats, rows), bf16) for m in range(hid)],
        ],
        (*xts, *cots, w1p, w1t, w2p, w2t, columns, turn, turn3t, gate_pad),
        scratch=[
            pltpu.VMEM((O * STREAMS, rows), f32),
            pltpu.VMEM((O * STREAMS, rows), bf16),
            pltpu.VMEM((O * STREAMS, rows), f32),
            pltpu.VMEM((H, rows), f32),
            pltpu.VMEM((H, rows), f32),
            pltpu.VMEM((H, rows), f32),
            pltpu.VMEM((2, H, rows), bf16),
            pltpu.VMEM((D, rows), f32),
            pltpu.VMEM((3, EXPERTS, 8, H), f32),
        ],
        vmem=24,
        us=10.0,
    )
    d_pooled = [d_pieces[0]] + [swap(d_pieces[m], "hid", m) for m in range(1, hid)]

    grads = call(
        functools.partial(grads_kernel, dp=dp, hid=hid),
        [shape((inner, outer, piece_rows, piece_cols), bf16) for m in range(hid)],
        (xt, hidden, d_inner, d_pre, turn),
        scratch=[
            pltpu.VMEM((H * EXPERTS, rows), bf16),
            pltpu.VMEM((D, piece_cols), bf16),
            pltpu.VMEM((H, O * EXPERTS), f32),
        ],
        vmem=16,
        us=3.0,
    )

    whole_shape = shape(grads[0].shape, bf16)
    small_shape = shape(small.shape, bf16)
    operands = []
    for m in range(0, hid, 2):
        operands += [grads[m], swap(grads[m + 1], "hid", 1)]
    *half, small = call(
        functools.partial(core_merge_kernel, pairs=hid // 2 + 1),
        [whole_shape] * (hid // 2) + [small_shape],
        (*operands, small, swap(small, "hid", 1), d_pooled[hid - 1]),
        in_specs=[VMEM] * (hid + 2) + [ANY],
        us=1.5,
    )
    step = 2
    while step < hid // 2:
        small = plus(small, swap(small, "hid", step))
        step *= 2
    *near, small, mixed_part = call(
        functools.partial(chip_merge_kernel, terms=hid // 2, inner=inner),
        [shape(grads[0].shape[1:], bf16)] * inner + [small_shape, shape(mixed_part.shape, bf16)],
        (half[0], *[swap(half[m], "hid", 2 * m) for m in range(1, hid // 2)])
        + (small, swap(small, "hid", step), mixed_part),
        us=1.5,
    )
    step = 1
    while step < inner // 2:
        small = plus(small, swap(small, "dp", step))
        step *= 2
    *far_parts, small = call(
        functools.partial(near_merge_kernel, terms=inner, outer=outer),
        [shape((piece_rows, piece_cols), bf16)] * outer + [small_shape],
        (near[0], *[swap(near[m], "dp", m) for m in range(1, inner)])
        + (small, swap(small, "dp", step)),
        us=1.5,
    )
    weight_terms = [far_parts[0]] + [swap(far_parts[m], "dp", m * inner) for m in range(1, outer)]
    small_terms = [small] + [swap(small, "dp", m * inner) for m in range(1, outer)]

    mixed_parts = {0: mixed_part}
    for m in range(2, hid, 2):
        mixed_parts[m] = swap(mixed_part, "hid", m)
    for m in range(0, hid, 2):
        mixed_parts[m + 1] = swap(mixed_parts[m], "hid", 1)
    mixed = call(
        functools.partial(mixed_kernel, hid=hid),
        shape((events, O * STREAMS), bf16),
        tuple(mixed_parts[m] for m in range(hid)),
        vmem=8,
        us=2.0,
    )

    d_table = call(
        functools.partial(table_kernel, chunks=chunks, dp=dp, hid=hid),
        [shape((slots, feats), bf16) for r in range(dp)],
        (block_owners, *counts, *d_pooled),
        in_specs=[SMEM] + [VMEM] * (chunks + hid),
        scratch=[
            pltpu.VMEM((feats, events), bf16),
            pltpu.VMEM((vocab, feats), bf16),
            pltpu.VMEM((dp, slots, feats), bf16),
            pltpu.SMEM((dp,), jnp.int32),
        ],
        vmem=20 if vocab <= 4096 else 58,
        us=6.0,
    )
    table_terms = []
    for far in reversed(range(outer)):
        value = d_table[far * inner]
        for m in range(1, inner):
            value = plus(value, swap(d_table[far * inner + m], "dp", m))
        table_terms.append(swap(value, "dp", far * inner) if far else value)

    table_new = call(
        functools.partial(table_adam_kernel, terms=outer),
        [shape(table_w.shape, f32)] * 4,
        (table_w, table_m, table_v, table_ema, *table_terms),
        vmem=8,
    )
    weights_new = call(
        functools.partial(weight_adam_kernel, terms=outer, dp=dp, hid=hid),
        [shape(first_w.shape, f32)] * 4
        + [shape(second_w.shape, f32)] * 4
        + [shape(vector_w.shape, f32)] * 4
        + [shape((gates, D), f32)] * 4,
        (
            first_w,
            first_m,
            first_v,
            first_ema,
            second_w,
            second_m,
            second_v,
            second_ema,
            vector_w,
            vector_m,
            vector_v,
            vector_ema,
            gate_pad,
            *[jnp.pad(g.T, ((0, gates - g.shape[1]), (0, 0))) for g in (gate_m, gate_v, gate_ema)],
            *weight_terms,
            *small_terms,
        ),
        vmem=8,
    )
    return (
        mixed,
        *table_new,
        *weights_new[0:12],
        *[g[0 : gate_w.shape[1]].T for g in weights_new[12:16]],
    )


def solution(mesh):
    split, spread, whole = P("dp", "hid"), P("hid", "dp"), P()
    return jax.shard_map(
        per_device,
        mesh=mesh,
        in_specs=(P("dp"), P("dp"), whole, split)
        + (split,) * 8
        + (spread,) * 4
        + (P(None, "hid"),) * 4
        + (whole,) * 4,
        out_specs=(P("dp", None),)
        + (split,) * 8
        + (spread,) * 4
        + (P(None, "hid"),) * 4
        + (whole,) * 4,
        check_vma=False,
    )
```

```python
import functools

import jax
import jax.numpy as jnp
from jax import lax
from jax.experimental import pallas as pl
from jax.experimental.pallas import tpu as pltpu
from jax.sharding import PartitionSpec as P

D = 512
H = 256
O = 256
EXPERTS = 6
STREAMS = 3
ROWS_BLOCK = 64
STEP = 5
CAP = 12
GATES = 14
HALF = 128
IDS_STEP = 256
EVENTS_STEP = 256

norm_eps = 1e-05
adam_eps = 1e-08
decay_rate = 0.01
ema_decay = 0.9

bf16 = jnp.bfloat16
f32 = jnp.float32
MIB = 1 << 20

STREAM_EXPERTS = ((0, 1, 4, 5), (2, 3, 4, 5), (0, 1, 2, 3, 4, 5))
STREAM_COLS = (0, 4, 8)

VMEM = pl.BlockSpec(memory_space=pltpu.VMEM)
SMEM = pl.BlockSpec(memory_space=pltpu.SMEM)
HBM = pl.BlockSpec(memory_space=pltpu.HBM)
ANY = pl.BlockSpec(memory_space=pl.ANY)


def shape(dims, dtype):
    return jax.ShapeDtypeStruct(tuple(dims), dtype)


def nn(a, b):
    return lax.dot_general(a, b, (((1,), (0,)), ((), ())), preferred_element_type=f32)


def nt(a, b):
    return lax.dot_general(a, b, (((1,), (1,)), ((), ())), preferred_element_type=f32)


def tn(a, b):
    return lax.dot_general(a, b, (((0,), (0,)), ((), ())), preferred_element_type=f32)


def call(kernel, out_shape, args, in_specs=None, scratch=(), vmem=24, us=2.0):
    single = not isinstance(out_shape, (list, tuple))
    outs = [out_shape] if single else list(out_shape)
    result = pl.pallas_call(
        kernel,
        out_shape=outs,
        in_specs=in_specs or [VMEM] * len(args),
        out_specs=[VMEM] * len(outs),
        scratch_shapes=list(scratch),
        compiler_params=pltpu.CompilerParams(vmem_limit_bytes=vmem * MIB),
        cost_estimate=pl.CostEstimate(
            flops=int(us * 1.0e9), bytes_accessed=int(us * 3.0e6), transcendentals=0
        ),
    )(*args)
    return result[0] if single else result


def swap(value, axis, mask):
    count = lax.axis_size(axis)
    return lax.ppermute(value, axis, [(i, i ^ mask) for i in range(count)])


def inner_size(dp_count):
    return 1 << ((dp_count.bit_length() - 1) // 2)


def low_kernel(table_hbm, first_hbm, second_hbm, vector_hbm, cot_hbm, *refs, hid):
    piece, weight_out, cots = refs[0], refs[1], refs[2 : 2 + hid]
    table, first, second, vector, cot, sems = refs[2 + hid :]
    copies = [
        pltpu.make_async_copy(source, target, sems.at[i])
        for i, (source, target) in enumerate(
            (
                (table_hbm, table),
                (first_hbm, first),
                (second_hbm, second),
                (vector_hbm, vector),
                (cot_hbm, cot),
            )
        )
    ]
    for copy in copies:
        copy.start()
    copies[0].wait()
    slots, feats = table.shape
    piece[0:slots, :] = table[...].astype(bf16)
    copies[1].wait()
    copies[2].wait()
    rows = first.shape[0]
    each = weight_out.shape[0] // 3
    fold = each - rows
    folded = jnp.concatenate(
        [second[i * fold : (i + 1) * fold, :] for i in range(second.shape[0] // fold)], axis=1
    )
    for g in range(3):
        lanes = slice(g * feats, (g + 1) * feats)
        for out, start in ((piece, slots), (weight_out, 0)):
            out[start + g * each : start + g * each + rows, :] = first[:, lanes].astype(bf16)
            out[start + g * each + rows : start + (g + 1) * each, :] = folded[:, lanes].astype(bf16)
    copies[3].wait()
    copies[4].wait()
    me = lax.axis_index("hid")
    cols, width = cot.shape[0], cots[0].shape[1]
    rest = vector[...]
    terms = []
    for i in range(3):
        terms.append(rest.astype(bf16).astype(f32))
        rest = rest - terms[i]
    span = vector.shape[1]
    stack = jnp.concatenate(terms + [jnp.zeros((7, span), f32)], axis=0)
    over = jnp.concatenate([stack[:, width:], jnp.zeros((16, 2 * width - span), f32)], axis=1)
    for m in range(hid):
        start = pl.multiple_of((me ^ m) * width, width)
        cots[m][0:cols, :] = cot[:, pl.ds(start, width)]
        cots[m][cols : cols + 16, :] = stack[:, 0:width].astype(bf16)
        cots[m][cols + 16 :, :] = over.astype(bf16)


def counts_kernel(offs_ref, ids_ref, off_ref, nxt_ref, *refs, chunk):
    c_ref, idb, acc = refs[-3:]
    id_rows, lanes = ids_ref.shape
    vocab = c_ref.shape[1]
    events = off_ref.shape[0] * lanes
    per = IDS_STEP // lanes
    idt = ids_ref[...].T
    for q in range(id_rows):
        idb[q // per, (q % per) * lanes : (q % per + 1) * lanes, :] = jnp.broadcast_to(
            idt[:, q : q + 1], (lanes, HALF)
        ).astype(jnp.int16)
    offt = off_ref[...].T
    nxtt = nxt_ref[...].T
    cols = EVENTS_STEP // lanes
    width = 512
    lane = lax.broadcasted_iota(jnp.int32, (IDS_STEP, HALF), 1).astype(jnp.int16)
    one, zero = jnp.ones((IDS_STEP, HALF), bf16), jnp.zeros((IDS_STEP, HALF), bf16)
    first = jnp.concatenate([offt[:, chunk * cols + i : chunk * cols + i + 1] for i in range(cols)], 0)
    last = jnp.concatenate([nxtt[:, chunk * cols + i : chunk * cols + i + 1] for i in range(cols)], 0)
    acc[...] = jnp.zeros_like(acc)
    low = offs_ref[chunk * EVENTS_STEP]
    if (chunk + 1) * EVENTS_STEP < events:
        high = offs_ref[(chunk + 1) * EVENTS_STEP]
    else:
        high = jnp.int32(id_rows * lanes)

    def body(step, carry):
        place = step * IDS_STEP + lax.broadcasted_iota(jnp.int32, (EVENTS_STEP, IDS_STEP), 1)
        member = jnp.where((place >= first) & (place < last), 1.0, 0.0).astype(bf16)
        ids = idb[step]
        for v in range(vocab // width):
            hot = jnp.concatenate(
                [
                    jnp.where(ids == lane + jnp.int16(v * width + i * HALF), one, zero)
                    for i in range(width // HALF)
                ],
                axis=1,
            )
            acc[:, v * width : (v + 1) * width] += nn(member, hot)
        return carry

    lax.fori_loop(low // IDS_STEP, (high + IDS_STEP - 1) // IDS_STEP, body, 0)
    c_ref[...] = acc[...].astype(bf16)


def each_block(owners_ref, count_ref, owners, body):
    for o in range(owners):
        count_ref[o] = 0

    def step(block, carry):
        owner = owners_ref[block]
        rank = count_ref[owner]
        count_ref[owner] = rank + 1
        body(block, owner, rank)
        return carry

    lax.fori_loop(0, owners_ref.shape[0], step, 0)


def pool_kernel(owners_ref, *refs, chunks, dp, hid):
    counts, pieces = refs[:chunks], refs[chunks : chunks + dp]
    outs = refs[chunks + dp : chunks + dp + hid]
    whole, table, pooled, count_ref = refs[chunks + dp + hid :]
    me_dp, me_hid = lax.axis_index("dp"), lax.axis_index("hid")
    slots = whole.shape[1]
    for r in range(dp):
        whole[me_dp ^ r] = pieces[r][0:slots, :]

    def place(block, owner, rank):
        table[pl.ds(pl.multiple_of(block * ROWS_BLOCK, ROWS_BLOCK), ROWS_BLOCK), :] = whole[
            owner, pl.ds(pl.multiple_of(rank * ROWS_BLOCK, ROWS_BLOCK), ROWS_BLOCK), :
        ]

    each_block(owners_ref, count_ref, dp, place)
    rows = pooled.shape[1]
    per = EVENTS_STEP // rows
    for q in range(hid):
        part = slice((q % per) * rows, (q % per + 1) * rows)
        pooled[q] = nn(counts[q // per][part, :], table[...])
    for m in range(hid):
        outs[m][...] = pooled[me_hid ^ m].T.astype(bf16)


def hot_cv(rows, cols, mult, start):
    group = cols // mult
    col = lax.broadcasted_iota(jnp.int32, (8, cols), 1)
    target = ((col % group) * mult + col // group - start)[0:1]
    row = lax.broadcasted_iota(jnp.int32, (rows, cols), 0)
    return jnp.where(row == target, 1.0, 0.0).astype(bf16)


def hot_vc(rows, cols, mult, start):
    group = rows // mult
    row = lax.broadcasted_iota(jnp.int32, (rows, HALF), 0)
    target = ((row % group) * mult + row // group - start)[:, 0:1]
    col = lax.broadcasted_iota(jnp.int32, (rows, cols), 1)
    return jnp.where(col == target, 1.0, 0.0).astype(bf16)


def weights_kernel(*refs, dp, hid):
    inner = inner_size(dp)
    given = hid * inner
    stacks, cots = refs[:given], refs[given : given + hid]
    w1p, w1t, w2p, w2t, col_ref, q_ref, q3t_ref = refs[given + hid : given + hid + 7]
    w1s, w2s, vecs = refs[given + hid + 7 :]
    me_dp, me_hid = lax.axis_index("dp"), lax.axis_index("hid")
    rows = D // dp
    fold = H // dp
    each = rows + fold
    width = (O * EXPERTS) // dp
    high = H // hid
    feats = stacks[0].shape[2]
    j_step = w1s.shape[2]
    k_step = w2s.shape[2]
    for r in range(hid):
        j = me_hid ^ r
        for s in range(dp):
            k = me_dp ^ s
            stack, at = stacks[r * inner + s % inner], s // inner
            for g in range(3):
                w1s[j, pl.ds(pl.multiple_of(k * rows, rows), rows), g * feats : (g + 1) * feats] = (
                    stack[at, g * each : g * each + rows, :]
                )
            part = jnp.concatenate(
                [stack[at, g * each + rows : (g + 1) * each, :].astype(f32) for g in range(3)],
                axis=1,
            )
            for q in range(high // fold):
                start = pl.multiple_of(j * high + q * fold, fold)
                w2s[k, pl.ds(start, fold), :] = part[:, q * width : (q + 1) * width].astype(bf16)
        cols, near = cots[r].shape[0] - 32, cots[r].shape[1]
        vecs[j] = jnp.concatenate(
            [cots[r][cols : cols + 16, :], cots[r][cols + 16 : cols + 32, 0 : j_step - near]], axis=1
        )
    span = HALF * EXPERTS
    q_ref[...] = hot_cv(span, span, EXPERTS, 0)
    q3t_ref[...] = hot_vc(O * STREAMS, O * STREAMS, STREAMS, 0)
    for half in range(2):
        lanes = slice(half * HALF, (half + 1) * HALF)
        total_p, total_t, total_c = None, None, None
        for i in range(span // j_step):
            w1 = w1s[half * (span // j_step) + i]
            hot = hot_vc(span, j_step, EXPERTS, i * j_step)
            p = nn(w1, q_ref[i * j_step : (i + 1) * j_step, :])
            t = nt(hot, w1)
            c = nt(hot, vecs[half * (span // j_step) + i])
            total_p = p if total_p is None else total_p + p
            total_t = t if total_t is None else total_t + t
            total_c = c if total_c is None else total_c + c
        for e in range(EXPERTS):
            w1p[e, :, lanes] = total_p[:, e * HALF : (e + 1) * HALF].astype(bf16)
            w1t[e, lanes, :] = total_t[e * HALF : (e + 1) * HALF, :].astype(bf16)
        cols = total_c[:, 0:3] + total_c[:, 3:6] + total_c[:, 6:9]
        for e in range(EXPERTS):
            for i in range(3):
                col_ref[i, e, lanes, :] = jnp.broadcast_to(
                    cols[e * HALF : (e + 1) * HALF, i : i + 1], (HALF, HALF)
                )
        total_p, total_t = None, None
        for i in range(span // k_step):
            w2 = w2s[half * (span // k_step) + i]
            p = nn(w2, q_ref[i * k_step : (i + 1) * k_step, :])
            t = nt(hot_vc(span, k_step, EXPERTS, i * k_step), w2)
            total_p = p if total_p is None else total_p + p
            total_t = t if total_t is None else total_t + t
        for e in range(EXPERTS):
            w2p[e, :, lanes] = total_p[:, e * HALF : (e + 1) * HALF].astype(bf16)
            w2t[e, lanes, :] = total_t[e * HALF : (e + 1) * HALF, :].astype(bf16)


def small_plan(hid):
    width = (H * EXPERTS) // hid
    whole = D // width
    packed = width // HALF
    rest = -(-GATES // packed)
    used = GATES * whole + rest + 3 * hid
    return width, whole, packed, rest, -(-used // 16) * 16


def softmax_rows(logits):
    top = jnp.max(logits, axis=0, keepdims=True)
    grown = jnp.exp(logits - top)
    return grown / jnp.sum(grown, axis=0, keepdims=True)


def wide(column, width):
    return jnp.concatenate([column] * (width // HALF), axis=1) if width > HALF else column


def main_kernel(*refs, hid):
    xts, cots = refs[:hid], refs[hid : 2 * hid]
    w1p, w1t, w2p, w2t, col_ref, q_ref, q3t_ref, gate_ref = refs[2 * hid : 2 * hid + 8]
    outs = refs[2 * hid + 8 :]
    mixed_ref, small_ref, xt, hid_ref, dinner_ref, dpre_ref = outs[:6]
    dx_outs = outs[6 : 6 + hid]
    up, upq, mix, work, slope, norm, dout, dx, vec = outs[6 + hid :]
    me = lax.axis_index("hid")
    feats, rows = xts[0].shape
    for m in range(hid):
        j = me ^ m
        xt[pl.ds(pl.multiple_of(j * feats, feats), feats), :] = xts[m][...]
        cols = cots[m].shape[0] - 32
        upq[pl.ds(pl.multiple_of(j * cols, cols), cols), :] = cots[m][0:cols, :]
    up[...] = nn(q3t_ref[...], upq[...])
    gate = gate_ref[...].astype(bf16)
    logits = nn(gate, xt[...])
    chances = [
        softmax_rows(logits[STREAM_COLS[t] : STREAM_COLS[t] + len(STREAM_EXPERTS[t])])
        for t in range(STREAMS)
    ]
    mix[...] = jnp.zeros_like(mix)
    chunk = 64
    parts = [slice(i * chunk, (i + 1) * chunk) for i in range(O // chunk)]
    ones = jnp.ones((8, rows), bf16)
    d_chances = [[None] * len(STREAM_EXPERTS[t]) for t in range(STREAMS)]
    for e in range(EXPERTS):
        streams = [t for t in range(STREAMS) if e in STREAM_EXPERTS[t]]
        coef = {
            t: chances[t][STREAM_EXPERTS[t].index(e) : STREAM_EXPERTS[t].index(e) + 1]
            for t in streams
        }
        work[...] = nn(w1t[e], xt[...])
        for p in parts:
            pre = work[p, :] + wide(col_ref[0, e, p, :], rows)
            phi = 0.5 + 0.5 * lax.erf(pre * 0.7071067811865476)
            hid_ref[e, p, :] = (pre * phi).astype(bf16)
            slope[p, :] = phi + pre * (jnp.exp(-0.5 * pre * pre) * 0.3989422804014327)
        work[...] = nn(w2t[e], hid_ref[e])
        total = jnp.zeros((1, rows), f32)
        for p in parts:
            total = total + jnp.sum(work[p, :], axis=0, keepdims=True)
        mean = total * (1.0 / O)
        total = jnp.zeros((1, rows), f32)
        for p in parts:
            off = work[p, :] - mean
            total = total + jnp.sum(off * off, axis=0, keepdims=True)
        inverse = lax.rsqrt(total * (1.0 / O) + norm_eps)
        sums = {t: jnp.zeros((1, rows), f32) for t in streams}
        first, second = jnp.zeros((1, rows), f32), jnp.zeros((1, rows), f32)
        for i, p in enumerate(parts):
            normed = (work[p, :] - mean) * inverse
            gain = wide(col_ref[1, e, p, :], rows)
            value = normed * gain + wide(col_ref[2, e, p, :], rows)
            grad = None
            for t in streams:
                rows_t = slice(t * O + i * chunk, t * O + (i + 1) * chunk)
                mix[rows_t, :] += value * coef[t]
                upward = up[rows_t, :]
                sums[t] = sums[t] + jnp.sum(upward * value, axis=0, keepdims=True)
                term = upward * coef[t]
                grad = term if grad is None else grad + term
            d_norm = grad * gain
            first = first + jnp.sum(d_norm, axis=0, keepdims=True)
            second = second + jnp.sum(d_norm * normed, axis=0, keepdims=True)
            norm[p, :] = normed
            work[p, :] = d_norm
            dout[0, p, :] = (grad * normed).astype(bf16)
            dout[1, p, :] = grad.astype(bf16)
        for t in streams:
            d_chances[t][STREAM_EXPERTS[t].index(e)] = sums[t]
        first, second = first * (1.0 / O), second * (1.0 / O)
        for p in parts:
            dinner_ref[e, p, :] = ((work[p, :] - first - norm[p, :] * second) * inverse).astype(bf16)
        work[...] = nn(w2p[e], dinner_ref[e])
        for p in parts:
            dpre_ref[e, p, :] = (work[p, :] * slope[p, :]).astype(bf16)
        vec[0, e] = nt(ones, dpre_ref[e])
        vec[1, e] = nt(ones, dout[0])
        vec[2, e] = nt(ones, dout[1])
        back = nn(w1p[e], dpre_ref[e])
        if e == 0:
            dx[...] = back
        else:
            dx[...] += back
    d_logits = []
    for t in range(STREAMS):
        upward = jnp.concatenate(d_chances[t], axis=0)
        g = chances[t]
        d_logits.append(g * (upward - jnp.sum(g * upward, axis=0, keepdims=True)))
    pad = jnp.zeros((gate_ref.shape[0] - GATES, rows), f32)
    d_logits = jnp.concatenate(d_logits + [pad], axis=0).astype(bf16)
    dx[...] += tn(gate, d_logits)
    for m in range(hid):
        start = pl.multiple_of((me ^ m) * feats, feats)
        dx_outs[m][...] = dx[pl.ds(start, feats), :].astype(bf16)
    width, whole, packed, rest, small_rows = small_plan(hid)
    d_gate = nt(d_logits, xt[...])[0:GATES]
    lines = [d_gate[:, i * width : (i + 1) * width] for i in range(whole)]
    tail = d_gate[:, whole * width :]
    if rest * packed > GATES:
        tail = jnp.concatenate([tail, jnp.zeros((rest * packed - GATES, HALF), f32)], axis=0)
    tail = jnp.concatenate([tail[i * rest : (i + 1) * rest] for i in range(packed)], axis=1)
    if packed * HALF < width:
        tail = jnp.concatenate([tail, jnp.zeros((rest, width - packed * HALF), f32)], axis=1)
    lines.append(tail)
    for half in range(2):
        lanes = slice(half * HALF, (half + 1) * HALF)
        stack = jnp.concatenate(
            [
                jnp.concatenate([vec[i, e, 0:1, lanes] for e in range(EXPERTS)], axis=1)
                for i in range(3)
            ]
            + [jnp.zeros((5, HALF * EXPERTS), f32)],
            axis=0,
        ).astype(bf16)
        turned = nt(stack, q_ref[...])
        for i in range((HALF * EXPERTS) // width):
            lines.append(turned[0:3, i * width : (i + 1) * width])
    spare = small_rows - sum(line.shape[0] for line in lines)
    if spare:
        lines.append(jnp.zeros((spare, width), f32))
    small_ref[...] = jnp.concatenate(lines, axis=0).astype(bf16)
    mixed_ref[...] = tn(mix[...].astype(bf16), q3t_ref[...]).astype(bf16)


def grads_kernel(xt, hid_ref, dinner_ref, dpre_ref, q_ref, small_ref, order_ref, *refs, dp, hid):
    home, away, turned, w1g, w2g = refs
    me_dp, me_hid = lax.axis_index("dp"), lax.axis_index("hid")
    span = HALF * EXPERTS
    rows = D // dp
    fold = H // dp
    each = rows + fold
    width = (O * EXPERTS) // dp
    high = H // hid
    cols = (H * EXPERTS) // hid
    inner = inner_size(dp)
    outer = dp // inner
    whole = [nt(hid_ref[e], dinner_ref[e]).astype(bf16) for e in range(EXPERTS)]
    for half in range(2):
        part = slice(half * HALF, (half + 1) * HALF)
        block = jnp.concatenate([dpre_ref[e, part, :] for e in range(EXPERTS)], axis=0)
        turned[half * span : (half + 1) * span, :] = nn(q_ref[...], block).astype(bf16)
        block = jnp.concatenate([w[:, part] for w in whole], axis=1)
        w2g[:, half * span : (half + 1) * span] = nt(block, q_ref[...])
    for m in range(hid):
        out, base = (away if m % 2 else home), (m // 2) * dp * each
        j = me_hid ^ m
        left = turned[pl.ds(pl.multiple_of(j * cols, cols), cols), :]
        w1g[...] = nt(xt[...], left).astype(bf16)
        for near in range(inner):
            for far in range(outer):
                k = me_dp ^ (far * inner + near)
                start = pl.multiple_of(k * rows, rows)
                to = base + (near * outer + far) * each
                out[to : to + rows, :] = w1g[pl.ds(start, rows), :]
        start = pl.multiple_of(j * high, high)
        for k in range(dp):
            part = w2g[pl.ds(start, high), k * width : (k + 1) * width]
            folded = jnp.concatenate(
                [part[i * fold : (i + 1) * fold, :] for i in range(high // fold)], axis=1
            ).astype(bf16)
            r = me_dp ^ k
            to = base + ((r % inner) * outer + r // inner) * each + rows
            out[pl.ds(pl.multiple_of(to, fold), fold), :] = folded
    away[(hid // 2) * dp * each :, :] = small_ref[...]


def table_kernel(owners_ref, *refs, chunks, dp, hid):
    counts, pieces = refs[:chunks], refs[chunks : chunks + hid]
    outs = refs[chunks + hid : chunks + hid + dp]
    back, grads, slots, count_ref = refs[chunks + hid + dp :]
    me_dp, me_hid = lax.axis_index("dp"), lax.axis_index("hid")
    rows = pieces[0].shape[1]
    for m in range(hid):
        start = pl.multiple_of((me_hid ^ m) * rows, rows)
        back[:, pl.ds(start, rows)] = pieces[m][...]
    part = None
    for i in range(chunks):
        p = nn(back[:, i * EVENTS_STEP : (i + 1) * EVENTS_STEP], counts[i][...])
        part = p if part is None else part + p
    grads[...] = part.T.astype(bf16)
    slots[...] = jnp.zeros_like(slots)

    def place(block, owner, rank):
        slots[
            owner ^ me_dp, pl.ds(pl.multiple_of(rank * ROWS_BLOCK, ROWS_BLOCK), ROWS_BLOCK), :
        ] = grads[pl.ds(pl.multiple_of(block * ROWS_BLOCK, ROWS_BLOCK), ROWS_BLOCK), :]

    each_block(owners_ref, count_ref, dp, place)
    for r in range(dp):
        outs[r][...] = slots[r]


def total(refs, *at):
    values = [(ref[at] if at else ref[...]).astype(f32) for ref in refs]
    while len(values) > 1:
        values = [values[i] + values[i + 1] for i in range(0, len(values), 2)]
    return values[0]


def plus(a, b):
    return (a.astype(f32) + b.astype(f32)).astype(bf16)


def core_merge_kernel(home, come, small, order_ref, *outs, rows):
    count = len(outs)
    for i in range(count):
        outs[i][0:rows, :] = plus(home[i * rows : (i + 1) * rows, :], come[i * rows : (i + 1) * rows, :])
        outs[i][rows:, :] = plus(small[...], come[count * rows :, :])


def chip_merge_kernel(*refs, terms, rows, inner):
    parts, mixed = refs[:terms], refs[terms]
    outs, mixed_out = refs[terms + 1 : terms + 1 + inner], refs[terms + 1 + inner]
    last = total(parts, slice(inner * rows, None)).astype(bf16)
    for near in range(inner):
        outs[near][0:rows, :] = total(parts, slice(near * rows, (near + 1) * rows)).astype(bf16)
        outs[near][rows:, :] = last
    mixed_out[...] = mixed[...]


def near_merge_kernel(*refs, terms, rows, outer):
    parts, outs = refs[:terms], refs[terms:]
    last = total(parts, slice(outer * rows, None)).astype(bf16)
    for far in range(outer):
        outs[far][0:rows, :] = total(parts, slice(far * rows, (far + 1) * rows)).astype(bf16)
        outs[far][rows:, :] = last


def stack_kernel_ordered(*refs, count, start):
    for r in range(count):
        refs[-1][r] = refs[r][start:, :]


def mixed_kernel(*refs, hid):
    out = refs[hid]
    rows = refs[0].shape[0]
    me = lax.axis_index("hid")
    for m in range(hid):
        out[pl.ds(pl.multiple_of((me ^ m) * rows, rows), rows), :] = refs[m][...]


def adam(weight, moment, second, average, grad, rate):
    new_moment = 0.5 * moment + 0.5 * grad
    new_second = 0.5 * second + 0.5 * grad * grad
    correct = 1.0 - 0.5**STEP
    new_weight = weight - rate * (
        new_moment / correct / (jnp.sqrt(new_second / correct) + adam_eps) + decay_rate * weight
    )
    new_average = ema_decay * average + (1.0 - ema_decay) * new_weight
    return (new_weight, new_moment, new_second, new_average)


def table_adam_kernel(*refs, terms):
    state, parts, outs = refs[:4], refs[4 : 4 + terms], refs[4 + terms :]
    rows = state[0].shape[0]
    chunk = 64
    for i in range(rows // chunk):
        p = slice(i * chunk, (i + 1) * chunk)
        new = adam(*[s[p, :] for s in state], total(parts, p), 0.3)
        for out, value in zip(outs, new):
            out[p, :] = value


def weight_adam_kernel(*refs, terms, dp, hid):
    first, second, vector, gate = refs[0:4], refs[4:8], refs[8:12], refs[12:16]
    parts, outs = refs[16 : 16 + terms], refs[16 + terms :]
    first_out, second_out, vector_out, gate_out = outs[0:4], outs[4:8], outs[8:12], outs[12:16]
    rows, fold = D // dp, H // dp
    width = (O * EXPERTS) // dp
    new = adam(*[s[...] for s in first], total(parts, slice(0, rows)), 0.04)
    for out, value in zip(first_out, new):
        out[...] = value
    grad = total(parts, slice(rows, rows + fold))
    for i in range((H // hid) // fold):
        p = slice(i * fold, (i + 1) * fold)
        new = adam(*[s[p, :] for s in second], grad[:, i * width : (i + 1) * width], 0.06)
        for out, value in zip(second_out, new):
            out[p, :] = value
    small = total(parts, slice(rows + fold, None))
    cols, whole, packed, rest, _ = small_plan(hid)
    tail = small[GATES * whole : GATES * whole + rest]
    tail = jnp.concatenate([tail[:, i * HALF : (i + 1) * HALF] for i in range(packed)], axis=0)
    grad = jnp.concatenate(
        [small[i * GATES : (i + 1) * GATES] for i in range(whole)] + [tail[0:GATES]], axis=1
    )
    new = adam(*[s[...] for s in gate], grad, 0.03)
    for out, value in zip(gate_out, new):
        out[...] = value
    me = lax.axis_index("hid")
    base = GATES * whole + rest
    grad = jnp.zeros((3, cols), f32)
    for j in range(hid):
        grad = jnp.where(me == j, small[base + 3 * j : base + 3 * j + 3], grad)
    new = adam(*[s[...] for s in vector], grad, 0.2)
    for out, value in zip(vector_out, new):
        out[...] = value


def per_device(
    bag_offsets,
    embed_ids,
    block_owners,
    cotangent,
    table_w,
    table_m,
    table_v,
    table_ema,
    first_w,
    first_m,
    first_v,
    first_ema,
    second_w,
    second_m,
    second_v,
    second_ema,
    vector_w,
    vector_m,
    vector_v,
    vector_ema,
    gate_w,
    gate_m,
    gate_v,
    gate_ema,
):
    dp, hid = lax.axis_size("dp"), lax.axis_size("hid")
    inner = inner_size(dp)
    outer = dp // inner
    events, ids = bag_offsets.shape[0], embed_ids.shape[0]
    rows = events // hid
    slots, feats = table_w.shape
    vocab = block_owners.shape[0] * ROWS_BLOCK
    piece_rows = D // dp + H // dp
    piece_cols = first_w.shape[1]

    cot_rows = cotangent.shape[1] + 32
    weight_rows = 3 * piece_rows
    piece, weight_low, *cot_pieces = call(
        functools.partial(low_kernel, hid=hid),
        [
            shape((slots + weight_rows, feats), bf16),
            shape((weight_rows, feats), bf16),
            *[shape((cot_rows, rows), bf16) for m in range(hid)],
        ],
        (table_w, first_w, second_w, vector_w, cotangent.T),
        in_specs=[HBM] * 5,
        scratch=[
            pltpu.VMEM(table_w.shape, f32),
            pltpu.VMEM(first_w.shape, f32),
            pltpu.VMEM(second_w.shape, f32),
            pltpu.VMEM(vector_w.shape, f32),
            pltpu.VMEM(cotangent.shape[::-1], bf16),
            pltpu.SemaphoreType.DMA((5,)),
        ],
        vmem=8,
    )
    cots = [cot_pieces[0]] + [swap(cot_pieces[m], "hid", m) for m in range(1, hid)]
    nexts = jnp.concatenate([bag_offsets[1:], jnp.full((1,), ids, jnp.int32)])
    lanes = 128
    chunks = events // EVENTS_STEP

    def count_bags(i, *order):
        return call(
            functools.partial(counts_kernel, chunk=i),
            shape((EVENTS_STEP, vocab), bf16),
            (
                bag_offsets,
                embed_ids.reshape(ids // lanes, lanes),
                bag_offsets.reshape(events // lanes, lanes),
                nexts.reshape(events // lanes, lanes),
                *order,
            ),
            in_specs=[SMEM, VMEM, VMEM, VMEM] + [ANY] * len(order),
            scratch=[
                pltpu.VMEM((ids // IDS_STEP, IDS_STEP, HALF), jnp.int16),
                pltpu.VMEM((EVENTS_STEP, vocab), f32),
            ],
            vmem=12 if vocab <= 4096 else 40,
            us=5.0,
        )

    far_pieces = [piece] + [None] * (outer - 1)
    for step in reversed(range(1, outer)):
        far_pieces[step] = swap(piece, "dp", step * inner)
    counts = [count_bags(i) for i in range(chunks // 2)]
    groups = [far_pieces] + [[swap(p, "dp", near) for p in far_pieces] for near in range(1, inner)]

    def stack(group, *order):
        return call(
            functools.partial(stack_kernel_ordered, count=outer, start=slots),
            shape((outer, weight_rows, feats), bf16),
            (*group, *order),
            in_specs=[VMEM] * outer + [ANY] * len(order),
            vmem=8,
            us=0.7,
        )

    stacks = {(0, 0): stack(groups[0], *counts)}
    counts += [count_bags(i, stacks[0, 0]) for i in range(chunks // 2, chunks)]
    for near in range(1, inner):
        stacks[0, near] = stack(groups[near])
    for near in range(inner):
        for m in range(2, hid, 2):
            stacks[m, near] = swap(stacks[0, near], "hid", m)
        for m in range(0, hid, 2):
            stacks[m + 1, near] = swap(stacks[m, near], "hid", 1)
    pieces = [groups[r % inner][r // inner] for r in range(dp)]
    span = HALF * EXPERTS
    w1p, w1t, w2p, w2t, columns, turn, turn3t = call(
        functools.partial(weights_kernel, dp=dp, hid=hid),
        [
            shape((EXPERTS, D, H), bf16),
            shape((EXPERTS, H, D), bf16),
            shape((EXPERTS, H, O), bf16),
            shape((EXPERTS, O, H), bf16),
            shape((3, EXPERTS, H, HALF), f32),
            shape((span, span), bf16),
            shape((O * STREAMS, O * STREAMS), bf16),
        ],
        (*[stacks[m, near] for m in range(hid) for near in range(inner)], *cots),
        scratch=[
            pltpu.VMEM((hid, D, piece_cols), bf16),
            pltpu.VMEM((dp, H, (O * EXPERTS) // dp), bf16),
            pltpu.VMEM((hid, 16, piece_cols), bf16),
        ],
        vmem=32,
        us=8.0,
    )

    pooled = call(
        functools.partial(pool_kernel, chunks=chunks, dp=dp, hid=hid),
        [shape((feats, rows), bf16) for m in range(hid)],
        (block_owners, *counts, *pieces),
        in_specs=[SMEM] + [VMEM] * (chunks + dp),
        scratch=[
            pltpu.VMEM((dp, slots, feats), bf16),
            pltpu.VMEM((vocab, feats), bf16),
            pltpu.VMEM((hid, rows, feats), f32),
            pltpu.SMEM((dp,), jnp.int32),
        ],
        vmem=20 if vocab <= 4096 else 58,
        us=4.0,
    )
    xts = [pooled[0]] + [swap(pooled[m], "hid", m) for m in range(1, hid)]

    gates = 16
    gate_pad = jnp.pad(gate_w.T, ((0, gates - gate_w.shape[1]), (0, 0)))
    small_rows = small_plan(hid)[-1]
    mixed_part, small, xt, hidden, d_inner, d_pre, *d_pieces = call(
        functools.partial(main_kernel, hid=hid),
        [
            shape((rows, O * STREAMS), bf16),
            shape((small_rows, piece_cols), bf16),
            shape((D, rows), bf16),
            shape((EXPERTS, H, rows), bf16),
            shape((EXPERTS, O, rows), bf16),
            shape((EXPERTS, H, rows), bf16),
            *[shape((feats, rows), bf16) for m in range(hid)],
        ],
        (*xts, *cots, w1p, w1t, w2p, w2t, columns, turn, turn3t, gate_pad),
        scratch=[
            pltpu.VMEM((O * STREAMS, rows), f32),
            pltpu.VMEM((O * STREAMS, rows), bf16),
            pltpu.VMEM((O * STREAMS, rows), f32),
            pltpu.VMEM((H, rows), f32),
            pltpu.VMEM((H, rows), f32),
            pltpu.VMEM((H, rows), f32),
            pltpu.VMEM((2, H, rows), bf16),
            pltpu.VMEM((D, rows), f32),
            pltpu.VMEM((3, EXPERTS, 8, H), f32),
        ],
        vmem=24,
        us=10.0,
    )
    d_pooled = [d_pieces[0]] + [swap(d_pieces[m], "hid", m) for m in range(1, hid)]

    some = dp * piece_rows
    home, away = call(
        functools.partial(grads_kernel, dp=dp, hid=hid),
        [
            shape((hid // 2 * some, piece_cols), bf16),
            shape((hid // 2 * some + small_rows, piece_cols), bf16),
        ],
        (xt, hidden, d_inner, d_pre, turn, small, d_pooled[1]),
        in_specs=[VMEM] * 6 + [ANY],
        scratch=[
            pltpu.VMEM((H * EXPERTS, rows), bf16),
            pltpu.VMEM((D, piece_cols), bf16),
            pltpu.VMEM((H, O * EXPERTS), f32),
        ],
        vmem=16,
        us=3.0,
    )

    half = call(
        functools.partial(core_merge_kernel, rows=some),
        [shape((some + small_rows, piece_cols), bf16)] * (hid // 2),
        (home, swap(away, "hid", 1), small, d_pooled[hid - 1]),
        in_specs=[VMEM] * 3 + [ANY],
        vmem=12,
        us=1.0,
    )
    *near, mixed_part = call(
        functools.partial(chip_merge_kernel, terms=hid // 2, rows=some // inner, inner=inner),
        [shape((some // inner + small_rows, piece_cols), bf16)] * inner
        + [shape(mixed_part.shape, bf16)],
        (half[0], *[swap(half[m], "hid", 2 * m) for m in range(1, hid // 2)], mixed_part),
        vmem=12,
        us=1.0,
    )
    far_parts = call(
        functools.partial(near_merge_kernel, terms=inner, rows=piece_rows, outer=outer),
        [shape((piece_rows + small_rows, piece_cols), bf16)] * outer,
        (near[0], *[swap(near[m], "dp", m) for m in range(1, inner)]),
        vmem=12,
        us=1.0,
    )
    weight_terms = [far_parts[0]] + [swap(far_parts[m], "dp", m * inner) for m in range(1, outer)]

    mixed_parts = {0: mixed_part}
    for m in range(2, hid, 2):
        mixed_parts[m] = swap(mixed_part, "hid", m)
    for m in range(0, hid, 2):
        mixed_parts[m + 1] = swap(mixed_parts[m], "hid", 1)
    mixed = call(
        functools.partial(mixed_kernel, hid=hid),
        shape((events, O * STREAMS), bf16),
        tuple(mixed_parts[m] for m in range(hid)),
        vmem=8,
        us=2.0,
    )

    d_table = call(
        functools.partial(table_kernel, chunks=chunks, dp=dp, hid=hid),
        [shape((slots, feats), bf16) for r in range(dp)],
        (block_owners, *counts, *d_pooled),
        in_specs=[SMEM] + [VMEM] * (chunks + hid),
        scratch=[
            pltpu.VMEM((feats, events), bf16),
            pltpu.VMEM((vocab, feats), bf16),
            pltpu.VMEM((dp, slots, feats), bf16),
            pltpu.SMEM((dp,), jnp.int32),
        ],
        vmem=20 if vocab <= 4096 else 58,
        us=6.0,
    )
    table_terms = []
    for far in reversed(range(outer)):
        value = d_table[far * inner]
        for m in range(1, inner):
            value = plus(value, swap(d_table[far * inner + m], "dp", m))
        table_terms.append(swap(value, "dp", far * inner) if far else value)

    table_new = call(
        functools.partial(table_adam_kernel, terms=outer),
        [shape(table_w.shape, f32)] * 4,
        (table_w, table_m, table_v, table_ema, *table_terms),
        vmem=8,
    )
    weights_new = call(
        functools.partial(weight_adam_kernel, terms=outer, dp=dp, hid=hid),
        [shape(first_w.shape, f32)] * 4
        + [shape(second_w.shape, f32)] * 4
        + [shape(vector_w.shape, f32)] * 4
        + [shape((GATES, D), f32)] * 4,
        (
            first_w,
            first_m,
            first_v,
            first_ema,
            second_w,
            second_m,
            second_v,
            second_ema,
            vector_w,
            vector_m,
            vector_v,
            vector_ema,
            *[g.T for g in (gate_w, gate_m, gate_v, gate_ema)],
            *weight_terms,
        ),
        vmem=8,
    )
    return (
        mixed,
        *table_new,
        *weights_new[0:12],
        *[g.T for g in weights_new[12:16]],
    )


def solution(mesh):
    split, spread, whole = P("dp", "hid"), P("hid", "dp"), P()
    return jax.shard_map(
        per_device,
        mesh=mesh,
        in_specs=(P("dp"), P("dp"), whole, split)
        + (split,) * 8
        + (spread,) * 4
        + (P(None, "hid"),) * 4
        + (whole,) * 4,
        out_specs=(P("dp", None),)
        + (split,) * 8
        + (spread,) * 4
        + (P(None, "hid"),) * 4
        + (whole,) * 4,
        check_vma=False,
    )
```

```python
import functools

import jax
import jax.numpy as jnp
from jax import lax
from jax.experimental import pallas as pl
from jax.experimental.pallas import tpu as pltpu
from jax.sharding import PartitionSpec as P

D = 512
H = 256
O = 256
EXPERTS = 6
STREAMS = 3
ROWS_BLOCK = 64
STEP = 5
CAP = 12
GATES = 14
HALF = 128
IDS_STEP = 256
EVENTS_STEP = 256

norm_eps = 1e-05
adam_eps = 1e-08
decay_rate = 0.01
ema_decay = 0.9

bf16 = jnp.bfloat16
f32 = jnp.float32
MIB = 1 << 20

STREAM_EXPERTS = ((0, 1, 4, 5), (2, 3, 4, 5), (0, 1, 2, 3, 4, 5))
STREAM_COLS = (0, 4, 8)

VMEM = pl.BlockSpec(memory_space=pltpu.VMEM)
SMEM = pl.BlockSpec(memory_space=pltpu.SMEM)
HBM = pl.BlockSpec(memory_space=pltpu.HBM)
ANY = pl.BlockSpec(memory_space=pl.ANY)


def shape(dims, dtype):
    return jax.ShapeDtypeStruct(tuple(dims), dtype)


def nn(a, b):
    return lax.dot_general(a, b, (((1,), (0,)), ((), ())), preferred_element_type=f32)


def nt(a, b):
    return lax.dot_general(a, b, (((1,), (1,)), ((), ())), preferred_element_type=f32)


def tn(a, b):
    return lax.dot_general(a, b, (((0,), (0,)), ((), ())), preferred_element_type=f32)


def call(kernel, out_shape, args, in_specs=None, scratch=(), vmem=24, us=2.0):
    single = not isinstance(out_shape, (list, tuple))
    outs = [out_shape] if single else list(out_shape)
    result = pl.pallas_call(
        kernel,
        out_shape=outs,
        in_specs=in_specs or [VMEM] * len(args),
        out_specs=[VMEM] * len(outs),
        scratch_shapes=list(scratch),
        compiler_params=pltpu.CompilerParams(vmem_limit_bytes=vmem * MIB),
        cost_estimate=pl.CostEstimate(
            flops=int(us * 1.0e9), bytes_accessed=int(us * 3.0e6), transcendentals=0
        ),
    )(*args)
    return result[0] if single else result


def swap(value, axis, mask):
    count = lax.axis_size(axis)
    return lax.ppermute(value, axis, [(i, i ^ mask) for i in range(count)])


def inner_size(dp_count):
    return 1 << ((dp_count.bit_length() - 1) // 2)


def low_kernel(table_hbm, first_hbm, second_hbm, vector_hbm, cot_hbm, *refs, hid):
    piece, keep, cots = refs[0], refs[1], refs[2 : 2 + hid]
    table, first, second, vector, cot, sems = refs[2 + hid :]
    copies = [
        pltpu.make_async_copy(source, target, sems.at[i])
        for i, (source, target) in enumerate(
            (
                (table_hbm, table),
                (first_hbm, first),
                (second_hbm, second),
                (vector_hbm, vector),
                (cot_hbm, cot),
            )
        )
    ]
    for copy in copies:
        copy.start()
    copies[0].wait()
    slots, feats = table.shape
    for out in (piece, keep):
        out[0:slots, :] = table[...].astype(bf16)
    copies[1].wait()
    copies[2].wait()
    rows = first.shape[0]
    each = (piece.shape[0] - slots) // 3
    fold = each - rows
    folded = jnp.concatenate(
        [second[i * fold : (i + 1) * fold, :] for i in range(second.shape[0] // fold)], axis=1
    )
    for g in range(3):
        lanes = slice(g * feats, (g + 1) * feats)
        start = slots + g * each
        for out in (piece, keep):
            out[start : start + rows, :] = first[:, lanes].astype(bf16)
            out[start + rows : start + each, :] = folded[:, lanes].astype(bf16)
    copies[3].wait()
    copies[4].wait()
    me = lax.axis_index("hid")
    cols, width = cot.shape[0], cots[0].shape[1]
    rest = vector[...]
    terms = []
    for i in range(3):
        terms.append(rest.astype(bf16).astype(f32))
        rest = rest - terms[i]
    span = vector.shape[1]
    stack = jnp.concatenate(terms + [jnp.zeros((7, span), f32)], axis=0)
    over = jnp.concatenate([stack[:, width:], jnp.zeros((16, 2 * width - span), f32)], axis=1)
    for m in range(hid):
        start = pl.multiple_of((me ^ m) * width, width)
        cots[m][0:cols, :] = cot[:, pl.ds(start, width)]
        cots[m][cols : cols + 16, :] = stack[:, 0:width].astype(bf16)
        cots[m][cols + 16 :, :] = over.astype(bf16)


def counts_kernel(offs_ref, ids_ref, off_ref, nxt_ref, *refs, chunk):
    c_ref, idb, acc = refs[-3:]
    id_rows, lanes = ids_ref.shape
    vocab = c_ref.shape[1]
    events = off_ref.shape[0] * lanes
    per = IDS_STEP // lanes
    idt = ids_ref[...].T
    for q in range(id_rows):
        idb[q // per, (q % per) * lanes : (q % per + 1) * lanes, :] = jnp.broadcast_to(
            idt[:, q : q + 1], (lanes, HALF)
        ).astype(jnp.int16)
    offt = off_ref[...].T
    nxtt = nxt_ref[...].T
    cols = EVENTS_STEP // lanes
    width = 512
    lane = lax.broadcasted_iota(jnp.int32, (IDS_STEP, HALF), 1).astype(jnp.int16)
    one, zero = jnp.ones((IDS_STEP, HALF), bf16), jnp.zeros((IDS_STEP, HALF), bf16)
    first = jnp.concatenate([offt[:, chunk * cols + i : chunk * cols + i + 1] for i in range(cols)], 0)
    last = jnp.concatenate([nxtt[:, chunk * cols + i : chunk * cols + i + 1] for i in range(cols)], 0)
    acc[...] = jnp.zeros_like(acc)
    low = offs_ref[chunk * EVENTS_STEP]
    if (chunk + 1) * EVENTS_STEP < events:
        high = offs_ref[(chunk + 1) * EVENTS_STEP]
    else:
        high = jnp.int32(id_rows * lanes)

    def body(step, carry):
        place = step * IDS_STEP + lax.broadcasted_iota(jnp.int32, (EVENTS_STEP, IDS_STEP), 1)
        member = jnp.where((place >= first) & (place < last), 1.0, 0.0).astype(bf16)
        ids = idb[step]
        for v in range(vocab // width):
            hot = jnp.concatenate(
                [
                    jnp.where(ids == lane + jnp.int16(v * width + i * HALF), one, zero)
                    for i in range(width // HALF)
                ],
                axis=1,
            )
            acc[:, v * width : (v + 1) * width] += nn(member, hot)
        return carry

    lax.fori_loop(low // IDS_STEP, (high + IDS_STEP - 1) // IDS_STEP, body, 0)
    c_ref[...] = acc[...].astype(bf16)


def each_block(owners_ref, count_ref, owners, body):
    for o in range(owners):
        count_ref[o] = 0

    def step(block, carry):
        owner = owners_ref[block]
        rank = count_ref[owner]
        count_ref[owner] = rank + 1
        body(block, owner, rank)
        return carry

    lax.fori_loop(0, owners_ref.shape[0], step, 0)


def pool_kernel(owners_ref, *refs, chunks, dp, hid):
    counts, pieces = refs[:chunks], refs[chunks : chunks + dp]
    outs = refs[chunks + dp : chunks + dp + hid]
    whole, table, pooled, count_ref = refs[chunks + dp + hid :]
    me_dp, me_hid = lax.axis_index("dp"), lax.axis_index("hid")
    slots = whole.shape[1]
    for r in range(dp):
        whole[me_dp ^ r] = pieces[r][0:slots, :]

    def place(block, owner, rank):
        table[pl.ds(pl.multiple_of(block * ROWS_BLOCK, ROWS_BLOCK), ROWS_BLOCK), :] = whole[
            owner, pl.ds(pl.multiple_of(rank * ROWS_BLOCK, ROWS_BLOCK), ROWS_BLOCK), :
        ]

    each_block(owners_ref, count_ref, dp, place)
    rows = pooled.shape[1]
    per = EVENTS_STEP // rows
    for q in range(hid):
        part = slice((q % per) * rows, (q % per + 1) * rows)
        pooled[q] = nn(counts[q // per][part, :], table[...])
    for m in range(hid):
        outs[m][...] = pooled[me_hid ^ m].T.astype(bf16)


def hot_cv(rows, cols, mult, start):
    group = cols // mult
    col = lax.broadcasted_iota(jnp.int32, (8, cols), 1)
    target = ((col % group) * mult + col // group - start)[0:1]
    row = lax.broadcasted_iota(jnp.int32, (rows, cols), 0)
    return jnp.where(row == target, 1.0, 0.0).astype(bf16)


def hot_vc(rows, cols, mult, start):
    group = rows // mult
    row = lax.broadcasted_iota(jnp.int32, (rows, HALF), 0)
    target = ((row % group) * mult + row // group - start)[:, 0:1]
    col = lax.broadcasted_iota(jnp.int32, (rows, cols), 1)
    return jnp.where(col == target, 1.0, 0.0).astype(bf16)


def turns_kernel(*refs, hid):
    cots = refs[:hid]
    col_ref, q_ref, q3t_ref, vecs = refs[hid:]
    me_hid = lax.axis_index("hid")
    j_step = vecs.shape[2]
    for r in range(hid):
        cols, near = cots[r].shape[0] - 32, cots[r].shape[1]
        vecs[me_hid ^ r] = jnp.concatenate(
            [cots[r][cols : cols + 16, :], cots[r][cols + 16 : cols + 32, 0 : j_step - near]], axis=1
        )
    span = HALF * EXPERTS
    q_ref[...] = hot_cv(span, span, EXPERTS, 0)
    q3t_ref[...] = hot_vc(O * STREAMS, O * STREAMS, STREAMS, 0)
    for half in range(2):
        lanes = slice(half * HALF, (half + 1) * HALF)
        value = None
        for i in range(span // j_step):
            c = nt(hot_vc(span, j_step, EXPERTS, i * j_step), vecs[half * (span // j_step) + i])
            value = c if value is None else value + c
        cols = value[:, 0:3] + value[:, 3:6] + value[:, 6:9]
        for e in range(EXPERTS):
            for i in range(3):
                col_ref[i, e, lanes, :] = jnp.broadcast_to(
                    cols[e * HALF : (e + 1) * HALF, i : i + 1], (HALF, HALF)
                )


def weights_kernel(*refs, dp, hid):
    inner = inner_size(dp)
    given = hid
    stacks, q_ref = refs[:given], refs[given]
    w1p, w2p = refs[given + 1 : given + 3]
    w1s, w2s = refs[given + 3 :]
    me_dp, me_hid = lax.axis_index("dp"), lax.axis_index("hid")
    rows = D // dp
    fold = H // dp
    each = rows + fold
    width = (O * EXPERTS) // dp
    high = H // hid
    feats = stacks[0].shape[-1]
    j_step = w1s.shape[2]
    k_step = w2s.shape[2]
    for r in range(hid):
        j = me_hid ^ r
        for s in range(dp):
            k = me_dp ^ s
            near, at = s % inner, s // inner
            for g in range(3):
                w1s[j, pl.ds(pl.multiple_of(k * rows, rows), rows), g * feats : (g + 1) * feats] = (
                    stacks[r][near, at, g * each : g * each + rows, :]
                )
            part = jnp.concatenate(
                [stacks[r][near, at, g * each + rows : (g + 1) * each, :].astype(f32) for g in range(3)],
                axis=1,
            )
            for q in range(high // fold):
                start = pl.multiple_of(j * high + q * fold, fold)
                w2s[k, pl.ds(start, fold), :] = part[:, q * width : (q + 1) * width].astype(bf16)
    span = HALF * EXPERTS
    for half in range(2):
        lanes = slice(half * HALF, (half + 1) * HALF)
        for step, source, out in ((j_step, w1s, w1p), (k_step, w2s, w2p)):
            value = None
            for i in range(span // step):
                p = nn(source[half * (span // step) + i], q_ref[i * step : (i + 1) * step, :])
                value = p if value is None else value + p
            for e in range(EXPERTS):
                out[e, :, lanes] = value[:, e * HALF : (e + 1) * HALF].astype(bf16)


def small_plan(hid):
    width = (H * EXPERTS) // hid
    whole = D // width
    packed = width // HALF
    rest = -(-GATES // packed)
    used = GATES * whole + rest + 3 * hid
    return width, whole, packed, rest, -(-used // 16) * 16


def softmax_rows(logits):
    top = jnp.max(logits, axis=0, keepdims=True)
    grown = jnp.exp(logits - top)
    return grown / jnp.sum(grown, axis=0, keepdims=True)


def wide(column, width):
    return jnp.concatenate([column] * (width // HALF), axis=1) if width > HALF else column


def main_kernel(*refs, dp, hid):
    xts, cots = refs[:hid], refs[hid : 2 * hid]
    w1p, w2p, col_ref, q_ref, q3t_ref, gate_ref = refs[2 * hid : 2 * hid + 6]
    outs = refs[2 * hid + 6 :]
    mixed_ref, small_ref, home, away = outs[:4]
    dx_outs = outs[4 : 4 + hid]
    xt, hid_ref, dinner_ref, dpre_ref, up, upq, mix, work, slope, norm, dout, dx, vec = outs[
        4 + hid : 17 + hid
    ]
    turned, w1g, w2n, w2g = outs[17 + hid :]
    me = lax.axis_index("hid")
    feats, rows = xts[0].shape
    for m in range(hid):
        j = me ^ m
        xt[pl.ds(pl.multiple_of(j * feats, feats), feats), :] = xts[m][...]
        cols = cots[m].shape[0] - 32
        upq[pl.ds(pl.multiple_of(j * cols, cols), cols), :] = cots[m][0:cols, :]
    up[...] = nn(q3t_ref[...], upq[...])
    gate = gate_ref[...].astype(bf16)
    logits = nn(gate, xt[...])
    chances = [
        softmax_rows(logits[STREAM_COLS[t] : STREAM_COLS[t] + len(STREAM_EXPERTS[t])])
        for t in range(STREAMS)
    ]
    mix[...] = jnp.zeros_like(mix)
    chunk = 64
    parts = [slice(i * chunk, (i + 1) * chunk) for i in range(O // chunk)]
    ones = jnp.ones((8, rows), bf16)
    d_chances = [[None] * len(STREAM_EXPERTS[t]) for t in range(STREAMS)]
    for e in range(EXPERTS):
        streams = [t for t in range(STREAMS) if e in STREAM_EXPERTS[t]]
        coef = {
            t: chances[t][STREAM_EXPERTS[t].index(e) : STREAM_EXPERTS[t].index(e) + 1]
            for t in streams
        }
        work[...] = tn(w1p[e], xt[...])
        for p in parts:
            pre = work[p, :] + wide(col_ref[0, e, p, :], rows)
            phi = 0.5 + 0.5 * lax.erf(pre * 0.7071067811865476)
            hid_ref[e, p, :] = (pre * phi).astype(bf16)
            slope[p, :] = phi + pre * (jnp.exp(-0.5 * pre * pre) * 0.3989422804014327)
        work[...] = tn(w2p[e], hid_ref[e])
        total = jnp.zeros((1, rows), f32)
        for p in parts:
            total = total + jnp.sum(work[p, :], axis=0, keepdims=True)
        mean = total * (1.0 / O)
        total = jnp.zeros((1, rows), f32)
        for p in parts:
            off = work[p, :] - mean
            total = total + jnp.sum(off * off, axis=0, keepdims=True)
        inverse = lax.rsqrt(total * (1.0 / O) + norm_eps)
        sums = {t: jnp.zeros((1, rows), f32) for t in streams}
        first, second = jnp.zeros((1, rows), f32), jnp.zeros((1, rows), f32)
        for i, p in enumerate(parts):
            normed = (work[p, :] - mean) * inverse
            gain = wide(col_ref[1, e, p, :], rows)
            value = normed * gain + wide(col_ref[2, e, p, :], rows)
            grad = None
            for t in streams:
                rows_t = slice(t * O + i * chunk, t * O + (i + 1) * chunk)
                mix[rows_t, :] += value * coef[t]
                upward = up[rows_t, :]
                sums[t] = sums[t] + jnp.sum(upward * value, axis=0, keepdims=True)
                term = upward * coef[t]
                grad = term if grad is None else grad + term
            d_norm = grad * gain
            first = first + jnp.sum(d_norm, axis=0, keepdims=True)
            second = second + jnp.sum(d_norm * normed, axis=0, keepdims=True)
            norm[p, :] = normed
            work[p, :] = d_norm
            dout[0, p, :] = (grad * normed).astype(bf16)
            dout[1, p, :] = grad.astype(bf16)
        for t in streams:
            d_chances[t][STREAM_EXPERTS[t].index(e)] = sums[t]
        first, second = first * (1.0 / O), second * (1.0 / O)
        for p in parts:
            dinner_ref[e, p, :] = ((work[p, :] - first - norm[p, :] * second) * inverse).astype(bf16)
        work[...] = nn(w2p[e], dinner_ref[e])
        for p in parts:
            dpre_ref[e, p, :] = (work[p, :] * slope[p, :]).astype(bf16)
        w2n[e] = nt(hid_ref[e], dinner_ref[e]).astype(bf16)
        vec[0, e] = nt(ones, dpre_ref[e])
        vec[1, e] = nt(ones, dout[0])
        vec[2, e] = nt(ones, dout[1])
        back = nn(w1p[e], dpre_ref[e])
        if e == 0:
            dx[...] = back
        else:
            dx[...] += back
    d_logits = []
    for t in range(STREAMS):
        upward = jnp.concatenate(d_chances[t], axis=0)
        g = chances[t]
        d_logits.append(g * (upward - jnp.sum(g * upward, axis=0, keepdims=True)))
    pad = jnp.zeros((gate_ref.shape[0] - GATES, rows), f32)
    d_logits = jnp.concatenate(d_logits + [pad], axis=0).astype(bf16)
    dx[...] += tn(gate, d_logits)
    for m in range(hid):
        start = pl.multiple_of((me ^ m) * feats, feats)
        dx_outs[m][...] = dx[pl.ds(start, feats), :].astype(bf16)
    width, whole, packed, rest, small_rows = small_plan(hid)
    d_gate = nt(d_logits, xt[...])[0:GATES]
    lines = [d_gate[:, i * width : (i + 1) * width] for i in range(whole)]
    tail = d_gate[:, whole * width :]
    if rest * packed > GATES:
        tail = jnp.concatenate([tail, jnp.zeros((rest * packed - GATES, HALF), f32)], axis=0)
    tail = jnp.concatenate([tail[i * rest : (i + 1) * rest] for i in range(packed)], axis=1)
    if packed * HALF < width:
        tail = jnp.concatenate([tail, jnp.zeros((rest, width - packed * HALF), f32)], axis=1)
    lines.append(tail)
    for half in range(2):
        lanes = slice(half * HALF, (half + 1) * HALF)
        stack = jnp.concatenate(
            [
                jnp.concatenate([vec[i, e, 0:1, lanes] for e in range(EXPERTS)], axis=1)
                for i in range(3)
            ]
            + [jnp.zeros((5, HALF * EXPERTS), f32)],
            axis=0,
        ).astype(bf16)
        unturned = nt(stack, q_ref[...])
        for i in range((HALF * EXPERTS) // width):
            lines.append(unturned[0:3, i * width : (i + 1) * width])
    spare = small_rows - sum(line.shape[0] for line in lines)
    if spare:
        lines.append(jnp.zeros((spare, width), f32))
    small_ref[...] = jnp.concatenate(lines, axis=0).astype(bf16)
    mixed_ref[...] = tn(mix[...].astype(bf16), q3t_ref[...]).astype(bf16)
    me_dp = lax.axis_index("dp")
    span = HALF * EXPERTS
    first_rows = D // dp
    fold = H // dp
    each = first_rows + fold
    second_cols = (O * EXPERTS) // dp
    high = H // hid
    inner = inner_size(dp)
    outer = dp // inner
    for half in range(2):
        part = slice(half * HALF, (half + 1) * HALF)
        block = jnp.concatenate([dpre_ref[e, part, :] for e in range(EXPERTS)], axis=0)
        turned[half * span : (half + 1) * span, :] = nn(q_ref[...], block).astype(bf16)
        block = jnp.concatenate([w2n[e, :, part] for e in range(EXPERTS)], axis=1)
        w2g[:, half * span : (half + 1) * span] = nt(block, q_ref[...])
    for m in range(hid):
        out, base = (away if m % 2 else home), (m // 2) * dp * each
        j = me ^ m
        left = turned[pl.ds(pl.multiple_of(j * width, width), width), :]
        w1g[...] = nt(xt[...], left).astype(bf16)
        for near in range(inner):
            for far in range(outer):
                k = me_dp ^ (far * inner + near)
                start = pl.multiple_of(k * first_rows, first_rows)
                to = base + (near * outer + far) * each
                out[to : to + first_rows, :] = w1g[pl.ds(start, first_rows), :]
        start = pl.multiple_of(j * high, high)
        for k in range(dp):
            part = w2g[pl.ds(start, high), k * second_cols : (k + 1) * second_cols]
            folded = jnp.concatenate(
                [part[i * fold : (i + 1) * fold, :] for i in range(high // fold)], axis=1
            ).astype(bf16)
            r = me_dp ^ k
            to = base + ((r % inner) * outer + r // inner) * each + first_rows
            out[pl.ds(pl.multiple_of(to, fold), fold), :] = folded
    away[(hid // 2) * dp * each :, :] = small_ref[...]


def table_kernel(owners_ref, *refs, chunks, dp, hid):
    counts, pieces = refs[:chunks], refs[chunks : chunks + hid]
    outs = refs[chunks + hid + 1 : chunks + hid + 1 + dp]
    back, grads, slots, count_ref = refs[chunks + hid + 1 + dp :]
    me_dp, me_hid = lax.axis_index("dp"), lax.axis_index("hid")
    rows = pieces[0].shape[1]
    for m in range(hid):
        start = pl.multiple_of((me_hid ^ m) * rows, rows)
        back[:, pl.ds(start, rows)] = pieces[m][...]
    part = None
    for i in range(chunks):
        p = nn(back[:, i * EVENTS_STEP : (i + 1) * EVENTS_STEP], counts[i][...])
        part = p if part is None else part + p
    grads[...] = part.T.astype(bf16)
    slots[...] = jnp.zeros_like(slots)

    def place(block, owner, rank):
        slots[
            owner ^ me_dp, pl.ds(pl.multiple_of(rank * ROWS_BLOCK, ROWS_BLOCK), ROWS_BLOCK), :
        ] = grads[pl.ds(pl.multiple_of(block * ROWS_BLOCK, ROWS_BLOCK), ROWS_BLOCK), :]

    each_block(owners_ref, count_ref, dp, place)
    for r in range(dp):
        outs[r][...] = slots[r]


def total(refs, *at):
    values = [(ref[at] if at else ref[...]).astype(f32) for ref in refs]
    while len(values) > 1:
        values = [values[i] + values[i + 1] for i in range(0, len(values), 2)]
    return values[0]


def plus(a, b):
    return (a.astype(f32) + b.astype(f32)).astype(bf16)


def core_merge_kernel(home, come, small, *outs, rows, inner):
    last = plus(small[...], come[len(outs) * rows :, :])
    for i, out in enumerate(outs):
        part = slice(i * rows, (i + 1) * rows)
        out[0:rows, :] = plus(home[part, :], come[part, :])
        if i % inner:
            out[rows:, :] = last


def chip_merge_kernel(*refs, terms):
    if len(refs) == terms + 3:
        refs[terms + 2][...] = refs[terms][...]
        refs[terms + 1][...] = total(refs[:terms]).astype(bf16)
    else:
        refs[terms][...] = total(refs[:terms]).astype(bf16)


def near_merge_kernel(mine, other, *refs, terms, rows, outer):
    come, outs = refs[: terms - 1], refs[terms - 1 :]
    last = total((other, *come), slice(outer * rows, None)).astype(bf16)
    for far in range(outer):
        part = slice(far * rows, (far + 1) * rows)
        outs[far][0:rows, :] = total((mine, *come), part).astype(bf16)
        outs[far][rows:, :] = last


def stack_kernel_ordered(*refs, count, start):
    for r in range(count):
        refs[-1][r] = refs[r][start:, :]


def sum_kernel(*refs, terms):
    refs[-1][...] = total(refs[:terms]).astype(bf16)


def join_kernel(*refs, count):
    for i in range(count):
        refs[-1][i] = refs[i][...]


def mixed_kernel(*refs, hid):
    out = refs[hid]
    rows = refs[0].shape[0]
    me = lax.axis_index("hid")
    for m in range(hid):
        out[pl.ds(pl.multiple_of((me ^ m) * rows, rows), rows), :] = refs[m][...]


def adam(weight, moment, second, average, grad, rate):
    new_moment = 0.5 * moment + 0.5 * grad
    new_second = 0.5 * second + 0.5 * grad * grad
    correct = 1.0 - 0.5**STEP
    new_weight = weight - rate * (
        new_moment / correct / (jnp.sqrt(new_second / correct) + adam_eps) + decay_rate * weight
    )
    new_average = ema_decay * average + (1.0 - ema_decay) * new_weight
    return (new_weight, new_moment, new_second, new_average)


def table_adam_kernel(*refs, terms):
    state, parts, outs = refs[:4], refs[4 : 4 + terms], refs[4 + terms :]
    rows = state[0].shape[0]
    chunk = 64
    for i in range(rows // chunk):
        p = slice(i * chunk, (i + 1) * chunk)
        new = adam(*[s[p, :] for s in state], total(parts, p), 0.3)
        for out, value in zip(outs, new):
            out[p, :] = value


def weight_adam_kernel(*refs, terms, dp, hid):
    first, second, vector, gate = refs[0:4], refs[4:8], refs[8:12], refs[12:16]
    parts, outs = refs[16 : 16 + terms], refs[16 + terms :]
    first_out, second_out, vector_out, gate_out = outs[0:4], outs[4:8], outs[8:12], outs[12:16]
    rows, fold = D // dp, H // dp
    width = (O * EXPERTS) // dp
    new = adam(*[s[...] for s in first], total(parts, slice(0, rows)), 0.04)
    for out, value in zip(first_out, new):
        out[...] = value
    grad = total(parts, slice(rows, rows + fold))
    for i in range((H // hid) // fold):
        p = slice(i * fold, (i + 1) * fold)
        new = adam(*[s[p, :] for s in second], grad[:, i * width : (i + 1) * width], 0.06)
        for out, value in zip(second_out, new):
            out[p, :] = value
    small = total(parts, slice(rows + fold, None))
    cols, whole, packed, rest, _ = small_plan(hid)
    tail = small[GATES * whole : GATES * whole + rest]
    tail = jnp.concatenate([tail[:, i * HALF : (i + 1) * HALF] for i in range(packed)], axis=0)
    grad = jnp.concatenate(
        [small[i * GATES : (i + 1) * GATES] for i in range(whole)] + [tail[0:GATES]], axis=1
    )
    new = adam(*[s[...] for s in gate], grad, 0.03)
    for out, value in zip(gate_out, new):
        out[...] = value
    me = lax.axis_index("hid")
    base = GATES * whole + rest
    grad = jnp.zeros((3, cols), f32)
    for j in range(hid):
        grad = jnp.where(me == j, small[base + 3 * j : base + 3 * j + 3], grad)
    new = adam(*[s[...] for s in vector], grad, 0.2)
    for out, value in zip(vector_out, new):
        out[...] = value


def finish_kernel(*refs, table_terms, terms, dp, hid):
    a, b, c = 4 + table_terms, 16 + terms, hid
    ins, outs = refs[: a + b + c], refs[a + b + c :]
    mixed_kernel(*ins[a + b :], outs[0], hid=hid)
    table_adam_kernel(*ins[:a], *outs[1:5], terms=table_terms)
    weight_adam_kernel(*ins[a : a + b], *outs[5:], terms=terms, dp=dp, hid=hid)


def per_device(
    bag_offsets,
    embed_ids,
    block_owners,
    cotangent,
    table_w,
    table_m,
    table_v,
    table_ema,
    first_w,
    first_m,
    first_v,
    first_ema,
    second_w,
    second_m,
    second_v,
    second_ema,
    vector_w,
    vector_m,
    vector_v,
    vector_ema,
    gate_w,
    gate_m,
    gate_v,
    gate_ema,
):
    dp, hid = lax.axis_size("dp"), lax.axis_size("hid")
    inner = inner_size(dp)
    outer = dp // inner
    events, ids = bag_offsets.shape[0], embed_ids.shape[0]
    rows = events // hid
    slots, feats = table_w.shape
    vocab = block_owners.shape[0] * ROWS_BLOCK
    piece_rows = D // dp + H // dp
    piece_cols = first_w.shape[1]

    cot_rows = cotangent.shape[1] + 32
    weight_rows = 3 * piece_rows
    piece, keep, *cot_pieces = call(
        functools.partial(low_kernel, hid=hid),
        [
            shape((slots + weight_rows, feats), bf16),
            shape((slots + weight_rows, feats), bf16),
            *[shape((cot_rows, rows), bf16) for m in range(hid)],
        ],
        (table_w, first_w, second_w, vector_w, cotangent.T),
        in_specs=[HBM] * 5,
        scratch=[
            pltpu.VMEM(table_w.shape, f32),
            pltpu.VMEM(first_w.shape, f32),
            pltpu.VMEM(second_w.shape, f32),
            pltpu.VMEM(vector_w.shape, f32),
            pltpu.VMEM(cotangent.shape[::-1], bf16),
            pltpu.SemaphoreType.DMA((5,)),
        ],
        vmem=62,
    )
    cots = [cot_pieces[0]] + [swap(cot_pieces[m], "hid", m) for m in range(1, hid)]
    nexts = jnp.concatenate([bag_offsets[1:], jnp.full((1,), ids, jnp.int32)])
    lanes = 128
    chunks = events // EVENTS_STEP

    def count_bags(i, *order):
        return call(
            functools.partial(counts_kernel, chunk=i),
            shape((EVENTS_STEP, vocab), bf16),
            (
                bag_offsets,
                embed_ids.reshape(ids // lanes, lanes),
                bag_offsets.reshape(events // lanes, lanes),
                nexts.reshape(events // lanes, lanes),
                *order,
            ),
            in_specs=[SMEM, VMEM, VMEM, VMEM] + [ANY] * len(order),
            scratch=[
                pltpu.VMEM((ids // IDS_STEP, IDS_STEP, HALF), jnp.int16),
                pltpu.VMEM((EVENTS_STEP, vocab), f32),
            ],
            vmem=12 if vocab <= 4096 else 40,
            us=5.0,
        )

    far_pieces = {0: piece}
    step = outer // 2
    while step:
        far_pieces.update({f ^ step: swap(p, "dp", step * inner) for f, p in far_pieces.items()})
        step //= 2
    far_pieces = [far_pieces[f] for f in range(outer)]
    groups = [[keep] + far_pieces[1:]] + [[swap(p, "dp", near) for p in far_pieces] for near in range(1, inner)]

    def stack(group, *order):
        return call(
            functools.partial(stack_kernel_ordered, count=outer, start=slots),
            shape((outer, weight_rows, feats), bf16),
            (*group, *order),
            in_specs=[VMEM] * outer + [ANY] * len(order),
            vmem=8,
            us=0.7,
        )

    stacks = {(0, near): stack(groups[near]) for near in range(inner)}
    span = HALF * EXPERTS
    columns, turn, turn3t = call(
        functools.partial(turns_kernel, hid=hid),
        [
            shape((3, EXPERTS, H, HALF), f32),
            shape((span, span), bf16),
            shape((O * STREAMS, O * STREAMS), bf16),
        ],
        tuple(cots),
        scratch=[pltpu.VMEM((hid, 16, piece_cols), bf16)],
        vmem=12,
        us=2.0,
    )
    early = chunks // 2
    counts = [count_bags(i) for i in range(early)]
    counts += [count_bags(i, far_pieces[outer // 2], turn3t) for i in range(early, chunks - 1)]
    counts.append(count_bags(chunks - 1, stacks[0, 0]))
    pieces = [groups[r % inner][r // inner] for r in range(dp)]
    pooled = call(
        functools.partial(pool_kernel, chunks=chunks, dp=dp, hid=hid),
        [shape((feats, rows), bf16) for m in range(hid)],
        (block_owners, *counts, *pieces),
        in_specs=[SMEM] + [VMEM] * (chunks + dp),
        scratch=[
            pltpu.VMEM((dp, slots, feats), bf16),
            pltpu.VMEM((vocab, feats), bf16),
            pltpu.VMEM((hid, rows, feats), f32),
            pltpu.SMEM((dp,), jnp.int32),
        ],
        vmem=20 if vocab <= 4096 else 58,
        us=4.0,
    )
    xts = [pooled[0]] + [swap(pooled[m], "hid", m) for m in range(1, hid)]
    for near in range(inner):
        for m in range(2, hid, 2):
            stacks[m, near] = swap(stacks[0, near], "hid", m)
    joined = {}
    for m in range(0, hid, 2):
        joined[m] = call(
            functools.partial(join_kernel, count=inner),
            shape((inner, outer, weight_rows, feats), bf16),
            (*[stacks[m, near] for near in range(inner)], xts[1]),
            in_specs=[VMEM] * inner + [ANY],
            vmem=8,
            us=0.7,
        )
        joined[m + 1] = swap(joined[m], "hid", 1)
    w1p, w2p = call(
        functools.partial(weights_kernel, dp=dp, hid=hid),
        [shape((EXPERTS, D, H), bf16), shape((EXPERTS, H, O), bf16)],
        (*[joined[m] for m in range(hid)], turn),
        scratch=[
            pltpu.VMEM((hid, D, piece_cols), bf16),
            pltpu.VMEM((dp, H, (O * EXPERTS) // dp), bf16),
        ],
        vmem=20,
        us=3.0,
    )

    gates = 16
    gate_pad = jnp.pad(gate_w.T, ((0, gates - gate_w.shape[1]), (0, 0)))
    small_rows = small_plan(hid)[-1]
    some = dp * piece_rows
    mixed_part, small, home, away, *d_pieces = call(
        functools.partial(main_kernel, dp=dp, hid=hid),
        [
            shape((rows, O * STREAMS), bf16),
            shape((small_rows, piece_cols), bf16),
            shape((hid // 2 * some, piece_cols), bf16),
            shape((hid // 2 * some + small_rows, piece_cols), bf16),
            *[shape((feats, rows), bf16) for m in range(hid)],
        ],
        (*xts, *cots, w1p, w2p, columns, turn, turn3t, gate_pad),
        scratch=[
            pltpu.VMEM((D, rows), bf16),
            pltpu.VMEM((EXPERTS, H, rows), bf16),
            pltpu.VMEM((EXPERTS, O, rows), bf16),
            pltpu.VMEM((EXPERTS, H, rows), bf16),
            pltpu.VMEM((O * STREAMS, rows), f32),
            pltpu.VMEM((O * STREAMS, rows), bf16),
            pltpu.VMEM((O * STREAMS, rows), f32),
            pltpu.VMEM((H, rows), f32),
            pltpu.VMEM((H, rows), f32),
            pltpu.VMEM((H, rows), f32),
            pltpu.VMEM((2, H, rows), bf16),
            pltpu.VMEM((D, rows), f32),
            pltpu.VMEM((3, EXPERTS, 8, H), f32),
            pltpu.VMEM((H * EXPERTS, rows), bf16),
            pltpu.VMEM((D, piece_cols), bf16),
            pltpu.VMEM((EXPERTS, H, O), bf16),
            pltpu.VMEM((H, O * EXPERTS), f32),
        ],
        vmem=36,
        us=10.0,
    )
    d_pooled = [d_pieces[0]] + [swap(d_pieces[m], "hid", m) for m in range(1, hid)]

    near_rows = some // inner
    half = call(
        functools.partial(core_merge_kernel, rows=near_rows, inner=inner),
        [
            shape((near_rows + small_rows * (near > 0), piece_cols), bf16)
            for m in range(hid // 2)
            for near in range(inner)
        ],
        (home, swap(away, "hid", 1), small),
        vmem=12,
        us=1.0,
    )
    sums = [None] * inner
    for i in reversed(range(inner)):
        passing = () if i else (mixed_part,)
        result = call(
            functools.partial(chip_merge_kernel, terms=hid // 2),
            [shape(v.shape, bf16) for v in (half[i], *passing)],
            (half[i], *[swap(half[m * inner + i], "hid", 2 * m) for m in range(1, hid // 2)])
            + passing,
            vmem=12,
            us=0.7,
        )
        sums[i] = result[0]
    mixed_part = result[1]
    far_parts = call(
        functools.partial(near_merge_kernel, terms=inner, rows=piece_rows, outer=outer),
        [shape((piece_rows + small_rows, piece_cols), bf16)] * outer,
        (sums[0], sums[1], *[swap(sums[i], "dp", i) for i in range(1, inner)]),
        vmem=12,
        us=1.0,
    )
    weight_terms = [far_parts[0]] + [swap(far_parts[m], "dp", m * inner) for m in range(1, outer)]

    mixed_parts = {0: mixed_part}
    for m in range(2, hid, 2):
        mixed_parts[m] = swap(mixed_part, "hid", m)
    for m in range(0, hid, 2):
        mixed_parts[m + 1] = swap(mixed_parts[m], "hid", 1)
    d_table = call(
        functools.partial(table_kernel, chunks=chunks, dp=dp, hid=hid),
        [shape((slots, feats), bf16) for r in range(dp)],
        (block_owners, *counts, *d_pooled, half[0]),
        in_specs=[SMEM] + [VMEM] * (chunks + hid) + [ANY],
        scratch=[
            pltpu.VMEM((feats, events), bf16),
            pltpu.VMEM((vocab, feats), bf16),
            pltpu.VMEM((dp, slots, feats), bf16),
            pltpu.SMEM((dp,), jnp.int32),
        ],
        vmem=20 if vocab <= 4096 else 58,
        us=6.0,
    )
    order = sums[1]
    sums = {}
    for far in reversed(range(outer)):
        terms = [d_table[far * inner]]
        terms += [swap(d_table[far * inner + m], "dp", m) for m in range(1, inner)]
        if far == outer - 1:
            sums[far] = call(
                functools.partial(sum_kernel, terms=inner),
                shape((slots, feats), bf16),
                (*terms, order),
                in_specs=[VMEM] * inner + [ANY],
                vmem=4,
                us=0.5,
            )
        else:
            sums[far] = functools.reduce(plus, terms)
    step = 1
    while step < outer // 2:
        for far in reversed([f for f in sums if f & step]):
            sums[far ^ step] = plus(sums[far ^ step], swap(sums.pop(far), "dp", step * inner))
        step *= 2
    table_terms = [sums[0], swap(sums[step], "dp", step * inner)]

    states = (
        table_w,
        table_m,
        table_v,
        table_ema,
        first_w,
        first_m,
        first_v,
        first_ema,
        second_w,
        second_m,
        second_v,
        second_ema,
        vector_w,
        vector_m,
        vector_v,
        vector_ema,
        *[g.T for g in (gate_w, gate_m, gate_v, gate_ema)],
    )
    mixed, *new = call(
        functools.partial(
            finish_kernel, table_terms=len(table_terms), terms=outer, dp=dp, hid=hid
        ),
        [shape((events, O * STREAMS), bf16)] + [shape(v.shape, f32) for v in states],
        (*states[:4], *table_terms, *states[4:], *weight_terms)
        + tuple(mixed_parts[m] for m in range(hid)),
        vmem=20,
        us=3.0,
    )
    return (mixed, *new[:16], *[g.T for g in new[16:]])


def solution(mesh):
    split, spread, whole = P("dp", "hid"), P("hid", "dp"), P()
    return jax.shard_map(
        per_device,
        mesh=mesh,
        in_specs=(P("dp"), P("dp"), whole, split)
        + (split,) * 8
        + (spread,) * 4
        + (P(None, "hid"),) * 4
        + (whole,) * 4,
        out_specs=(P("dp", None),)
        + (split,) * 8
        + (spread,) * 4
        + (P(None, "hid"),) * 4
        + (whole,) * 4,
        check_vma=False,
    )
```

```python
import functools

import jax
import jax.numpy as jnp
from jax import lax
from jax.experimental import pallas as pl
from jax.experimental.pallas import tpu as pltpu
from jax.sharding import PartitionSpec as P

D = 512
H = 256
O = 256
EXPERTS = 6
STREAMS = 3
ROWS_BLOCK = 64
STEP = 5
CAP = 12
GATES = 14
HALF = 128
IDS_STEP = 256
EVENTS_STEP = 256

norm_eps = 1e-05
adam_eps = 1e-08
decay_rate = 0.01
ema_decay = 0.9

bf16 = jnp.bfloat16
f32 = jnp.float32
MIB = 1 << 20

STREAM_EXPERTS = ((0, 1, 4, 5), (2, 3, 4, 5), (0, 1, 2, 3, 4, 5))
STREAM_COLS = (0, 4, 8)

COST = {'low': 1.605, 'cut': 0.491, 'turns': 6.876, 'counts': 2.06, 'pool': 4.0, 'stack': 0.045, 'join': 0.7, 'weights': 0.778, 'main': 10.0, 'table': 6.0, 'half': 0.7, 'chip': 0.7, 'near': 1.0, 'sum': 0.5, 'finish': 3.0}
OPT = {'a': 1, 'b': 0, 'c': 0, 'd': 1, 'e': 0, 'f': 1, 'h': 0, 'i': 0, 'j': 1, 'k': 0, 'm': 3, 'n': 1, 'q': 1, 'g': 2, 'p': 0, 'r': 0}
RNG = {'a': 4, 'b': 3, 'c': 3, 'd': 2, 'e': 3, 'f': 2, 'h': 2, 'i': 3, 'j': 2, 'k': 2, 'm': 4, 'n': 2, 'q': 2, 'g': 3, 'p': 2, 'r': 2}

VMEM = pl.BlockSpec(memory_space=pltpu.VMEM)
SMEM = pl.BlockSpec(memory_space=pltpu.SMEM)
HBM = pl.BlockSpec(memory_space=pltpu.HBM)
ANY = pl.BlockSpec(memory_space=pl.ANY)


def shape(dims, dtype):
    return jax.ShapeDtypeStruct(tuple(dims), dtype)


def nn(a, b):
    return lax.dot_general(a, b, (((1,), (0,)), ((), ())), preferred_element_type=f32)


def nt(a, b):
    return lax.dot_general(a, b, (((1,), (1,)), ((), ())), preferred_element_type=f32)


def tn(a, b):
    return lax.dot_general(a, b, (((0,), (0,)), ((), ())), preferred_element_type=f32)


def call(kernel, out_shape, args, in_specs=None, scratch=(), vmem=24, us=2.0):
    single = not isinstance(out_shape, (list, tuple))
    outs = [out_shape] if single else list(out_shape)
    result = pl.pallas_call(
        kernel,
        out_shape=outs,
        in_specs=in_specs or [VMEM] * len(args),
        out_specs=[VMEM] * len(outs),
        scratch_shapes=list(scratch),
        compiler_params=pltpu.CompilerParams(vmem_limit_bytes=vmem * MIB),
        name=getattr(kernel, "func", kernel).__name__,
        cost_estimate=pl.CostEstimate(
            flops=int(us * 1.0e9), bytes_accessed=int(us * 3.0e6), transcendentals=0
        ),
    )(*args)
    return result[0] if single else result


def swap(value, axis, mask):
    count = lax.axis_size(axis)
    return lax.ppermute(value, axis, [(i, i ^ mask) for i in range(count)])


def inner_size(dp_count):
    return 1 << ((dp_count.bit_length() - 1) // 2)


def low_kernel(table_hbm, first_hbm, second_hbm, piece, keep, table, first, second, sems):
    copies = [
        pltpu.make_async_copy(source, target, sems.at[i])
        for i, (source, target) in enumerate(
            ((table_hbm, table), (first_hbm, first), (second_hbm, second))
        )
    ]
    for copy in copies:
        copy.start()
    copies[0].wait()
    slots, feats = table.shape
    for out in (piece, keep):
        out[0:slots, :] = table[...].astype(bf16)
    copies[1].wait()
    copies[2].wait()
    rows = first.shape[0]
    each = (piece.shape[0] - slots) // 3
    fold = each - rows
    folded = jnp.concatenate(
        [second[i * fold : (i + 1) * fold, :] for i in range(second.shape[0] // fold)], axis=1
    )
    for g in range(3):
        lanes = slice(g * feats, (g + 1) * feats)
        start = slots + g * each
        for out in (piece, keep):
            out[start : start + rows, :] = first[:, lanes].astype(bf16)
            out[start + rows : start + each, :] = folded[:, lanes].astype(bf16)


def cut_kernel(vector, cot, ids_ref, order_ref, idb, *cots):
    id_rows, lanes = ids_ref.shape
    per = IDS_STEP // lanes
    idt = ids_ref[...].T
    for q in range(id_rows):
        idb[q // per, (q % per) * lanes : (q % per + 1) * lanes, :] = jnp.broadcast_to(
            idt[:, q : q + 1], (lanes, HALF)
        ).astype(jnp.int16)
    me = lax.axis_index("hid")
    cols, width = cot.shape[0], cots[0].shape[1]
    rest = vector[...]
    terms = []
    for i in range(3):
        terms.append(rest.astype(bf16).astype(f32))
        rest = rest - terms[i]
    span = vector.shape[1]
    stack = jnp.concatenate(terms + [jnp.zeros((7, span), f32)], axis=0)
    over = jnp.concatenate([stack[:, width:], jnp.zeros((16, 2 * width - span), f32)], axis=1)
    for m, out in enumerate(cots):
        start = pl.multiple_of((me ^ m) * width, width)
        out[0:cols, :] = cot[:, pl.ds(start, width)]
        out[cols : cols + 16, :] = stack[:, 0:width].astype(bf16)
        out[cols + 16 :, :] = over.astype(bf16)


def counts_kernel(offs_ref, idb, off_ref, nxt_ref, *refs, chunk):
    c_ref, acc = refs[-2:]
    vocab = c_ref.shape[1]
    lanes = off_ref.shape[1]
    events = off_ref.shape[0] * lanes
    offt = off_ref[...].T
    nxtt = nxt_ref[...].T
    cols = EVENTS_STEP // lanes
    width = 512
    lane = lax.broadcasted_iota(jnp.int32, (IDS_STEP, HALF), 1).astype(jnp.int16)
    one, zero = jnp.ones((IDS_STEP, HALF), bf16), jnp.zeros((IDS_STEP, HALF), bf16)
    first = jnp.concatenate([offt[:, chunk * cols + i : chunk * cols + i + 1] for i in range(cols)], 0)
    last = jnp.concatenate([nxtt[:, chunk * cols + i : chunk * cols + i + 1] for i in range(cols)], 0)
    acc[...] = jnp.zeros_like(acc)
    low = offs_ref[chunk * EVENTS_STEP]
    if (chunk + 1) * EVENTS_STEP < events:
        high = offs_ref[(chunk + 1) * EVENTS_STEP]
    else:
        high = jnp.int32(idb.shape[0] * IDS_STEP)

    def body(step, carry):
        place = step * IDS_STEP + lax.broadcasted_iota(jnp.int32, (EVENTS_STEP, IDS_STEP), 1)
        member = jnp.where((place >= first) & (place < last), 1.0, 0.0).astype(bf16)
        ids = idb[step]
        for v in range(vocab // width):
            hot = jnp.concatenate(
                [
                    jnp.where(ids == lane + jnp.int16(v * width + i * HALF), one, zero)
                    for i in range(width // HALF)
                ],
                axis=1,
            )
            acc[:, v * width : (v + 1) * width] += nn(member, hot)
        return carry

    lax.fori_loop(low // IDS_STEP, (high + IDS_STEP - 1) // IDS_STEP, body, 0)
    c_ref[...] = acc[...].astype(bf16)


def each_block(owners_ref, count_ref, owners, body):
    for o in range(owners):
        count_ref[o] = 0

    def step(block, carry):
        owner = owners_ref[block]
        rank = count_ref[owner]
        count_ref[owner] = rank + 1
        body(block, owner, rank)
        return carry

    lax.fori_loop(0, owners_ref.shape[0], step, 0)


def pool_kernel(owners_ref, *refs, chunks, dp, hid):
    counts, pieces = refs[:chunks], refs[chunks : chunks + dp]
    outs = refs[chunks + dp : chunks + dp + hid]
    whole, table, pooled, count_ref = refs[chunks + dp + hid :]
    me_dp, me_hid = lax.axis_index("dp"), lax.axis_index("hid")
    slots = whole.shape[1]
    for r in range(dp):
        whole[me_dp ^ r] = pieces[r][0:slots, :]

    def place(block, owner, rank):
        table[pl.ds(pl.multiple_of(block * ROWS_BLOCK, ROWS_BLOCK), ROWS_BLOCK), :] = whole[
            owner, pl.ds(pl.multiple_of(rank * ROWS_BLOCK, ROWS_BLOCK), ROWS_BLOCK), :
        ]

    each_block(owners_ref, count_ref, dp, place)
    rows = pooled.shape[1]
    per = EVENTS_STEP // rows
    for q in range(hid):
        part = slice((q % per) * rows, (q % per + 1) * rows)
        pooled[q] = nn(counts[q // per][part, :], table[...])
    for m in range(hid):
        outs[m][...] = pooled[me_hid ^ m].T.astype(bf16)


def hot_cv(rows, cols, mult, start):
    group = cols // mult
    col = lax.broadcasted_iota(jnp.int32, (8, cols), 1)
    target = ((col % group) * mult + col // group - start)[0:1]
    row = lax.broadcasted_iota(jnp.int32, (rows, cols), 0)
    return jnp.where(row == target, 1.0, 0.0).astype(bf16)


def hot_vc(rows, cols, mult, start):
    group = rows // mult
    row = lax.broadcasted_iota(jnp.int32, (rows, HALF), 0)
    target = ((row % group) * mult + row // group - start)[:, 0:1]
    col = lax.broadcasted_iota(jnp.int32, (rows, cols), 1)
    return jnp.where(col == target, 1.0, 0.0).astype(bf16)


def turns_kernel(*refs, hid):
    cots = refs[:hid]
    col_ref, q_ref, q3t_ref, vecs = refs[-4:]
    me_hid = lax.axis_index("hid")
    j_step = vecs.shape[2]
    for r in range(hid):
        cols, near = cots[r].shape[0] - 32, cots[r].shape[1]
        vecs[me_hid ^ r] = jnp.concatenate(
            [cots[r][cols : cols + 16, :], cots[r][cols + 16 : cols + 32, 0 : j_step - near]], axis=1
        )
    span = HALF * EXPERTS
    q_ref[...] = hot_cv(span, span, EXPERTS, 0)
    q3t_ref[...] = hot_vc(O * STREAMS, O * STREAMS, STREAMS, 0)
    for half in range(2):
        lanes = slice(half * HALF, (half + 1) * HALF)
        value = None
        for i in range(span // j_step):
            c = nt(hot_vc(span, j_step, EXPERTS, i * j_step), vecs[half * (span // j_step) + i])
            value = c if value is None else value + c
        cols = value[:, 0:3] + value[:, 3:6] + value[:, 6:9]
        for e in range(EXPERTS):
            for i in range(3):
                col_ref[i, e, lanes, :] = jnp.broadcast_to(
                    cols[e * HALF : (e + 1) * HALF, i : i + 1], (HALF, HALF)
                )


def weights_kernel(*refs, dp, hid):
    inner = inner_size(dp)
    given = hid
    stacks, q_ref = refs[:given], refs[given]
    w1p, w2p = refs[given + 1 : given + 3]
    w1s, w2s = refs[given + 3 :]
    me_dp, me_hid = lax.axis_index("dp"), lax.axis_index("hid")
    rows = D // dp
    fold = H // dp
    each = rows + fold
    width = (O * EXPERTS) // dp
    high = H // hid
    feats = stacks[0].shape[-1]
    j_step = w1s.shape[2]
    k_step = w2s.shape[2]
    for r in range(hid):
        j = me_hid ^ r
        for s in range(dp):
            k = me_dp ^ s
            for g in range(3):
                w1s[j, pl.ds(pl.multiple_of(k * rows, rows), rows), g * feats : (g + 1) * feats] = (
                    stacks[r][s, g * each : g * each + rows, :]
                )
            part = jnp.concatenate(
                [stacks[r][s, g * each + rows : (g + 1) * each, :].astype(f32) for g in range(3)],
                axis=1,
            )
            for q in range(high // fold):
                start = pl.multiple_of(j * high + q * fold, fold)
                w2s[k, pl.ds(start, fold), :] = part[:, q * width : (q + 1) * width].astype(bf16)
    span = HALF * EXPERTS
    for half in range(2):
        lanes = slice(half * HALF, (half + 1) * HALF)
        for step, source, out in ((j_step, w1s, w1p), (k_step, w2s, w2p)):
            value = None
            for i in range(span // step):
                p = nn(source[half * (span // step) + i], q_ref[i * step : (i + 1) * step, :])
                value = p if value is None else value + p
            for e in range(EXPERTS):
                out[e, :, lanes] = value[:, e * HALF : (e + 1) * HALF].astype(bf16)


def small_plan(hid):
    width = (H * EXPERTS) // hid
    whole = D // width
    packed = width // HALF
    rest = -(-GATES // packed)
    used = GATES * whole + rest + 3 * hid
    return width, whole, packed, rest, -(-used // 16) * 16


def softmax_rows(logits):
    top = jnp.max(logits, axis=0, keepdims=True)
    grown = jnp.exp(logits - top)
    return grown / jnp.sum(grown, axis=0, keepdims=True)


def wide(column, width):
    return jnp.concatenate([column] * (width // HALF), axis=1) if width > HALF else column


def main_kernel(*refs, dp, hid):
    xts, cots = refs[:hid], refs[hid : 2 * hid]
    w1p, w2p, col_ref, q_ref, q3t_ref, gate_ref = refs[2 * hid : 2 * hid + 6]
    outs = refs[2 * hid + 6 :]
    mixed_ref, small_ref, home, away = outs[:4]
    dx_outs = outs[4 : 4 + hid]
    xt, hid_ref, dinner_ref, dpre_ref, up, upq, mix, work, slope, norm, dout, dx, vec = outs[
        4 + hid : 17 + hid
    ]
    turned, w1g, w2n, w2g = outs[17 + hid :]
    me = lax.axis_index("hid")
    feats, rows = xts[0].shape
    for m in range(hid):
        j = me ^ m
        xt[pl.ds(pl.multiple_of(j * feats, feats), feats), :] = xts[m][...]
        cols = cots[m].shape[0] - 32
        upq[pl.ds(pl.multiple_of(j * cols, cols), cols), :] = cots[m][0:cols, :]
    up[...] = nn(q3t_ref[...], upq[...])
    gate = gate_ref[...].astype(bf16)
    logits = nn(gate, xt[...])
    chances = [
        softmax_rows(logits[STREAM_COLS[t] : STREAM_COLS[t] + len(STREAM_EXPERTS[t])])
        for t in range(STREAMS)
    ]
    mix[...] = jnp.zeros_like(mix)
    chunk = 64
    parts = [slice(i * chunk, (i + 1) * chunk) for i in range(O // chunk)]
    ones = jnp.ones((8, rows), bf16)
    d_chances = [[None] * len(STREAM_EXPERTS[t]) for t in range(STREAMS)]
    for e in range(EXPERTS):
        streams = [t for t in range(STREAMS) if e in STREAM_EXPERTS[t]]
        coef = {
            t: chances[t][STREAM_EXPERTS[t].index(e) : STREAM_EXPERTS[t].index(e) + 1]
            for t in streams
        }
        work[...] = tn(w1p[e], xt[...])
        for p in parts:
            pre = work[p, :] + wide(col_ref[0, e, p, :], rows)
            phi = 0.5 + 0.5 * lax.erf(pre * 0.7071067811865476)
            hid_ref[e, p, :] = (pre * phi).astype(bf16)
            slope[p, :] = phi + pre * (jnp.exp(-0.5 * pre * pre) * 0.3989422804014327)
        work[...] = tn(w2p[e], hid_ref[e])
        total = jnp.zeros((1, rows), f32)
        for p in parts:
            total = total + jnp.sum(work[p, :], axis=0, keepdims=True)
        mean = total * (1.0 / O)
        total = jnp.zeros((1, rows), f32)
        for p in parts:
            off = work[p, :] - mean
            total = total + jnp.sum(off * off, axis=0, keepdims=True)
        inverse = lax.rsqrt(total * (1.0 / O) + norm_eps)
        sums = {t: jnp.zeros((1, rows), f32) for t in streams}
        first, second = jnp.zeros((1, rows), f32), jnp.zeros((1, rows), f32)
        for i, p in enumerate(parts):
            normed = (work[p, :] - mean) * inverse
            gain = wide(col_ref[1, e, p, :], rows)
            value = normed * gain + wide(col_ref[2, e, p, :], rows)
            grad = None
            for t in streams:
                rows_t = slice(t * O + i * chunk, t * O + (i + 1) * chunk)
                mix[rows_t, :] += value * coef[t]
                upward = up[rows_t, :]
                sums[t] = sums[t] + jnp.sum(upward * value, axis=0, keepdims=True)
                term = upward * coef[t]
                grad = term if grad is None else grad + term
            d_norm = grad * gain
            first = first + jnp.sum(d_norm, axis=0, keepdims=True)
            second = second + jnp.sum(d_norm * normed, axis=0, keepdims=True)
            norm[p, :] = normed
            work[p, :] = d_norm
            dout[0, p, :] = (grad * normed).astype(bf16)
            dout[1, p, :] = grad.astype(bf16)
        for t in streams:
            d_chances[t][STREAM_EXPERTS[t].index(e)] = sums[t]
        first, second = first * (1.0 / O), second * (1.0 / O)
        for p in parts:
            dinner_ref[e, p, :] = ((work[p, :] - first - norm[p, :] * second) * inverse).astype(bf16)
        work[...] = nn(w2p[e], dinner_ref[e])
        for p in parts:
            dpre_ref[e, p, :] = (work[p, :] * slope[p, :]).astype(bf16)
        w2n[e] = nt(hid_ref[e], dinner_ref[e]).astype(bf16)
        vec[0, e] = nt(ones, dpre_ref[e])
        vec[1, e] = nt(ones, dout[0])
        vec[2, e] = nt(ones, dout[1])
        back = nn(w1p[e], dpre_ref[e])
        if e == 0:
            dx[...] = back
        else:
            dx[...] += back
    d_logits = []
    for t in range(STREAMS):
        upward = jnp.concatenate(d_chances[t], axis=0)
        g = chances[t]
        d_logits.append(g * (upward - jnp.sum(g * upward, axis=0, keepdims=True)))
    pad = jnp.zeros((gate_ref.shape[0] - GATES, rows), f32)
    d_logits = jnp.concatenate(d_logits + [pad], axis=0).astype(bf16)
    dx[...] += tn(gate, d_logits)
    for m in range(hid):
        start = pl.multiple_of((me ^ m) * feats, feats)
        dx_outs[m][...] = dx[pl.ds(start, feats), :].astype(bf16)
    width, whole, packed, rest, small_rows = small_plan(hid)
    d_gate = nt(d_logits, xt[...])[0:GATES]
    lines = [d_gate[:, i * width : (i + 1) * width] for i in range(whole)]
    tail = d_gate[:, whole * width :]
    if rest * packed > GATES:
        tail = jnp.concatenate([tail, jnp.zeros((rest * packed - GATES, HALF), f32)], axis=0)
    tail = jnp.concatenate([tail[i * rest : (i + 1) * rest] for i in range(packed)], axis=1)
    if packed * HALF < width:
        tail = jnp.concatenate([tail, jnp.zeros((rest, width - packed * HALF), f32)], axis=1)
    lines.append(tail)
    for half in range(2):
        lanes = slice(half * HALF, (half + 1) * HALF)
        stack = jnp.concatenate(
            [
                jnp.concatenate([vec[i, e, 0:1, lanes] for e in range(EXPERTS)], axis=1)
                for i in range(3)
            ]
            + [jnp.zeros((5, HALF * EXPERTS), f32)],
            axis=0,
        ).astype(bf16)
        unturned = nt(stack, q_ref[...])
        for i in range((HALF * EXPERTS) // width):
            lines.append(unturned[0:3, i * width : (i + 1) * width])
    spare = small_rows - sum(line.shape[0] for line in lines)
    if spare:
        lines.append(jnp.zeros((spare, width), f32))
    small_ref[...] = jnp.concatenate(lines, axis=0).astype(bf16)
    mixed_ref[...] = tn(mix[...].astype(bf16), q3t_ref[...]).astype(bf16)
    me_dp = lax.axis_index("dp")
    span = HALF * EXPERTS
    first_rows = D // dp
    fold = H // dp
    each = first_rows + fold
    second_cols = (O * EXPERTS) // dp
    high = H // hid
    inner = inner_size(dp)
    outer = dp // inner
    for half in range(2):
        part = slice(half * HALF, (half + 1) * HALF)
        block = jnp.concatenate([dpre_ref[e, part, :] for e in range(EXPERTS)], axis=0)
        turned[half * span : (half + 1) * span, :] = nn(q_ref[...], block).astype(bf16)
        block = jnp.concatenate([w2n[e, :, part] for e in range(EXPERTS)], axis=1)
        w2g[:, half * span : (half + 1) * span] = nt(block, q_ref[...])
    for m in range(hid):
        out, base = (away if m % 2 else home), (m // 2) * dp * each
        j = me ^ m
        left = turned[pl.ds(pl.multiple_of(j * width, width), width), :]
        w1g[...] = nt(xt[...], left).astype(bf16)
        for near in range(inner):
            for far in range(outer):
                k = me_dp ^ (far * inner + near)
                start = pl.multiple_of(k * first_rows, first_rows)
                to = base + (near * outer + far) * each
                out[to : to + first_rows, :] = w1g[pl.ds(start, first_rows), :]
        start = pl.multiple_of(j * high, high)
        for k in range(dp):
            part = w2g[pl.ds(start, high), k * second_cols : (k + 1) * second_cols]
            folded = jnp.concatenate(
                [part[i * fold : (i + 1) * fold, :] for i in range(high // fold)], axis=1
            ).astype(bf16)
            r = me_dp ^ k
            to = base + ((r % inner) * outer + r // inner) * each + first_rows
            out[pl.ds(pl.multiple_of(to, fold), fold), :] = folded
    away[(hid // 2) * dp * each :, :] = small_ref[...]


def table_kernel(owners_ref, *refs, chunks, dp, hid):
    counts, pieces = refs[:chunks], refs[chunks : chunks + hid]
    outs = refs[chunks + hid + 1 : chunks + hid + 1 + dp]
    back, grads, slots, count_ref = refs[chunks + hid + 1 + dp :]
    me_dp, me_hid = lax.axis_index("dp"), lax.axis_index("hid")
    rows = pieces[0].shape[1]
    for m in range(hid):
        start = pl.multiple_of((me_hid ^ m) * rows, rows)
        back[:, pl.ds(start, rows)] = pieces[m][...]
    part = None
    for i in range(chunks):
        p = nn(back[:, i * EVENTS_STEP : (i + 1) * EVENTS_STEP], counts[i][...])
        part = p if part is None else part + p
    grads[...] = part.T.astype(bf16)
    slots[...] = jnp.zeros_like(slots)

    def place(block, owner, rank):
        slots[
            owner ^ me_dp, pl.ds(pl.multiple_of(rank * ROWS_BLOCK, ROWS_BLOCK), ROWS_BLOCK), :
        ] = grads[pl.ds(pl.multiple_of(block * ROWS_BLOCK, ROWS_BLOCK), ROWS_BLOCK), :]

    each_block(owners_ref, count_ref, dp, place)
    for r in range(dp):
        outs[r][...] = slots[r]


def total(refs, *at):
    values = [(ref[at] if at else ref[...]).astype(f32) for ref in refs]
    while len(values) > 1:
        values = [values[i] + values[i + 1] for i in range(0, len(values), 2)]
    return values[0]


def plus(a, b):
    return (a.astype(f32) + b.astype(f32)).astype(bf16)


def core_merge_kernel(home, come, small, *refs, rows, inner, nears):
    chips = home.shape[0] // rows // inner
    outs = refs[-chips * len(nears) :]
    last = plus(small[...], come[home.shape[0] :, :])
    for m in range(chips):
        for i, near in enumerate(nears):
            out = outs[m * len(nears) + i]
            part = slice((m * inner + near) * rows, (m * inner + near + 1) * rows)
            out[0:rows, :] = plus(home[part, :], come[part, :])
            if near:
                out[rows:, :] = last


def chip_merge_kernel(*refs, terms, passing):
    outs = refs[-1 - passing :]
    outs[0][...] = total(refs[:terms]).astype(bf16)
    if passing:
        outs[1][...] = refs[terms][...]


def near_merge_kernel(mine, other, *refs, terms, rows, outer, passing):
    come, outs = refs[: terms - 1], refs[terms - 1 + passing :]
    last = total((other, *come), slice(outer * rows, None)).astype(bf16)
    for far in range(outer):
        part = slice(far * rows, (far + 1) * rows)
        outs[far][0:rows, :] = total((mine, *come), part).astype(bf16)
        outs[far][rows:, :] = last
    if passing:
        outs[outer][...] = refs[terms - 1][...]


def stack_kernel(*refs, start):
    for r, ref in enumerate(refs[:-1]):
        refs[-1][r] = ref[start:, :]


def sum_kernel(*refs, terms):
    refs[-1][...] = total(refs[:terms]).astype(bf16)


def join_kernel(early, late, order_ref, out, *, places):
    count = early.shape[0]
    for i, place in enumerate(places):
        out[place] = early[i] if i < count else late[i - count]


def mixed_kernel(*refs, hid):
    out = refs[hid]
    rows = refs[0].shape[0]
    me = lax.axis_index("hid")
    for m in range(hid):
        out[pl.ds(pl.multiple_of((me ^ m) * rows, rows), rows), :] = refs[m][...]


def adam(weight, moment, second, average, grad, rate):
    new_moment = 0.5 * moment + 0.5 * grad
    new_second = 0.5 * second + 0.5 * grad * grad
    correct = 1.0 - 0.5**STEP
    new_weight = weight - rate * (
        new_moment / correct / (jnp.sqrt(new_second / correct) + adam_eps) + decay_rate * weight
    )
    new_average = ema_decay * average + (1.0 - ema_decay) * new_weight
    return (new_weight, new_moment, new_second, new_average)


def table_adam_kernel(*refs, terms):
    state, parts, outs = refs[:4], refs[4 : 4 + terms], refs[4 + terms :]
    rows = state[0].shape[0]
    chunk = 64
    for i in range(rows // chunk):
        p = slice(i * chunk, (i + 1) * chunk)
        new = adam(*[s[p, :] for s in state], total(parts, p), 0.3)
        for out, value in zip(outs, new):
            out[p, :] = value


def weight_adam_kernel(*refs, terms, dp, hid):
    first, second, vector, gate = refs[0:4], refs[4:8], refs[8:12], refs[12:16]
    parts, outs = refs[16 : 16 + terms], refs[16 + terms :]
    first_out, second_out, vector_out, gate_out = outs[0:4], outs[4:8], outs[8:12], outs[12:16]
    rows, fold = D // dp, H // dp
    width = (O * EXPERTS) // dp
    new = adam(*[s[...] for s in first], total(parts, slice(0, rows)), 0.04)
    for out, value in zip(first_out, new):
        out[...] = value
    grad = total(parts, slice(rows, rows + fold))
    for i in range((H // hid) // fold):
        p = slice(i * fold, (i + 1) * fold)
        new = adam(*[s[p, :] for s in second], grad[:, i * width : (i + 1) * width], 0.06)
        for out, value in zip(second_out, new):
            out[p, :] = value
    small = total(parts, slice(rows + fold, None))
    cols, whole, packed, rest, _ = small_plan(hid)
    tail = small[GATES * whole : GATES * whole + rest]
    tail = jnp.concatenate([tail[:, i * HALF : (i + 1) * HALF] for i in range(packed)], axis=0)
    grad = jnp.concatenate(
        [small[i * GATES : (i + 1) * GATES] for i in range(whole)] + [tail[0:GATES]], axis=1
    )
    new = adam(*[s[...] for s in gate], grad, 0.03)
    for out, value in zip(gate_out, new):
        out[...] = value
    me = lax.axis_index("hid")
    base = GATES * whole + rest
    grad = jnp.zeros((3, cols), f32)
    for j in range(hid):
        grad = jnp.where(me == j, small[base + 3 * j : base + 3 * j + 3], grad)
    new = adam(*[s[...] for s in vector], grad, 0.2)
    for out, value in zip(vector_out, new):
        out[...] = value


def finish_kernel(*refs, table_terms, terms, dp, hid):
    a, b, c = 4 + table_terms, 16 + terms, hid
    ins, outs = refs[: a + b + c], refs[a + b + c :]
    mixed_kernel(*ins[a + b :], outs[0], hid=hid)
    table_adam_kernel(*ins[:a], *outs[1:5], terms=table_terms)
    weight_adam_kernel(*ins[a : a + b], *outs[5:], terms=terms, dp=dp, hid=hid)


def per_device(
    bag_offsets,
    embed_ids,
    block_owners,
    cotangent,
    table_w,
    table_m,
    table_v,
    table_ema,
    first_w,
    first_m,
    first_v,
    first_ema,
    second_w,
    second_m,
    second_v,
    second_ema,
    vector_w,
    vector_m,
    vector_v,
    vector_ema,
    gate_w,
    gate_m,
    gate_v,
    gate_ema,
):
    dp, hid = lax.axis_size("dp"), lax.axis_size("hid")
    inner = inner_size(dp)
    outer = dp // inner
    events, ids = bag_offsets.shape[0], embed_ids.shape[0]
    rows = events // hid
    slots, feats = table_w.shape
    vocab = block_owners.shape[0] * ROWS_BLOCK
    piece_rows = D // dp + H // dp
    piece_cols = first_w.shape[1]

    cot_rows = cotangent.shape[1] + 32
    weight_rows = 3 * piece_rows
    piece, keep = call(
        low_kernel,
        [shape((slots + weight_rows, feats), bf16)] * 2,
        (table_w, first_w, second_w),
        in_specs=[HBM] * 3,
        scratch=[
            pltpu.VMEM(table_w.shape, f32),
            pltpu.VMEM(first_w.shape, f32),
            pltpu.VMEM(second_w.shape, f32),
            pltpu.SemaphoreType.DMA((3,)),
        ],
        vmem=62,
        us=COST["low"],
    )
    nexts = jnp.concatenate([bag_offsets[1:], jnp.full((1,), ids, jnp.int32)])
    lanes = 128
    chunks = events // EVENTS_STEP

    def count_bags(i, *order):
        return call(
            functools.partial(counts_kernel, chunk=i),
            shape((EVENTS_STEP, vocab), bf16),
            (
                bag_offsets,
                id_columns,
                bag_offsets.reshape(events // lanes, lanes),
                nexts.reshape(events // lanes, lanes),
                *order,
            ),
            in_specs=[SMEM, VMEM, VMEM, VMEM] + [ANY] * len(order),
            scratch=[
                pltpu.VMEM((EVENTS_STEP, vocab), f32),
            ],
            vmem=12 if vocab <= 4096 else 40,
            us=COST["counts"],
        )

    far_pieces = {0: piece}
    step = outer // 2
    while step:
        far_pieces.update({f ^ step: swap(p, "dp", step * inner) for f, p in far_pieces.items()})
        step //= 2
    far_pieces = [far_pieces[f] for f in range(outer)]
    groups = [[keep] + far_pieces[1:]] + [[swap(p, "dp", near) for p in far_pieces] for near in range(1, inner)]

    def stack(group):
        return call(
            functools.partial(stack_kernel, start=slots),
            shape((len(group), weight_rows, feats), bf16),
            tuple(groups[near][far] for far, near in group),
            vmem=8,
            us=COST["stack"],
        )

    if OPT["n"]:
        first = [(far, 0) for far in range(outer)] + [(0, near) for near in range(1, inner)]
    else:
        first = [(far, 0) for far in range(outer)]
    rest = [(far, near) for far in range(outer) for near in range(inner) if (far, near) not in first]
    stacks = {0: [stack(first), stack(rest)]}
    id_columns, *cot_pieces = call(
        cut_kernel,
        [shape((ids // IDS_STEP, IDS_STEP, HALF), jnp.int16)]
        + [shape((cot_rows, rows), bf16) for m in range(hid)],
        (
            vector_w,
            cotangent.T,
            embed_ids.reshape(ids // lanes, lanes),
            (block_owners, far_pieces[outer // 2], far_pieces[outer - 1])[OPT["b"]],
        ),
        in_specs=[VMEM, VMEM, VMEM, ANY],
        vmem=8,
        us=COST["cut"],
    )
    cots = [cot_pieces[0]] + [swap(cot_pieces[m], "hid", m) for m in range(1, hid)]
    span = HALF * EXPERTS
    def make_turns(*order):
        return call(
            functools.partial(turns_kernel, hid=hid),
            [
                shape((3, EXPERTS, H, HALF), f32),
                shape((span, span), bf16),
                shape((O * STREAMS, O * STREAMS), bf16),
            ],
            (*cots, *order),
            in_specs=[VMEM] * hid + [ANY] * len(order),
            scratch=[pltpu.VMEM((hid, 16, piece_cols), bf16)],
            vmem=12,
            us=COST["turns"],
        )

    if not OPT["r"]:
        columns, turn, turn3t = make_turns()
    early = chunks // 2
    counts = [count_bags(i, *(((), (groups[1][0],), (far_pieces[1],), (groups[1][0], far_pieces[1]))[OPT["a"]] if i else ())) for i in range(early)]
    counts += [count_bags(i, *((), (far_pieces[outer // 2],), (far_pieces[outer // 2], far_pieces[1]), (groups[1][1],))[OPT["m"]]) for i in range(early, chunks - 1)]
    counts.append(count_bags(chunks - 1, *(((stacks[0][0],), ()) if OPT["r"] else ((stacks[0][0], turn3t), (turn3t,)))[OPT["j"]]))
    pieces = [groups[r % inner][r // inner] for r in range(dp)]
    pooled = call(
        functools.partial(pool_kernel, chunks=chunks, dp=dp, hid=hid),
        [shape((feats, rows), bf16) for m in range(hid)],
        (block_owners, *counts, *pieces),
        in_specs=[SMEM] + [VMEM] * (chunks + dp),
        scratch=[
            pltpu.VMEM((dp, slots, feats), bf16),
            pltpu.VMEM((vocab, feats), bf16),
            pltpu.VMEM((hid, rows, feats), f32),
            pltpu.SMEM((dp,), jnp.int32),
        ],
        vmem=20 if vocab <= 4096 else 58,
        us=COST["pool"],
    )
    if OPT["r"]:
        columns, turn, turn3t = make_turns(pooled[0])
    xts = [pooled[0]] + [swap(pooled[m], "hid", m) for m in range(1, hid)]
    for m in range(2, hid, 2):
        stacks[m] = [swap(part, "hid", m) for part in stacks[0]]
    places = [far * inner + near for far, near in first + rest]
    joined = {}
    for m in range(0, hid, 2):
        joined[m] = call(
            functools.partial(join_kernel, places=places),
            shape((dp, weight_rows, feats), bf16),
            (*stacks[m], (pooled[0], xts[1], xts[hid - 1])[OPT["i"]]),
            in_specs=[VMEM, VMEM, ANY],
            vmem=8,
            us=COST["join"],
        )
        joined[m + 1] = swap(joined[m], "hid", 1)
    w1p, w2p = call(
        functools.partial(weights_kernel, dp=dp, hid=hid),
        [shape((EXPERTS, D, H), bf16), shape((EXPERTS, H, O), bf16)],
        (*[joined[m] for m in range(hid)], turn),
        scratch=[
            pltpu.VMEM((hid, D, piece_cols), bf16),
            pltpu.VMEM((dp, H, (O * EXPERTS) // dp), bf16),
        ],
        vmem=20,
        us=COST["weights"],
    )

    gates = 16
    gate_pad = jnp.pad(gate_w.T, ((0, gates - gate_w.shape[1]), (0, 0)))
    small_rows = small_plan(hid)[-1]
    some = dp * piece_rows
    mixed_part, small, home, away, *d_pieces = call(
        functools.partial(main_kernel, dp=dp, hid=hid),
        [
            shape((rows, O * STREAMS), bf16),
            shape((small_rows, piece_cols), bf16),
            shape((hid // 2 * some, piece_cols), bf16),
            shape((hid // 2 * some + small_rows, piece_cols), bf16),
            *[shape((feats, rows), bf16) for m in range(hid)],
        ],
        (*xts, *cots, w1p, w2p, columns, turn, turn3t, gate_pad),
        scratch=[
            pltpu.VMEM((D, rows), bf16),
            pltpu.VMEM((EXPERTS, H, rows), bf16),
            pltpu.VMEM((EXPERTS, O, rows), bf16),
            pltpu.VMEM((EXPERTS, H, rows), bf16),
            pltpu.VMEM((O * STREAMS, rows), f32),
            pltpu.VMEM((O * STREAMS, rows), bf16),
            pltpu.VMEM((O * STREAMS, rows), f32),
            pltpu.VMEM((H, rows), f32),
            pltpu.VMEM((H, rows), f32),
            pltpu.VMEM((H, rows), f32),
            pltpu.VMEM((2, H, rows), bf16),
            pltpu.VMEM((D, rows), f32),
            pltpu.VMEM((3, EXPERTS, 8, H), f32),
            pltpu.VMEM((H * EXPERTS, rows), bf16),
            pltpu.VMEM((D, piece_cols), bf16),
            pltpu.VMEM((EXPERTS, H, O), bf16),
            pltpu.VMEM((H, O * EXPERTS), f32),
        ],
        vmem=36,
        us=COST["main"],
    )
    d_pooled = [d_pieces[0]] + [swap(d_pieces[m], "hid", m) for m in range(1, hid)]

    near_rows = some // inner
    def reduce_table(order):
        return call(
            functools.partial(table_kernel, chunks=chunks, dp=dp, hid=hid),
            [shape((slots, feats), bf16) for r in range(dp)],
            (block_owners, *counts, *d_pooled, order),
            in_specs=[SMEM] + [VMEM] * (chunks + hid) + [ANY],
            scratch=[
                pltpu.VMEM((feats, events), bf16),
                pltpu.VMEM((vocab, feats), bf16),
                pltpu.VMEM((dp, slots, feats), bf16),
                pltpu.SMEM((dp,), jnp.int32),
            ],
            vmem=20 if vocab <= 4096 else 58,
            us=COST["table"],
        )

    come = swap(away, "hid", 1)

    def half(nears, *order):
        return call(
            functools.partial(core_merge_kernel, rows=near_rows, inner=inner, nears=nears),
            [
                shape((near_rows + small_rows * (near > 0), piece_cols), bf16)
                for m in range(hid // 2)
                for near in nears
            ],
            (home, come, small, *order),
            in_specs=[VMEM] * 3 + [ANY] * len(order),
            vmem=12,
            us=COST["half"],
        )

    def chip_sum(parts, order, passing):
        result = call(
            functools.partial(chip_merge_kernel, terms=hid // 2, passing=len(passing)),
            [shape(v.shape, bf16) for v in (parts[0], *passing)],
            (parts[0], *[swap(parts[m], "hid", 2 * m) for m in range(1, hid // 2)])
            + (*passing, *order),
            in_specs=[VMEM] * (hid // 2 + len(passing)) + [ANY] * len(order),
            vmem=12,
            us=COST["chip"],
        )
        return result if passing else result[0]

    order = ((), (d_pooled[1],), (d_pooled[hid - 1],))[OPT["e"]]
    if OPT["q"]:
        parts = half(tuple(range(inner)), *order)
        parts = [parts[i::inner] for i in range(inner)]
    else:
        parts = half(tuple(range(1, inner)), *order)
        parts = [None] + [parts[i :: inner - 1] for i in range(inner - 1)]
    d_table = reduce_table((block_owners, parts[1][0])[OPT["f"]])
    sums = {}
    for far in reversed(range(outer)):
        terms = [d_table[far * inner]]
        terms += [swap(d_table[far * inner + m], "dp", m) for m in range(1, inner)]
        sums[far] = terms

    def add_up(terms, *order):
        return call(
            functools.partial(sum_kernel, terms=len(terms)),
            shape((slots, feats), bf16),
            (*terms, *order),
            in_specs=[VMEM] * len(terms) + [ANY] * len(order),
            vmem=4,
            us=COST["sum"],
        )

    last = outer - 1
    if OPT["c"] == 2:
        sums[last] = add_up(sums[last])
    orders = ((), (d_table[0],), (sums[last],))[OPT["c"]]
    chips = [None] + [chip_sum(parts[i], orders, ()) for i in range(1, inner)]
    order = ((), (chips[1],))[OPT["k"]]
    if not OPT["q"]:
        parts[0], order = half((0,), *order), ()
    if OPT["g"] == 1:
        chips[0], mixed_part = chip_sum(parts[0], order, (mixed_part,))
    else:
        chips[0] = chip_sum(parts[0], order, ())
    if OPT["c"] != 2:
        sums[last] = add_up(sums[last], *((), (chips[1],))[OPT["d"]])
    later = [far for far in range(1, last) if far % 2] if OPT["p"] and not OPT["h"] else []
    for far in range(last):
        if far not in later:
            sums[far] = functools.reduce(plus, sums[far])
    passing = (mixed_part,) if OPT["g"] == 0 else ()
    far_parts = call(
        functools.partial(
            near_merge_kernel, terms=inner, rows=piece_rows, outer=outer, passing=len(passing)
        ),
        [shape((piece_rows + small_rows, piece_cols), bf16)] * outer
        + [shape(v.shape, bf16) for v in passing],
        (chips[0], chips[1], *[swap(chips[i], "dp", i) for i in range(1, inner)], *passing),
        vmem=12,
        us=COST["near"],
    )
    if passing:
        mixed_part = far_parts[outer]
    weight_terms = [far_parts[0]] + [swap(far_parts[m], "dp", m * inner) for m in range(1, outer)]

    mixed_parts = {0: mixed_part}
    for m in range(2, hid, 2):
        mixed_parts[m] = swap(mixed_part, "hid", m)
    for m in range(0, hid, 2):
        mixed_parts[m + 1] = swap(mixed_parts[m], "hid", 1)
    if OPT["h"]:
        table_terms = [sums[0]]
        table_terms += [swap(sums[far], "dp", far * inner) for far in reversed(range(1, outer))]
    else:
        step = 1
        while step < outer // 2:
            for far in reversed([f for f in sums if f & step]):
                if far in later and step == 1:
                    sums[far] = add_up(sums[far], sums[(far ^ step) + 2])
                sums[far ^ step] = plus(sums[far ^ step], swap(sums.pop(far), "dp", step * inner))
            step *= 2
        table_terms = [sums[0], swap(sums[step], "dp", step * inner)]

    states = (
        table_w,
        table_m,
        table_v,
        table_ema,
        first_w,
        first_m,
        first_v,
        first_ema,
        second_w,
        second_m,
        second_v,
        second_ema,
        vector_w,
        vector_m,
        vector_v,
        vector_ema,
        *[g.T for g in (gate_w, gate_m, gate_v, gate_ema)],
    )
    mixed, *new = call(
        functools.partial(
            finish_kernel,
            table_terms=len(table_terms),
            terms=len(weight_terms),
            dp=dp,
            hid=hid,
        ),
        [shape((events, O * STREAMS), bf16)] + [shape(v.shape, f32) for v in states],
        (*states[:4], *table_terms, *states[4:], *weight_terms)
        + tuple(mixed_parts[m] for m in range(hid)),
        vmem=20,
        us=COST["finish"],
    )
    return (mixed, *new[:16], *[g.T for g in new[16:]])


def solution(mesh):
    split, spread, whole = P("dp", "hid"), P("hid", "dp"), P()
    return jax.shard_map(
        per_device,
        mesh=mesh,
        in_specs=(P("dp"), P("dp"), whole, split)
        + (split,) * 8
        + (spread,) * 4
        + (P(None, "hid"),) * 4
        + (whole,) * 4,
        out_specs=(P("dp", None),)
        + (split,) * 8
        + (spread,) * 4
        + (P(None, "hid"),) * 4
        + (whole,) * 4,
        check_vma=False,
    )
```

```python
import functools

import jax
import jax.numpy as jnp
from jax import lax
from jax.experimental import pallas as pl
from jax.experimental.pallas import tpu as pltpu
from jax.sharding import PartitionSpec as P

D = 512
H = 256
O = 256
EXPERTS = 6
STREAMS = 3
ROWS_BLOCK = 64
STEP = 5
CAP = 12
GATES = 14
HALF = 128
IDS_STEP = 256
EVENTS_STEP = 256

norm_eps = 1e-05
adam_eps = 1e-08
decay_rate = 0.01
ema_decay = 0.9

bf16 = jnp.bfloat16
f32 = jnp.float32
MIB = 1 << 20

STREAM_EXPERTS = ((0, 1, 4, 5), (2, 3, 4, 5), (0, 1, 2, 3, 4, 5))
STREAM_COLS = (0, 4, 8)

COST = {'low': 1.605, 'cut': 0.491, 'turns': 6.876, 'counts': 2.06, 'pool': 4.0, 'stack': 0.045, 'join': 0.7, 'weights': 0.778, 'main': 10.0, 'table': 6.0, 'half': 0.7, 'chip': 0.7, 'near': 1.0, 'sum': 0.5, 'finish': 3.0}
OPT = {'a': 1, 'b': 0, 'c': 0, 'd': 0, 'e': 0, 'f': 1, 'h': 0, 'i': 0, 'j': 1, 'k': 0, 'm': 3, 'n': 1, 'p': 0, 'r': 0, 's': 1}
RNG = {'a': 4, 'b': 3, 'c': 3, 'd': 2, 'e': 3, 'f': 2, 'h': 2, 'i': 3, 'j': 2, 'k': 4, 'm': 4, 'n': 2, 'p': 2, 'r': 2, 's': 4}

VMEM = pl.BlockSpec(memory_space=pltpu.VMEM)
SMEM = pl.BlockSpec(memory_space=pltpu.SMEM)
HBM = pl.BlockSpec(memory_space=pltpu.HBM)
ANY = pl.BlockSpec(memory_space=pl.ANY)


def shape(dims, dtype):
    return jax.ShapeDtypeStruct(tuple(dims), dtype)


def nn(a, b):
    return lax.dot_general(a, b, (((1,), (0,)), ((), ())), preferred_element_type=f32)


def nt(a, b):
    return lax.dot_general(a, b, (((1,), (1,)), ((), ())), preferred_element_type=f32)


def tn(a, b):
    return lax.dot_general(a, b, (((0,), (0,)), ((), ())), preferred_element_type=f32)


def call(kernel, out_shape, args, in_specs=None, scratch=(), vmem=24, us=2.0):
    single = not isinstance(out_shape, (list, tuple))
    outs = [out_shape] if single else list(out_shape)
    result = pl.pallas_call(
        kernel,
        out_shape=outs,
        in_specs=in_specs or [VMEM] * len(args),
        out_specs=[VMEM] * len(outs),
        scratch_shapes=list(scratch),
        compiler_params=pltpu.CompilerParams(vmem_limit_bytes=vmem * MIB),
        name=getattr(kernel, "func", kernel).__name__,
        cost_estimate=pl.CostEstimate(
            flops=int(us * 1.0e9), bytes_accessed=int(us * 3.0e6), transcendentals=0
        ),
    )(*args)
    return result[0] if single else result


def swap(value, axis, mask):
    count = lax.axis_size(axis)
    return lax.ppermute(value, axis, [(i, i ^ mask) for i in range(count)])


def inner_size(dp_count):
    return 1 << ((dp_count.bit_length() - 1) // 2)


def low_kernel(table_hbm, first_hbm, second_hbm, piece, keep, table, first, second, sems):
    copies = [
        pltpu.make_async_copy(source, target, sems.at[i])
        for i, (source, target) in enumerate(
            ((table_hbm, table), (first_hbm, first), (second_hbm, second))
        )
    ]
    for copy in copies:
        copy.start()
    copies[0].wait()
    slots, feats = table.shape
    for out in (piece, keep):
        out[0:slots, :] = table[...].astype(bf16)
    copies[1].wait()
    copies[2].wait()
    rows = first.shape[0]
    each = (piece.shape[0] - slots) // 3
    fold = each - rows
    folded = jnp.concatenate(
        [second[i * fold : (i + 1) * fold, :] for i in range(second.shape[0] // fold)], axis=1
    )
    for g in range(3):
        lanes = slice(g * feats, (g + 1) * feats)
        start = slots + g * each
        for out in (piece, keep):
            out[start : start + rows, :] = first[:, lanes].astype(bf16)
            out[start + rows : start + each, :] = folded[:, lanes].astype(bf16)


def cut_kernel(vector, cot, ids_ref, order_ref, idb, *cots):
    id_rows, lanes = ids_ref.shape
    per = IDS_STEP // lanes
    idt = ids_ref[...].T
    for q in range(id_rows):
        idb[q // per, (q % per) * lanes : (q % per + 1) * lanes, :] = jnp.broadcast_to(
            idt[:, q : q + 1], (lanes, HALF)
        ).astype(jnp.int16)
    me = lax.axis_index("hid")
    cols, width = cot.shape[0], cots[0].shape[1]
    rest = vector[...]
    terms = []
    for i in range(3):
        terms.append(rest.astype(bf16).astype(f32))
        rest = rest - terms[i]
    span = vector.shape[1]
    stack = jnp.concatenate(terms + [jnp.zeros((7, span), f32)], axis=0)
    over = jnp.concatenate([stack[:, width:], jnp.zeros((16, 2 * width - span), f32)], axis=1)
    for m, out in enumerate(cots):
        start = pl.multiple_of((me ^ m) * width, width)
        out[0:cols, :] = cot[:, pl.ds(start, width)]
        out[cols : cols + 16, :] = stack[:, 0:width].astype(bf16)
        out[cols + 16 :, :] = over.astype(bf16)


def counts_kernel(offs_ref, idb, off_ref, nxt_ref, *refs, chunk):
    c_ref, acc = refs[-2:]
    vocab = c_ref.shape[1]
    lanes = off_ref.shape[1]
    events = off_ref.shape[0] * lanes
    offt = off_ref[...].T
    nxtt = nxt_ref[...].T
    cols = EVENTS_STEP // lanes
    width = 512
    lane = lax.broadcasted_iota(jnp.int32, (IDS_STEP, HALF), 1).astype(jnp.int16)
    one, zero = jnp.ones((IDS_STEP, HALF), bf16), jnp.zeros((IDS_STEP, HALF), bf16)
    first = jnp.concatenate([offt[:, chunk * cols + i : chunk * cols + i + 1] for i in range(cols)], 0)
    last = jnp.concatenate([nxtt[:, chunk * cols + i : chunk * cols + i + 1] for i in range(cols)], 0)
    acc[...] = jnp.zeros_like(acc)
    low = offs_ref[chunk * EVENTS_STEP]
    if (chunk + 1) * EVENTS_STEP < events:
        high = offs_ref[(chunk + 1) * EVENTS_STEP]
    else:
        high = jnp.int32(idb.shape[0] * IDS_STEP)

    def body(step, carry):
        place = step * IDS_STEP + lax.broadcasted_iota(jnp.int32, (EVENTS_STEP, IDS_STEP), 1)
        member = jnp.where((place >= first) & (place < last), 1.0, 0.0).astype(bf16)
        ids = idb[step]
        for v in range(vocab // width):
            hot = jnp.concatenate(
                [
                    jnp.where(ids == lane + jnp.int16(v * width + i * HALF), one, zero)
                    for i in range(width // HALF)
                ],
                axis=1,
            )
            acc[:, v * width : (v + 1) * width] += nn(member, hot)
        return carry

    lax.fori_loop(low // IDS_STEP, (high + IDS_STEP - 1) // IDS_STEP, body, 0)
    c_ref[...] = acc[...].astype(bf16)


def each_block(owners_ref, count_ref, owners, body):
    for o in range(owners):
        count_ref[o] = 0

    def step(block, carry):
        owner = owners_ref[block]
        rank = count_ref[owner]
        count_ref[owner] = rank + 1
        body(block, owner, rank)
        return carry

    lax.fori_loop(0, owners_ref.shape[0], step, 0)


def pool_kernel(owners_ref, *refs, chunks, dp, hid):
    counts, pieces = refs[:chunks], refs[chunks : chunks + dp]
    outs = refs[chunks + dp : chunks + dp + hid]
    whole, table, pooled, count_ref = refs[chunks + dp + hid :]
    me_dp, me_hid = lax.axis_index("dp"), lax.axis_index("hid")
    slots = whole.shape[1]
    for r in range(dp):
        whole[me_dp ^ r] = pieces[r][0:slots, :]

    def place(block, owner, rank):
        table[pl.ds(pl.multiple_of(block * ROWS_BLOCK, ROWS_BLOCK), ROWS_BLOCK), :] = whole[
            owner, pl.ds(pl.multiple_of(rank * ROWS_BLOCK, ROWS_BLOCK), ROWS_BLOCK), :
        ]

    each_block(owners_ref, count_ref, dp, place)
    rows = pooled.shape[1]
    per = EVENTS_STEP // rows
    for q in range(hid):
        part = slice((q % per) * rows, (q % per + 1) * rows)
        pooled[q] = nn(counts[q // per][part, :], table[...])
    for m in range(hid):
        outs[m][...] = pooled[me_hid ^ m].T.astype(bf16)


def hot_cv(rows, cols, mult, start):
    group = cols // mult
    col = lax.broadcasted_iota(jnp.int32, (8, cols), 1)
    target = ((col % group) * mult + col // group - start)[0:1]
    row = lax.broadcasted_iota(jnp.int32, (rows, cols), 0)
    return jnp.where(row == target, 1.0, 0.0).astype(bf16)


def hot_vc(rows, cols, mult, start):
    group = rows // mult
    row = lax.broadcasted_iota(jnp.int32, (rows, HALF), 0)
    target = ((row % group) * mult + row // group - start)[:, 0:1]
    col = lax.broadcasted_iota(jnp.int32, (rows, cols), 1)
    return jnp.where(col == target, 1.0, 0.0).astype(bf16)


def turns_kernel(*refs, hid):
    cots = refs[:hid]
    col_ref, q_ref, q3t_ref, vecs = refs[-4:]
    me_hid = lax.axis_index("hid")
    j_step = vecs.shape[2]
    for r in range(hid):
        cols, near = cots[r].shape[0] - 32, cots[r].shape[1]
        vecs[me_hid ^ r] = jnp.concatenate(
            [cots[r][cols : cols + 16, :], cots[r][cols + 16 : cols + 32, 0 : j_step - near]], axis=1
        )
    span = HALF * EXPERTS
    q_ref[...] = hot_cv(span, span, EXPERTS, 0)
    q3t_ref[...] = hot_vc(O * STREAMS, O * STREAMS, STREAMS, 0)
    for half in range(2):
        lanes = slice(half * HALF, (half + 1) * HALF)
        value = None
        for i in range(span // j_step):
            c = nt(hot_vc(span, j_step, EXPERTS, i * j_step), vecs[half * (span // j_step) + i])
            value = c if value is None else value + c
        cols = value[:, 0:3] + value[:, 3:6] + value[:, 6:9]
        for e in range(EXPERTS):
            for i in range(3):
                col_ref[i, e, lanes, :] = jnp.broadcast_to(
                    cols[e * HALF : (e + 1) * HALF, i : i + 1], (HALF, HALF)
                )


def weights_kernel(*refs, dp, hid):
    inner = inner_size(dp)
    given = hid
    stacks, q_ref = refs[:given], refs[given]
    w1p, w2p = refs[given + 1 : given + 3]
    w1s, w2s = refs[given + 3 :]
    me_dp, me_hid = lax.axis_index("dp"), lax.axis_index("hid")
    rows = D // dp
    fold = H // dp
    each = rows + fold
    width = (O * EXPERTS) // dp
    high = H // hid
    feats = stacks[0].shape[-1]
    j_step = w1s.shape[2]
    k_step = w2s.shape[2]
    for r in range(hid):
        j = me_hid ^ r
        for s in range(dp):
            k = me_dp ^ s
            for g in range(3):
                w1s[j, pl.ds(pl.multiple_of(k * rows, rows), rows), g * feats : (g + 1) * feats] = (
                    stacks[r][s, g * each : g * each + rows, :]
                )
            part = jnp.concatenate(
                [stacks[r][s, g * each + rows : (g + 1) * each, :].astype(f32) for g in range(3)],
                axis=1,
            )
            for q in range(high // fold):
                start = pl.multiple_of(j * high + q * fold, fold)
                w2s[k, pl.ds(start, fold), :] = part[:, q * width : (q + 1) * width].astype(bf16)
    span = HALF * EXPERTS
    for half in range(2):
        lanes = slice(half * HALF, (half + 1) * HALF)
        for step, source, out in ((j_step, w1s, w1p), (k_step, w2s, w2p)):
            value = None
            for i in range(span // step):
                p = nn(source[half * (span // step) + i], q_ref[i * step : (i + 1) * step, :])
                value = p if value is None else value + p
            for e in range(EXPERTS):
                out[e, :, lanes] = value[:, e * HALF : (e + 1) * HALF].astype(bf16)


def small_plan(hid):
    width = (H * EXPERTS) // hid
    whole = D // width
    packed = width // HALF
    rest = -(-GATES // packed)
    used = GATES * whole + rest + 3 * hid
    return width, whole, packed, rest, -(-used // 16) * 16


def softmax_rows(logits):
    top = jnp.max(logits, axis=0, keepdims=True)
    grown = jnp.exp(logits - top)
    return grown / jnp.sum(grown, axis=0, keepdims=True)


def wide(column, width):
    return jnp.concatenate([column] * (width // HALF), axis=1) if width > HALF else column


def main_kernel(*refs, dp, hid):
    xts, cots = refs[:hid], refs[hid : 2 * hid]
    w1p, w2p, col_ref, q_ref, q3t_ref, gate_ref = refs[2 * hid : 2 * hid + 6]
    outs = refs[2 * hid + 6 :]
    mixed_ref, small_ref, home, away = outs[:4]
    dx_outs = outs[4 : 4 + hid]
    xt, hid_ref, dinner_ref, dpre_ref, up, upq, mix, work, slope, norm, dout, dx, vec = outs[
        4 + hid : 17 + hid
    ]
    turned, w1g, w2n, w2g = outs[17 + hid :]
    me = lax.axis_index("hid")
    feats, rows = xts[0].shape
    for m in range(hid):
        j = me ^ m
        xt[pl.ds(pl.multiple_of(j * feats, feats), feats), :] = xts[m][...]
        cols = cots[m].shape[0] - 32
        upq[pl.ds(pl.multiple_of(j * cols, cols), cols), :] = cots[m][0:cols, :]
    up[...] = nn(q3t_ref[...], upq[...])
    gate = gate_ref[...].astype(bf16)
    logits = nn(gate, xt[...])
    chances = [
        softmax_rows(logits[STREAM_COLS[t] : STREAM_COLS[t] + len(STREAM_EXPERTS[t])])
        for t in range(STREAMS)
    ]
    mix[...] = jnp.zeros_like(mix)
    chunk = 64
    parts = [slice(i * chunk, (i + 1) * chunk) for i in range(O // chunk)]
    ones = jnp.ones((8, rows), bf16)
    d_chances = [[None] * len(STREAM_EXPERTS[t]) for t in range(STREAMS)]
    for e in range(EXPERTS):
        streams = [t for t in range(STREAMS) if e in STREAM_EXPERTS[t]]
        coef = {
            t: chances[t][STREAM_EXPERTS[t].index(e) : STREAM_EXPERTS[t].index(e) + 1]
            for t in streams
        }
        work[...] = tn(w1p[e], xt[...])
        for p in parts:
            pre = work[p, :] + wide(col_ref[0, e, p, :], rows)
            phi = 0.5 + 0.5 * lax.erf(pre * 0.7071067811865476)
            hid_ref[e, p, :] = (pre * phi).astype(bf16)
            slope[p, :] = phi + pre * (jnp.exp(-0.5 * pre * pre) * 0.3989422804014327)
        work[...] = tn(w2p[e], hid_ref[e])
        total = jnp.zeros((1, rows), f32)
        for p in parts:
            total = total + jnp.sum(work[p, :], axis=0, keepdims=True)
        mean = total * (1.0 / O)
        total = jnp.zeros((1, rows), f32)
        for p in parts:
            off = work[p, :] - mean
            total = total + jnp.sum(off * off, axis=0, keepdims=True)
        inverse = lax.rsqrt(total * (1.0 / O) + norm_eps)
        sums = {t: jnp.zeros((1, rows), f32) for t in streams}
        first, second = jnp.zeros((1, rows), f32), jnp.zeros((1, rows), f32)
        for i, p in enumerate(parts):
            normed = (work[p, :] - mean) * inverse
            gain = wide(col_ref[1, e, p, :], rows)
            value = normed * gain + wide(col_ref[2, e, p, :], rows)
            grad = None
            for t in streams:
                rows_t = slice(t * O + i * chunk, t * O + (i + 1) * chunk)
                mix[rows_t, :] += value * coef[t]
                upward = up[rows_t, :]
                sums[t] = sums[t] + jnp.sum(upward * value, axis=0, keepdims=True)
                term = upward * coef[t]
                grad = term if grad is None else grad + term
            d_norm = grad * gain
            first = first + jnp.sum(d_norm, axis=0, keepdims=True)
            second = second + jnp.sum(d_norm * normed, axis=0, keepdims=True)
            norm[p, :] = normed
            work[p, :] = d_norm
            dout[0, p, :] = (grad * normed).astype(bf16)
            dout[1, p, :] = grad.astype(bf16)
        for t in streams:
            d_chances[t][STREAM_EXPERTS[t].index(e)] = sums[t]
        first, second = first * (1.0 / O), second * (1.0 / O)
        for p in parts:
            dinner_ref[e, p, :] = ((work[p, :] - first - norm[p, :] * second) * inverse).astype(bf16)
        work[...] = nn(w2p[e], dinner_ref[e])
        for p in parts:
            dpre_ref[e, p, :] = (work[p, :] * slope[p, :]).astype(bf16)
        w2n[e] = nt(hid_ref[e], dinner_ref[e]).astype(bf16)
        vec[0, e] = nt(ones, dpre_ref[e])
        vec[1, e] = nt(ones, dout[0])
        vec[2, e] = nt(ones, dout[1])
        back = nn(w1p[e], dpre_ref[e])
        if e == 0:
            dx[...] = back
        else:
            dx[...] += back
    d_logits = []
    for t in range(STREAMS):
        upward = jnp.concatenate(d_chances[t], axis=0)
        g = chances[t]
        d_logits.append(g * (upward - jnp.sum(g * upward, axis=0, keepdims=True)))
    pad = jnp.zeros((gate_ref.shape[0] - GATES, rows), f32)
    d_logits = jnp.concatenate(d_logits + [pad], axis=0).astype(bf16)
    dx[...] += tn(gate, d_logits)
    for m in range(hid):
        start = pl.multiple_of((me ^ m) * feats, feats)
        dx_outs[m][...] = dx[pl.ds(start, feats), :].astype(bf16)
    width, whole, packed, rest, small_rows = small_plan(hid)
    d_gate = nt(d_logits, xt[...])[0:GATES]
    lines = [d_gate[:, i * width : (i + 1) * width] for i in range(whole)]
    tail = d_gate[:, whole * width :]
    if rest * packed > GATES:
        tail = jnp.concatenate([tail, jnp.zeros((rest * packed - GATES, HALF), f32)], axis=0)
    tail = jnp.concatenate([tail[i * rest : (i + 1) * rest] for i in range(packed)], axis=1)
    if packed * HALF < width:
        tail = jnp.concatenate([tail, jnp.zeros((rest, width - packed * HALF), f32)], axis=1)
    lines.append(tail)
    for half in range(2):
        lanes = slice(half * HALF, (half + 1) * HALF)
        stack = jnp.concatenate(
            [
                jnp.concatenate([vec[i, e, 0:1, lanes] for e in range(EXPERTS)], axis=1)
                for i in range(3)
            ]
            + [jnp.zeros((5, HALF * EXPERTS), f32)],
            axis=0,
        ).astype(bf16)
        unturned = nt(stack, q_ref[...])
        for i in range((HALF * EXPERTS) // width):
            lines.append(unturned[0:3, i * width : (i + 1) * width])
    spare = small_rows - sum(line.shape[0] for line in lines)
    if spare:
        lines.append(jnp.zeros((spare, width), f32))
    small_ref[...] = jnp.concatenate(lines, axis=0).astype(bf16)
    mixed_ref[...] = tn(mix[...].astype(bf16), q3t_ref[...]).astype(bf16)
    me_dp = lax.axis_index("dp")
    span = HALF * EXPERTS
    first_rows = D // dp
    fold = H // dp
    each = first_rows + fold
    second_cols = (O * EXPERTS) // dp
    high = H // hid
    inner = inner_size(dp)
    outer = dp // inner
    for half in range(2):
        part = slice(half * HALF, (half + 1) * HALF)
        block = jnp.concatenate([dpre_ref[e, part, :] for e in range(EXPERTS)], axis=0)
        turned[half * span : (half + 1) * span, :] = nn(q_ref[...], block).astype(bf16)
        block = jnp.concatenate([w2n[e, :, part] for e in range(EXPERTS)], axis=1)
        w2g[:, half * span : (half + 1) * span] = nt(block, q_ref[...])
    for m in range(hid):
        out, base = (away if m % 2 else home), (m // 2) * dp * each
        j = me ^ m
        left = turned[pl.ds(pl.multiple_of(j * width, width), width), :]
        w1g[...] = nt(xt[...], left).astype(bf16)
        for near in range(inner):
            for far in range(outer):
                k = me_dp ^ (far * inner + near)
                start = pl.multiple_of(k * first_rows, first_rows)
                to = base + (near * outer + far) * each
                out[to : to + first_rows, :] = w1g[pl.ds(start, first_rows), :]
        start = pl.multiple_of(j * high, high)
        for k in range(dp):
            part = w2g[pl.ds(start, high), k * second_cols : (k + 1) * second_cols]
            folded = jnp.concatenate(
                [part[i * fold : (i + 1) * fold, :] for i in range(high // fold)], axis=1
            ).astype(bf16)
            r = me_dp ^ k
            to = base + ((r % inner) * outer + r // inner) * each + first_rows
            out[pl.ds(pl.multiple_of(to, fold), fold), :] = folded
    away[(hid // 2) * dp * each :, :] = small_ref[...]


def table_kernel(owners_ref, *refs, chunks, dp, hid):
    counts, pieces = refs[:chunks], refs[chunks : chunks + hid]
    outs = refs[chunks + hid + 1 : chunks + hid + 1 + dp]
    back, grads, slots, count_ref = refs[chunks + hid + 1 + dp :]
    me_dp, me_hid = lax.axis_index("dp"), lax.axis_index("hid")
    rows = pieces[0].shape[1]
    for m in range(hid):
        start = pl.multiple_of((me_hid ^ m) * rows, rows)
        back[:, pl.ds(start, rows)] = pieces[m][...]
    part = None
    for i in range(chunks):
        p = nn(back[:, i * EVENTS_STEP : (i + 1) * EVENTS_STEP], counts[i][...])
        part = p if part is None else part + p
    grads[...] = part.T.astype(bf16)
    slots[...] = jnp.zeros_like(slots)

    def place(block, owner, rank):
        slots[
            owner ^ me_dp, pl.ds(pl.multiple_of(rank * ROWS_BLOCK, ROWS_BLOCK), ROWS_BLOCK), :
        ] = grads[pl.ds(pl.multiple_of(block * ROWS_BLOCK, ROWS_BLOCK), ROWS_BLOCK), :]

    each_block(owners_ref, count_ref, dp, place)
    for r in range(dp):
        outs[r][...] = slots[r]


def total(refs, *at):
    values = [(ref[at] if at else ref[...]).astype(f32) for ref in refs]
    while len(values) > 1:
        values = [values[i] + values[i + 1] for i in range(0, len(values), 2)]
    return values[0]


def plus(a, b):
    return (a.astype(f32) + b.astype(f32)).astype(bf16)


def core_merge_kernel(home, come, small, *refs, rows, inner, nears):
    chips = home.shape[0] // rows // inner
    outs = refs[-chips * len(nears) :]
    last = plus(small[...], come[home.shape[0] :, :])
    for m in range(chips):
        for i, near in enumerate(nears):
            out = outs[m * len(nears) + i]
            part = slice((m * inner + near) * rows, (m * inner + near + 1) * rows)
            out[0:rows, :] = plus(home[part, :], come[part, :])
            if near:
                out[rows:, :] = last


def chip_merge_kernel(*refs, terms):
    refs[-1][...] = total(refs[:terms]).astype(bf16)


def stay_kernel(home, come, mixed, order_ref, *outs, rows, inner):
    cols = home.shape[1]
    events = mixed.shape[0]
    for m, out in enumerate(outs):
        part = slice(m * inner * rows, (m * inner + 1) * rows)
        out[0:rows, :] = plus(home[part, :], come[part, :])
        if m:
            for i in range(mixed.shape[1] // cols):
                out[rows + i * events : rows + (i + 1) * events, :] = mixed[:, i * cols : (i + 1) * cols]


def stay_merge_kernel(*refs, terms, rows):
    parts, mixed, sums, pieces = refs[:terms], refs[terms], refs[-2], refs[-1]
    sums[...] = total(parts, slice(0, rows)).astype(bf16)
    cols = sums.shape[1]
    pieces[0] = mixed[...]
    events = mixed.shape[0]
    for m in range(1, terms):
        for i in range(mixed.shape[1] // cols):
            pieces[m, :, i * cols : (i + 1) * cols] = parts[m][
                rows + i * events : rows + (i + 1) * events, :
            ]


def near_merge_kernel(mine, other, *refs, terms, rows, outer):
    come, outs = refs[: terms - 1], refs[terms - 1 :]
    last = total((other, *come), slice(outer * rows, None)).astype(bf16)
    for far in range(outer):
        part = slice(far * rows, (far + 1) * rows)
        outs[far][0:rows, :] = total((mine, *come), part).astype(bf16)
        outs[far][rows:, :] = last


def stack_kernel(*refs, start):
    for r, ref in enumerate(refs[:-1]):
        refs[-1][r] = ref[start:, :]


def sum_kernel(*refs, terms):
    refs[-1][...] = total(refs[:terms]).astype(bf16)


def join_kernel(early, late, order_ref, out, *, places):
    count = early.shape[0]
    for i, place in enumerate(places):
        out[place] = early[i] if i < count else late[i - count]


def mixed_kernel(own, other, out, *, hid):
    rows = own.shape[1]
    me = lax.axis_index("hid")
    for m in range(hid):
        start = pl.multiple_of((me ^ m) * rows, rows)
        out[pl.ds(start, rows), :] = other[m // 2] if m % 2 else own[m // 2]


def adam(weight, moment, second, average, grad, rate):
    new_moment = 0.5 * moment + 0.5 * grad
    new_second = 0.5 * second + 0.5 * grad * grad
    correct = 1.0 - 0.5**STEP
    new_weight = weight - rate * (
        new_moment / correct / (jnp.sqrt(new_second / correct) + adam_eps) + decay_rate * weight
    )
    new_average = ema_decay * average + (1.0 - ema_decay) * new_weight
    return (new_weight, new_moment, new_second, new_average)


def table_adam_kernel(*refs, terms):
    state, parts, outs = refs[:4], refs[4 : 4 + terms], refs[4 + terms :]
    rows = state[0].shape[0]
    chunk = 64
    for i in range(rows // chunk):
        p = slice(i * chunk, (i + 1) * chunk)
        new = adam(*[s[p, :] for s in state], total(parts, p), 0.3)
        for out, value in zip(outs, new):
            out[p, :] = value


def weight_adam_kernel(*refs, terms, dp, hid):
    first, second, vector, gate = refs[0:4], refs[4:8], refs[8:12], refs[12:16]
    parts, outs = refs[16 : 16 + terms], refs[16 + terms :]
    first_out, second_out, vector_out, gate_out = outs[0:4], outs[4:8], outs[8:12], outs[12:16]
    rows, fold = D // dp, H // dp
    width = (O * EXPERTS) // dp
    new = adam(*[s[...] for s in first], total(parts, slice(0, rows)), 0.04)
    for out, value in zip(first_out, new):
        out[...] = value
    grad = total(parts, slice(rows, rows + fold))
    for i in range((H // hid) // fold):
        p = slice(i * fold, (i + 1) * fold)
        new = adam(*[s[p, :] for s in second], grad[:, i * width : (i + 1) * width], 0.06)
        for out, value in zip(second_out, new):
            out[p, :] = value
    small = total(parts, slice(rows + fold, None))
    cols, whole, packed, rest, _ = small_plan(hid)
    tail = small[GATES * whole : GATES * whole + rest]
    tail = jnp.concatenate([tail[:, i * HALF : (i + 1) * HALF] for i in range(packed)], axis=0)
    grad = jnp.concatenate(
        [small[i * GATES : (i + 1) * GATES] for i in range(whole)] + [tail[0:GATES]], axis=1
    )
    new = adam(*[s[...] for s in gate], grad, 0.03)
    for out, value in zip(gate_out, new):
        out[...] = value
    me = lax.axis_index("hid")
    base = GATES * whole + rest
    grad = jnp.zeros((3, cols), f32)
    for j in range(hid):
        grad = jnp.where(me == j, small[base + 3 * j : base + 3 * j + 3], grad)
    new = adam(*[s[...] for s in vector], grad, 0.2)
    for out, value in zip(vector_out, new):
        out[...] = value


def finish_kernel(*refs, table_terms, terms, dp, hid):
    a, b, c = 4 + table_terms, 16 + terms, 2
    ins, outs = refs[: a + b + c], refs[a + b + c :]
    mixed_kernel(*ins[a + b :], outs[0], hid=hid)
    table_adam_kernel(*ins[:a], *outs[1:5], terms=table_terms)
    weight_adam_kernel(*ins[a : a + b], *outs[5:], terms=terms, dp=dp, hid=hid)


def per_device(
    bag_offsets,
    embed_ids,
    block_owners,
    cotangent,
    table_w,
    table_m,
    table_v,
    table_ema,
    first_w,
    first_m,
    first_v,
    first_ema,
    second_w,
    second_m,
    second_v,
    second_ema,
    vector_w,
    vector_m,
    vector_v,
    vector_ema,
    gate_w,
    gate_m,
    gate_v,
    gate_ema,
):
    dp, hid = lax.axis_size("dp"), lax.axis_size("hid")
    inner = inner_size(dp)
    outer = dp // inner
    events, ids = bag_offsets.shape[0], embed_ids.shape[0]
    rows = events // hid
    slots, feats = table_w.shape
    vocab = block_owners.shape[0] * ROWS_BLOCK
    piece_rows = D // dp + H // dp
    piece_cols = first_w.shape[1]

    cot_rows = cotangent.shape[1] + 32
    weight_rows = 3 * piece_rows
    piece, keep = call(
        low_kernel,
        [shape((slots + weight_rows, feats), bf16)] * 2,
        (table_w, first_w, second_w),
        in_specs=[HBM] * 3,
        scratch=[
            pltpu.VMEM(table_w.shape, f32),
            pltpu.VMEM(first_w.shape, f32),
            pltpu.VMEM(second_w.shape, f32),
            pltpu.SemaphoreType.DMA((3,)),
        ],
        vmem=62,
        us=COST["low"],
    )
    nexts = jnp.concatenate([bag_offsets[1:], jnp.full((1,), ids, jnp.int32)])
    lanes = 128
    chunks = events // EVENTS_STEP

    def count_bags(i, *order):
        return call(
            functools.partial(counts_kernel, chunk=i),
            shape((EVENTS_STEP, vocab), bf16),
            (
                bag_offsets,
                id_columns,
                bag_offsets.reshape(events // lanes, lanes),
                nexts.reshape(events // lanes, lanes),
                *order,
            ),
            in_specs=[SMEM, VMEM, VMEM, VMEM] + [ANY] * len(order),
            scratch=[
                pltpu.VMEM((EVENTS_STEP, vocab), f32),
            ],
            vmem=12 if vocab <= 4096 else 40,
            us=COST["counts"],
        )

    far_pieces = {0: piece}
    step = outer // 2
    while step:
        far_pieces.update({f ^ step: swap(p, "dp", step * inner) for f, p in far_pieces.items()})
        step //= 2
    far_pieces = [far_pieces[f] for f in range(outer)]
    groups = [[keep] + far_pieces[1:]] + [[swap(p, "dp", near) for p in far_pieces] for near in range(1, inner)]

    def stack(group):
        return call(
            functools.partial(stack_kernel, start=slots),
            shape((len(group), weight_rows, feats), bf16),
            tuple(groups[near][far] for far, near in group),
            vmem=8,
            us=COST["stack"],
        )

    if OPT["n"]:
        first = [(far, 0) for far in range(outer)] + [(0, near) for near in range(1, inner)]
    else:
        first = [(far, 0) for far in range(outer)]
    rest = [(far, near) for far in range(outer) for near in range(inner) if (far, near) not in first]
    stacks = {0: [stack(first), stack(rest)]}
    id_columns, *cot_pieces = call(
        cut_kernel,
        [shape((ids // IDS_STEP, IDS_STEP, HALF), jnp.int16)]
        + [shape((cot_rows, rows), bf16) for m in range(hid)],
        (
            vector_w,
            cotangent.T,
            embed_ids.reshape(ids // lanes, lanes),
            (block_owners, far_pieces[outer // 2], far_pieces[outer - 1])[OPT["b"]],
        ),
        in_specs=[VMEM, VMEM, VMEM, ANY],
        vmem=8,
        us=COST["cut"],
    )
    cots = [cot_pieces[0]] + [swap(cot_pieces[m], "hid", m) for m in range(1, hid)]
    span = HALF * EXPERTS
    def make_turns(*order):
        return call(
            functools.partial(turns_kernel, hid=hid),
            [
                shape((3, EXPERTS, H, HALF), f32),
                shape((span, span), bf16),
                shape((O * STREAMS, O * STREAMS), bf16),
            ],
            (*cots, *order),
            in_specs=[VMEM] * hid + [ANY] * len(order),
            scratch=[pltpu.VMEM((hid, 16, piece_cols), bf16)],
            vmem=12,
            us=COST["turns"],
        )

    if not OPT["r"]:
        columns, turn, turn3t = make_turns()
    early = chunks // 2
    counts = [count_bags(i, *(((), (groups[1][0],), (far_pieces[1],), (groups[1][0], far_pieces[1]))[OPT["a"]] if i else ())) for i in range(early)]
    counts += [count_bags(i, *((), (far_pieces[outer // 2],), (far_pieces[outer // 2], far_pieces[1]), (groups[1][1],))[OPT["m"]]) for i in range(early, chunks - 1)]
    counts.append(count_bags(chunks - 1, *(((stacks[0][0],), ()) if OPT["r"] else ((stacks[0][0], turn3t), (turn3t,)))[OPT["j"]]))
    pieces = [groups[r % inner][r // inner] for r in range(dp)]
    pooled = call(
        functools.partial(pool_kernel, chunks=chunks, dp=dp, hid=hid),
        [shape((feats, rows), bf16) for m in range(hid)],
        (block_owners, *counts, *pieces),
        in_specs=[SMEM] + [VMEM] * (chunks + dp),
        scratch=[
            pltpu.VMEM((dp, slots, feats), bf16),
            pltpu.VMEM((vocab, feats), bf16),
            pltpu.VMEM((hid, rows, feats), f32),
            pltpu.SMEM((dp,), jnp.int32),
        ],
        vmem=20 if vocab <= 4096 else 58,
        us=COST["pool"],
    )
    if OPT["r"]:
        columns, turn, turn3t = make_turns(pooled[0])
    xts = [pooled[0]] + [swap(pooled[m], "hid", m) for m in range(1, hid)]
    for m in range(2, hid, 2):
        stacks[m] = [swap(part, "hid", m) for part in stacks[0]]
    places = [far * inner + near for far, near in first + rest]
    joined = {}
    for m in range(0, hid, 2):
        joined[m] = call(
            functools.partial(join_kernel, places=places),
            shape((dp, weight_rows, feats), bf16),
            (*stacks[m], (pooled[0], xts[1], xts[hid - 1])[OPT["i"]]),
            in_specs=[VMEM, VMEM, ANY],
            vmem=8,
            us=COST["join"],
        )
        joined[m + 1] = swap(joined[m], "hid", 1)
    w1p, w2p = call(
        functools.partial(weights_kernel, dp=dp, hid=hid),
        [shape((EXPERTS, D, H), bf16), shape((EXPERTS, H, O), bf16)],
        (*[joined[m] for m in range(hid)], turn),
        scratch=[
            pltpu.VMEM((hid, D, piece_cols), bf16),
            pltpu.VMEM((dp, H, (O * EXPERTS) // dp), bf16),
        ],
        vmem=20,
        us=COST["weights"],
    )

    gates = 16
    gate_pad = jnp.pad(gate_w.T, ((0, gates - gate_w.shape[1]), (0, 0)))
    small_rows = small_plan(hid)[-1]
    some = dp * piece_rows
    mixed_part, small, home, away, *d_pieces = call(
        functools.partial(main_kernel, dp=dp, hid=hid),
        [
            shape((rows, O * STREAMS), bf16),
            shape((small_rows, piece_cols), bf16),
            shape((hid // 2 * some, piece_cols), bf16),
            shape((hid // 2 * some + small_rows, piece_cols), bf16),
            *[shape((feats, rows), bf16) for m in range(hid)],
        ],
        (*xts, *cots, w1p, w2p, columns, turn, turn3t, gate_pad),
        scratch=[
            pltpu.VMEM((D, rows), bf16),
            pltpu.VMEM((EXPERTS, H, rows), bf16),
            pltpu.VMEM((EXPERTS, O, rows), bf16),
            pltpu.VMEM((EXPERTS, H, rows), bf16),
            pltpu.VMEM((O * STREAMS, rows), f32),
            pltpu.VMEM((O * STREAMS, rows), bf16),
            pltpu.VMEM((O * STREAMS, rows), f32),
            pltpu.VMEM((H, rows), f32),
            pltpu.VMEM((H, rows), f32),
            pltpu.VMEM((H, rows), f32),
            pltpu.VMEM((2, H, rows), bf16),
            pltpu.VMEM((D, rows), f32),
            pltpu.VMEM((3, EXPERTS, 8, H), f32),
            pltpu.VMEM((H * EXPERTS, rows), bf16),
            pltpu.VMEM((D, piece_cols), bf16),
            pltpu.VMEM((EXPERTS, H, O), bf16),
            pltpu.VMEM((H, O * EXPERTS), f32),
        ],
        vmem=36,
        us=COST["main"],
    )
    d_pooled = [d_pieces[0]] + [swap(d_pieces[m], "hid", m) for m in range(1, hid)]

    near_rows = some // inner
    def reduce_table(order):
        return call(
            functools.partial(table_kernel, chunks=chunks, dp=dp, hid=hid),
            [shape((slots, feats), bf16) for r in range(dp)],
            (block_owners, *counts, *d_pooled, order),
            in_specs=[SMEM] + [VMEM] * (chunks + hid) + [ANY],
            scratch=[
                pltpu.VMEM((feats, events), bf16),
                pltpu.VMEM((vocab, feats), bf16),
                pltpu.VMEM((dp, slots, feats), bf16),
                pltpu.SMEM((dp,), jnp.int32),
            ],
            vmem=20 if vocab <= 4096 else 58,
            us=COST["table"],
        )

    come = swap(away, "hid", 1)

    def half(nears, *order):
        return call(
            functools.partial(core_merge_kernel, rows=near_rows, inner=inner, nears=nears),
            [
                shape((near_rows + small_rows * (near > 0), piece_cols), bf16)
                for m in range(hid // 2)
                for near in nears
            ],
            (home, come, small, *order),
            in_specs=[VMEM] * 3 + [ANY] * len(order),
            vmem=12,
            us=COST["half"],
        )

    def chip_sum(parts, *order):
        return call(
            functools.partial(chip_merge_kernel, terms=hid // 2),
            shape(parts[0].shape, bf16),
            (parts[0], *[swap(parts[m], "hid", 2 * m) for m in range(1, hid // 2)], *order),
            in_specs=[VMEM] * (hid // 2) + [ANY] * len(order),
            vmem=6,
            us=COST["chip"],
        )

    order = ((), (d_pooled[1],), (d_pooled[hid - 1],))[OPT["e"]]
    parts = half(tuple(range(1, inner)), *order)
    parts = [None] + [parts[i :: inner - 1] for i in range(inner - 1)]
    d_table = reduce_table((block_owners, parts[1][0])[OPT["f"]])
    sums = {}
    for far in reversed(range(outer)):
        terms = [d_table[far * inner]]
        terms += [swap(d_table[far * inner + m], "dp", m) for m in range(1, inner)]
        sums[far] = terms

    def add_up(terms, *order):
        return call(
            functools.partial(sum_kernel, terms=len(terms)),
            shape((slots, feats), bf16),
            (*terms, *order),
            in_specs=[VMEM] * len(terms) + [ANY] * len(order),
            vmem=4,
            us=COST["sum"],
        )

    last = outer - 1
    if OPT["c"] == 2:
        sums[last] = add_up(sums[last])
    orders = ((), (d_table[0],), (sums[last],))[OPT["c"]]
    chips = [None] + [chip_sum(parts[i], *orders) for i in range(1, inner)]
    blocks = O * STREAMS // piece_cols
    stay = call(
        functools.partial(stay_kernel, rows=near_rows, inner=inner),
        [
            shape((near_rows + blocks * rows * (m > 0), piece_cols), bf16)
            for m in range(hid // 2)
        ],
        (home, come, mixed_part, (block_owners, chips[1], d_table[0], sums[last] if OPT["c"] == 2 else d_table[1])[OPT["k"]]),
        in_specs=[VMEM] * 3 + [ANY],
        vmem=8,
        us=COST["half"],
    )
    if OPT["c"] != 2:
        sums[last] = add_up(sums[last], *((), (chips[1],))[OPT["d"]])
    later = [far for far in range(1, last) if far % 2] if OPT["p"] and not OPT["h"] else []
    for far in range(last):
        if far not in later:
            sums[far] = functools.reduce(plus, sums[far])
    recent = sums[last]
    if OPT["h"]:
        leaves = sums[1]
        table_terms = [sums[0]]
        table_terms += [swap(sums[far], "dp", far * inner) for far in reversed(range(1, outer))]
    else:
        step = 1
        while step < outer // 2:
            for far in reversed([f for f in sums if f & step]):
                if far in later and step == 1:
                    sums[far] = add_up(sums[far], sums[(far ^ step) + 2])
                sums[far ^ step] = plus(sums[far ^ step], swap(sums.pop(far), "dp", step * inner))
            step *= 2
        leaves = sums[step]
        table_terms = [sums[0], swap(leaves, "dp", step * inner)]
    order = (block_owners, leaves, sums[0], recent)[OPT["s"]]
    chips[0], mixed_own = call(
        functools.partial(stay_merge_kernel, terms=hid // 2, rows=near_rows),
        [
            shape((near_rows, piece_cols), bf16),
            shape((hid // 2, *mixed_part.shape), bf16),
        ],
        (stay[0], *[swap(stay[m], "hid", 2 * m) for m in range(1, hid // 2)], mixed_part, order),
        in_specs=[VMEM] * (hid // 2 + 1) + [ANY],
        vmem=8,
        us=COST["chip"],
    )
    mixed_list = [mixed_own, swap(mixed_own, "hid", 1)]
    far_parts = call(
        functools.partial(near_merge_kernel, terms=inner, rows=piece_rows, outer=outer),
        [shape((piece_rows + small_rows, piece_cols), bf16)] * outer,
        (chips[0], chips[1], *[swap(chips[i], "dp", i) for i in range(1, inner)]),
        vmem=12,
        us=COST["near"],
    )
    weight_terms = [far_parts[0]] + [swap(far_parts[m], "dp", m * inner) for m in range(1, outer)]

    states = (
        table_w,
        table_m,
        table_v,
        table_ema,
        first_w,
        first_m,
        first_v,
        first_ema,
        second_w,
        second_m,
        second_v,
        second_ema,
        vector_w,
        vector_m,
        vector_v,
        vector_ema,
        *[g.T for g in (gate_w, gate_m, gate_v, gate_ema)],
    )
    mixed, *new = call(
        functools.partial(
            finish_kernel,
            table_terms=len(table_terms),
            terms=len(weight_terms),
            dp=dp,
            hid=hid,
        ),
        [shape((events, O * STREAMS), bf16)] + [shape(v.shape, f32) for v in states],
        (*states[:4], *table_terms, *states[4:], *weight_terms)
        + tuple(mixed_list),
        vmem=20,
        us=COST["finish"],
    )
    return (mixed, *new[:16], *[g.T for g in new[16:]])


def solution(mesh):
    split, spread, whole = P("dp", "hid"), P("hid", "dp"), P()
    return jax.shard_map(
        per_device,
        mesh=mesh,
        in_specs=(P("dp"), P("dp"), whole, split)
        + (split,) * 8
        + (spread,) * 4
        + (P(None, "hid"),) * 4
        + (whole,) * 4,
        out_specs=(P("dp", None),)
        + (split,) * 8
        + (spread,) * 4
        + (P(None, "hid"),) * 4
        + (whole,) * 4,
        check_vma=False,
    )
```
